32 devices in a mesh: dp: 4 (over y, core), mp: 8 (over z, x).
Axes of the slice: x: 2, y: 2, z: 4, core: 2. Of those that a mesh axis runs over, the one named last changes fastest.
Arguments:
- tokens: bfloat16 [32768, 1024], P(('dp', 'mp')), may hold values from -6 to 6
- segment_ids: int32 [32, 1024], P(('dp', 'mp')), may hold values from 0 to 15, never falling along the last dimension, each value on 1 to 256 neighbouring positions
- w_query: bfloat16 [1024, 1024], replicated, may hold values from -0.1875 to 0.1875
- w_key: bfloat16 [1024, 1024], replicated, may hold values from -0.1875 to 0.1875
- w_value: bfloat16 [1024, 1024], replicated, may hold values from -0.1875 to 0.1875
- w_out: bfloat16 [1024, 1024], replicated, may hold values from -2 to 2
- gain_one: float32 [1024], replicated, may hold values from 0.5 to 1.5
- gain_two: float32 [1024], replicated, may hold values from 0.5 to 1.5
- w_in: bfloat16 [1024, 4096], P(None, 'mp'), may hold values from -0.1875 to 0.1875
- w_back: bfloat16 [4096, 1024], P('mp'), may hold values from -0.09375 to 0.09375
- prefix_master: float32 [2, 64, 1024], replicated, may hold values from -6 to 6
- moment_one: float32 [2, 64, 1024], replicated, may hold values from -6 to 6
- moment_two: float32 [2, 64, 1024], replicated, may hold values from 0.064 to 1.024
- cotangent: bfloat16 [32768, 1024], P(('dp', 'mp')), may hold values from -6 to 6
Outputs:
- layer_output: bfloat16 [32768, 1024], P(('dp', 'mp'))
- input_grad: float32 [32768, 1024], P(('dp', 'mp'))
- new_master: float32 [2, 64, 1024], replicated
- new_first: float32 [2, 64, 1024], replicated
- new_second: float32 [2, 64, 1024], replicated
- new_copy: bfloat16 [2, 64, 1024], replicated
The draws below stay inside these ranges and needn't reach their ends.
Inputs may be any that keep to these rules, and one draw needn't show every extreme that they name: `segment_ids`: within each packed row the ids never fall, start at 0 and number whole sentences of 1 to 256 tokens, one of exactly that length.
All inputs are finite; a program needn't handle non-finite values.
Results may differ from the reference program's by a relative error of at most 0.014.
Values may be sent and summed in bfloat16 or wider, within the bound.
No kernel may reach another device: no remote copies, remote signals or barrier semaphores. Data moves between devices by JAX's collectives and lax.ppermute only.
A program may use at most 320 MiB of HBM per device.

```python
import math
import jax
import jax.numpy as jnp
import numpy as np
from jax import lax

D = 1024
HEADS = 16
FF = 4096
SLOTS = 64
LEN = 1024
STEP = 5
ROWS = 32
TOKENS = 32768
KEYS = 128


def steps_of(rng, extent, cuts, low, largest):
    level, own = 1.0, jax.random.fold_in(rng, 6)
    for dim, blocks in cuts:
        heights = jnp.exp(jax.random.uniform(jax.random.fold_in(own, dim), (blocks,), jnp.float32, low / len(cuts), largest / len(cuts)))
        level = level * jnp.repeat(heights, extent[dim] // blocks).reshape([-1 if axis == dim else 1 for axis in range(len(extent))])
    return level


def length_profile(count, total, most, lean):
    weights = [(1 << 20) // math.isqrt(standing ** lean) + 1 for standing in range(2, count + 1)]
    rest, holding = total - most - (count - 1), [1] * (count - 1)
    while rest > 0:
        movable = [i for i in range(count - 1) if holding[i] < most]
        whole, budget = sum([weights[i] for i in movable]), rest
        for i in movable:
            addition = min(most - holding[i], max(1, budget * weights[i] // whole), rest)
            holding[i] = holding[i] + addition
            rest = rest - addition
    return np.array([most] + holding)


def ragged_sizes(key, amount, total, most, lean):
    if amount == 2:
        one = jax.random.randint(key, (), max(1, total - most), min(most, total - 1) + 1)
        return jnp.stack([one, total - one])
    lengths = jnp.asarray(length_profile(amount, total, most, lean), jnp.int32)
    couples = (amount - 1) // 2
    giver, sink = lengths[1:1 + 2 * couples:2], lengths[2:2 + 2 * couples:2]
    slack = jnp.minimum(giver - 1, most - sink)
    moved = jax.random.randint(jax.random.fold_in(key, 1), (couples,), 0, 1 << 20) % (slack + 1)
    lengths = lengths.at[1:1 + 2 * couples:2].set(giver - moved).at[2:2 + 2 * couples:2].set(sink + moved)
    return lengths[jax.random.permutation(jax.random.fold_in(key, 2), amount)]


def scatter_about(stream_key, extent, width, bound, shards=(), held_as=jnp.bfloat16):
    array = width * jax.random.normal(stream_key, extent, jnp.float32)
    if shards:
        array = array * steps_of(stream_key, extent, shards, -0.22, 0.18)
    return jnp.clip(array, -bound, bound).astype(held_as)


def setup_inputs(seed: int = 0) -> dict:
    key_of = jax.random.split(jax.random.key(seed), 15)
    return {
        "tokens": scatter_about(key_of[0], (TOKENS, D), 1.0, 6.0, ((0, 32),)),
        "segment_ids": jax.vmap(lambda own: jnp.searchsorted(jnp.cumsum(ragged_sizes(own, max(LEN // 64, 8), LEN, LEN // 4, 0)), jnp.arange(LEN), side="right"))(jax.random.split(key_of[1], ROWS)).reshape((ROWS, LEN)).astype(jnp.int32),
        "w_query": scatter_about(key_of[2], (D, D), D ** -0.5, 0.1875),
        "w_key": scatter_about(key_of[3], (D, D), D ** -0.5, 0.1875),
        "w_value": scatter_about(key_of[4], (D, D), D ** -0.5, 0.1875),
        "w_out": scatter_about(key_of[5], (D, D), (D // KEYS) ** -0.5, 2.0),
        "gain_one": jnp.clip(1.0 + 0.1 * jax.random.normal(key_of[6], (D,), jnp.float32), 0.5, 1.5),
        "gain_two": jnp.clip(1.0 + 0.1 * jax.random.normal(key_of[7], (D,), jnp.float32), 0.5, 1.5),
        "w_in": scatter_about(key_of[8], (D, FF), D ** -0.5, 0.1875, ((1, 8),)),
        "w_back": scatter_about(key_of[9], (FF, D), FF ** -0.5, 0.09375, ((0, 8),)),
        "prefix_master": scatter_about(key_of[10], (2, SLOTS, D), 1.0, 6.0, (), jnp.float32),
        "moment_one": scatter_about(key_of[11], (2, SLOTS, D), (0.08 * (TOKENS // KEYS) ** 0.5), 6.0, (), jnp.float32),
        "moment_two": jnp.clip(jnp.exp(jax.random.uniform(key_of[12], (2, SLOTS, D), jnp.float32, math.log(0.064), math.log(1.024))), 0.064, 1.024),
        "cotangent": scatter_about(key_of[13], (TOKENS, D), 1.0, 6.0, ((0, 32),)),
    }


epsilon_norm = 1e-05
masked_score = -1e+30
learn_rate = 1.0
weight_decay = 0.01
beta_one = 0.9
beta_two = 0.999
epsilon_adam = 1e-08

@jax.custom_vjp
def low(v):
    return lax.optimization_barrier(v.astype(jnp.bfloat16)).astype(jnp.float32)

@jax.custom_vjp
def low_back(v):
    return v

def low_keep(v):
    return (low(v), None)

def low_pass(kept, grad):
    return (grad,)

def back_keep(v):
    return (v, None)

def back_low(kept, grad):
    return (low(grad),)
low.defvjp(low_keep, low_pass)
low_back.defvjp(back_keep, back_low)

def layer_norm(values, gain):
    average = lax.optimization_barrier(jnp.mean(values, axis=-1, keepdims=True))
    centred = values - average
    spread = lax.optimization_barrier(jnp.mean(centred * centred, axis=-1, keepdims=True))
    return gain * centred * lax.rsqrt(spread + epsilon_norm)

def product(left, right):
    return jnp.dot(left, right, precision=lax.Precision.HIGHEST)

def group_forward(tok_group, seg_group, w_query, w_key, w_value, w_out, gain_one, gain_two, w_in, w_back, prefix_val):
    row_count, length, model_width = tok_group.shape
    head_width = model_width // HEADS
    score_scale = head_width ** (-0.5)
    flat_rows = tok_group.reshape(row_count * length, model_width)
    queries = low_back(low(product(flat_rows, w_query))).reshape(row_count, length, HEADS, head_width)
    keys_own = low_back(low(product(flat_rows, w_key))).reshape(row_count, length, HEADS, head_width)
    values_own = low_back(low(product(flat_rows, w_value))).reshape(row_count, length, HEADS, head_width)
    prefix_low = low(prefix_val)
    prefix_keys = jnp.broadcast_to(prefix_low[0].reshape(1, SLOTS, HEADS, head_width), (row_count, SLOTS, HEADS, head_width))
    prefix_vals = jnp.broadcast_to(prefix_low[1].reshape(1, SLOTS, HEADS, head_width), (row_count, SLOTS, HEADS, head_width))
    all_keys = jnp.concatenate([prefix_keys, keys_own], axis=1)
    all_vals = jnp.concatenate([prefix_vals, values_own], axis=1)
    raw_score = jnp.einsum('rqhd,rkhd->rhqk', queries, all_keys, precision=lax.Precision.HIGHEST) * score_scale
    same_segment = seg_group[:, :, None] == seg_group[:, None, :]
    visible = jnp.concatenate([jnp.ones((row_count, length, SLOTS), dtype=bool), same_segment], axis=2)
    scores = low_back(jnp.where(visible[:, None], raw_score, masked_score))
    weights_attn = low(jax.nn.softmax(scores, axis=-1))
    attended = jnp.einsum('rhqk,rkhd->rqhd', weights_attn, all_vals, precision=lax.Precision.HIGHEST)
    attended = low_back(low(attended.reshape(row_count * length, model_width)))
    normed_one = layer_norm(flat_rows + product(attended, w_out), gain_one)
    normed_low = low(normed_one)
    pre_act = low_back(product(normed_low, w_in))
    activation = low(jax.nn.gelu(pre_act, approximate=False))
    branch = low_back(product(activation, w_back))
    return layer_norm(normed_one + branch, gain_two)

def reference(tokens, segment_ids, w_query, w_key, w_value, w_out, gain_one, gain_two, w_in, w_back, prefix_master, moment_one, moment_two, cotangent):
    matrices = tuple((mat_in.astype(jnp.float32) for mat_in in (w_query, w_key, w_value, w_out)))
    ffn_in = w_in.astype(jnp.float32)
    ffn_back = w_back.astype(jnp.float32)
    group_total = TOKENS // (2 * LEN)
    tok_groups = tokens.astype(jnp.float32).reshape(group_total, 2, LEN, D)
    seg_groups = segment_ids.reshape(group_total, 2, LEN)
    cot_groups = cotangent.astype(jnp.float32).reshape(group_total, 2 * LEN, D)

    def advance(summed, pieces):
        tok_group, seg_group, cot_group = pieces

        def forward(tok_values, prefix_val):
            return group_forward(tok_values, seg_group, matrices[0], matrices[1], matrices[2], matrices[3], gain_one, gain_two, ffn_in, ffn_back, prefix_val)
        result, backward = jax.vjp(forward, tok_group, prefix_master)
        tok_grad, prefix_grad = backward(cot_group)
        return (summed + prefix_grad, (result.astype(jnp.bfloat16), tok_grad.reshape(2 * LEN, D)))
    prefix_grad, (results, tok_grads) = lax.scan(advance, jnp.zeros_like(prefix_master), (tok_groups, seg_groups, cot_groups))
    new_first = beta_one * moment_one + (1.0 - beta_one) * prefix_grad
    new_second = beta_two * moment_two + (1.0 - beta_two) * prefix_grad * prefix_grad
    first_hat = new_first / (1.0 - beta_one ** STEP)
    second_hat = new_second / (1.0 - beta_two ** STEP)
    new_master = prefix_master * (1.0 - learn_rate * weight_decay) - learn_rate * first_hat / (jnp.sqrt(second_hat) + epsilon_adam)
    return (results.reshape(TOKENS, D), tok_grads.reshape(TOKENS, D), new_master, new_first, new_second, new_master.astype(jnp.bfloat16))
```

```python
import jax
import jax.numpy as jnp
from jax import lax
from jax.experimental import pallas as pl
from jax.experimental.pallas import tpu as pltpu
from jax.sharding import PartitionSpec as P

STEP = 5
HEAD_SCALE = 0.125

epsilon_norm = 1e-05
learn_rate = 1.0
weight_decay = 0.01
beta_one = 0.9
beta_two = 0.999
epsilon_adam = 1e-08

f32, bf16 = jnp.float32, jnp.bfloat16
NEG = -1e30
WIN = 256
KC = 64
QUAD = 256
NT = (((1,), (1,)), ((), ()))
NN = (((1,), (0,)), ((), ()))
TN = (((0,), (0,)), ((), ()))

def dot(a, b, d=NN):
    return lax.dot_general(a, b, d, preferred_element_type=f32)

def vm():
    return pl.BlockSpec(memory_space=pltpu.VMEM)

def sm():
    return pl.BlockSpec(memory_space=pltpu.SMEM)

def block_diag(piece):
    lane = lax.broadcasted_iota(jnp.int32, piece.shape, 1) // 64
    zero = jnp.zeros_like(piece)
    return jnp.concatenate([jnp.where(lane == h, piece, zero) for h in range(4)], axis=0)

def diag_of(full):
    lane = lax.broadcasted_iota(jnp.int32, (KC, 128), 1) < 64
    left = jnp.where(lane, full[0:64, 0:128], full[64:128, 0:128])
    right = jnp.where(lane, full[128:192, 128:256], full[192:256, 128:256])
    return jnp.concatenate([left, right], axis=1)

def window(lo_ref, seg_col_ref, seg_key_ref, c, w, length):
    nominal = lo_ref[c] + w * WIN
    start = pl.multiple_of(jnp.minimum(nominal, length - WIN), 16)
    rows = pl.ds(start, WIN)
    row_id = lax.broadcasted_iota(jnp.int32, (WIN, 128), 0) + start
    seg_q = seg_col_ref[rows, :]
    seg_k = seg_key_ref[pl.ds(c, 1), :]
    keep = jnp.logical_and(seg_q == seg_k, row_id >= nominal)
    bias = jnp.where(keep, 0.0, NEG)
    return rows, jnp.concatenate([bias, bias], axis=1)

def half_reduce(x, op, fill):
    lane = lax.broadcasted_iota(jnp.int32, x.shape, 1) < 64
    a = op(jnp.where(lane, x, fill), axis=1, keepdims=True)
    b = op(jnp.where(lane, fill, x), axis=1, keepdims=True)
    return jnp.where(lane, a, b)

def fwd_kernel(lo_ref, nw_ref, q_ref, k_ref, v_ref, pk_ref, pv_ref, segc_ref, segk_ref, att_ref, lse_ref, m_ref, l_ref, acc_ref, bdk_ref, bdv_ref):
    length, lanes = q_ref.shape
    quads = lanes // QUAD
    chunks = length // KC
    tiles = length // WIN
    for g in range(quads):
        cols = slice(g * QUAD, (g + 1) * QUAD)
        bdk_ref[g] = block_diag(pk_ref[:, cols])
        bdv_ref[g] = block_diag(pv_ref[:, cols])

    @pl.loop(0, tiles)
    def _(r):
        rows = pl.ds(pl.multiple_of(r * WIN, WIN), WIN)
        for g in range(quads):
            cols = slice(g * QUAD, (g + 1) * QUAD)
            m_ref[rows, cols] = dot(q_ref[rows, cols], bdk_ref[g], NT)

    def load_k(c, ref, bd):
        krows = pl.ds(pl.multiple_of(c * KC, KC), KC)
        for g in range(quads):
            bd[g] = block_diag(ref[krows, g * QUAD:(g + 1) * QUAD])

    @pl.loop(0, chunks)
    def _(c):
        load_k(c, k_ref, bdv_ref)

        @pl.loop(0, nw_ref[c])
        def _(w):
            rows, bias = window(lo_ref, segc_ref, segk_ref, c, w, length)
            parts = [slice(g * QUAD, (g + 1) * QUAD) for g in range(quads)]
            scores = [dot(q_ref[rows, cols], bdv_ref[g], NT) for g, cols in enumerate(parts)]
            for g, cols in enumerate(parts):
                m_ref[rows, cols] = jnp.maximum(m_ref[rows, cols], scores[g] + bias)

    for g in range(quads):
        bdv_ref[g] = block_diag(pv_ref[:, g * QUAD:(g + 1) * QUAD])

    @pl.loop(0, tiles)
    def _(r):
        rows = pl.ds(pl.multiple_of(r * WIN, WIN), WIN)
        for t in range(lanes // 128):
            cols = slice(t * 128, (t + 1) * 128)
            m_ref[rows, cols] = half_reduce(m_ref[rows, cols], jnp.max, NEG)
        parts = [slice(g * QUAD, (g + 1) * QUAD) for g in range(quads)]
        score = dot(q_ref[rows, parts[0]], bdk_ref[0], NT)
        for g, cols in enumerate(parts):
            later = dot(q_ref[rows, parts[g + 1]], bdk_ref[g + 1], NT) if g + 1 < quads else None
            p = jnp.exp(score - m_ref[rows, cols])
            l_ref[rows, cols] = p
            acc_ref[rows, cols] = dot(p.astype(bf16), bdv_ref[g])
            score = later

    @pl.loop(0, chunks)
    def _(c):
        load_k(c, k_ref, bdk_ref)
        load_k(c, v_ref, bdv_ref)

        @pl.loop(0, nw_ref[c])
        def _(w):
            rows, bias = window(lo_ref, segc_ref, segk_ref, c, w, length)
            parts = [slice(g * QUAD, (g + 1) * QUAD) for g in range(quads)]
            score = dot(q_ref[rows, parts[0]], bdk_ref[0], NT)
            for g, cols in enumerate(parts):
                later = dot(q_ref[rows, parts[g + 1]], bdk_ref[g + 1], NT) if g + 1 < quads else None
                p = jnp.exp(score + bias - m_ref[rows, cols])
                l_ref[rows, cols] += p
                acc_ref[rows, cols] += dot(p.astype(bf16), bdv_ref[g])
                score = later

    @pl.loop(0, tiles)
    def _(r):
        rows = pl.ds(pl.multiple_of(r * WIN, WIN), WIN)
        for t in range(lanes // 128):
            cols = slice(t * 128, (t + 1) * 128)
            total = half_reduce(l_ref[rows, cols], jnp.sum, 0.0)
            att_ref[rows, cols] = (acc_ref[rows, cols] / total).astype(bf16)
            lse_ref[rows, cols] = m_ref[rows, cols] + jnp.log(total)

def attend(lo, nw, q, k, v, pk, pv, segc, segk):
    length, lanes = q.shape
    quads = lanes // QUAD
    return pl.pallas_call(
        fwd_kernel,
        out_shape=(jax.ShapeDtypeStruct((length, lanes), bf16), jax.ShapeDtypeStruct((length, lanes), f32)),
        in_specs=[sm(), sm()] + [vm()] * 7,
        out_specs=(vm(), vm()),
        scratch_shapes=[pltpu.VMEM((length, lanes), f32)] * 3 + [pltpu.VMEM((quads, 256, 256), bf16)] * 2,
        compiler_params=pltpu.CompilerParams(vmem_limit_bytes=52 << 20),
        name="attend",
    )(lo, nw, q, k, v, pk, pv, segc, segk)

def windows(seg):
    length = seg.shape[0]
    chunks = length // KC
    by = seg.reshape(chunks, KC)
    first, last = by[:, 0], by[:, -1]
    lo = jnp.sum((seg[None, :] < first[:, None]).astype(jnp.int32), axis=1)
    hi = jnp.sum((seg[None, :] <= last[:, None]).astype(jnp.int32), axis=1)
    lo = lo // 16 * 16
    nw = (hi - lo + WIN - 1) // WIN
    segc = jnp.broadcast_to(seg[:, None], (length, 128))
    segk = jnp.concatenate([by, by], axis=1)
    return lo, nw, segc, segk

def pre_kernel(q_ref, g_ref, a_ref, lse_ref, pk_ref, pv_ref, delta_ref, ds_ref, dpk_ref, dpv_ref):
    length, lanes = q_ref.shape
    tiles = length // WIN
    bdk = block_diag(pk_ref[...])
    bdv = block_diag(pv_ref[...])
    row = lax.broadcasted_iota(jnp.int32, (QUAD, QUAD), 0) // 64
    lane = lax.broadcasted_iota(jnp.int32, (QUAD, QUAD), 1) // 64
    ones = jnp.where(row == lane, 1.0, 0.0).astype(bf16)
    dpk = jnp.zeros((KC, QUAD), f32)
    dpv = jnp.zeros((KC, QUAD), f32)
    spans = [slice(r * WIN, (r + 1) * WIN) for r in range(tiles)]

    def first(rows):
        g = g_ref[rows, :]
        prod = g.astype(f32) * a_ref[rows, :].astype(f32)
        high = prod.astype(bf16)
        rest = (prod - high.astype(f32)).astype(bf16)
        return dot(q_ref[rows, :], bdk, NT), dot(g, bdv, NT), dot(high, ones) + dot(rest, ones)

    def second(rows, three):
        delta_ref[rows, :] = three[2]
        p = jnp.exp(three[0] - lse_ref[rows, :])
        ds = (p * (three[1] - three[2])).astype(bf16)
        ds_ref[rows, :] = ds
        return p.astype(bf16), ds

    raw, done = first(spans[0]), None
    for r in range(tiles + 1):
        upcoming = first(spans[r + 1]) if r + 1 < tiles else None
        fresh = second(spans[r], raw) if r < tiles else None
        if done is not None:
            dpv = dpv + diag_of(dot(done[0], g_ref[spans[r - 1], :], TN))
            dpk = dpk + diag_of(dot(done[1], q_ref[spans[r - 1], :], TN))
        raw, done = upcoming, fresh
    dpk_ref[...] = dpk
    dpv_ref[...] = dpv

def prefix_back(q, g, a, lse, pk, pv):
    length, lanes = q.shape
    quads = lanes // QUAD
    slots = pk.shape[0]
    tall = pl.BlockSpec((length, QUAD), lambda i: (0, i))
    short = pl.BlockSpec((slots, QUAD), lambda i: (0, i))
    return pl.pallas_call(
        pre_kernel,
        grid=(quads,),
        out_shape=(jax.ShapeDtypeStruct((length, lanes), f32), jax.ShapeDtypeStruct((length, lanes), bf16),
                   jax.ShapeDtypeStruct((slots, lanes), f32), jax.ShapeDtypeStruct((slots, lanes), f32)),
        in_specs=[tall, tall, tall, tall, short, short],
        out_specs=(tall, tall, short, short),
        compiler_params=pltpu.CompilerParams(vmem_limit_bytes=48 << 20),
        name="prefix_back",
    )(q, g, a, lse, pk, pv)

def back_kernel(lo_ref, nw_ref, q_ref, k_ref, v_ref, g_ref, lse_ref, delta_ref, ds_ref, pk_ref, segc_ref, segk_ref,
                wq_ref, wk_ref, wv_ref, one_ref, out_ref, dq_ref, dk_ref, dv_ref, bdk_ref, bdv_ref, sk_ref, sv_ref):
    length, lanes = q_ref.shape
    quads = lanes // QUAD
    chunks = length // KC
    tiles = length // WIN
    for g in range(quads):
        cols = slice(g * QUAD, (g + 1) * QUAD)
        bdk_ref[g] = block_diag(pk_ref[:, cols])

    @pl.loop(0, tiles)
    def _(r):
        rows = pl.ds(pl.multiple_of(r * WIN, WIN), WIN)
        for g in range(quads):
            cols = slice(g * QUAD, (g + 1) * QUAD)
            dq_ref[rows, cols] = dot(ds_ref[rows, cols], bdk_ref[g])

    @pl.loop(0, chunks)
    def _(c):
        krows = pl.ds(pl.multiple_of(c * KC, KC), KC)
        for g in range(quads):
            cols = slice(g * QUAD, (g + 1) * QUAD)
            bdk_ref[g] = block_diag(k_ref[krows, cols])
            bdv_ref[g] = block_diag(v_ref[krows, cols])
        sk_ref[...] = jnp.zeros_like(sk_ref)
        sv_ref[...] = jnp.zeros_like(sv_ref)

        @pl.loop(0, nw_ref[c])
        def _(w):
            rows, bias = window(lo_ref, segc_ref, segk_ref, c, w, length)
            parts = [slice(g * QUAD, (g + 1) * QUAD) for g in range(quads)]

            def first(g):
                return dot(q_ref[rows, parts[g]], bdk_ref[g], NT), dot(g_ref[rows, parts[g]], bdv_ref[g], NT)

            def second(g, pair):
                p = jnp.exp(pair[0] + bias - lse_ref[rows, parts[g]])
                return p.astype(bf16), (p * (pair[1] - delta_ref[rows, parts[g]])).astype(bf16)

            def third(g, pair):
                cols = parts[g]
                sv_ref[:, cols] += diag_of(dot(pair[0], g_ref[rows, cols], TN))
                sk_ref[:, cols] += diag_of(dot(pair[1], q_ref[rows, cols], TN))
                dq_ref[rows, cols] += dot(pair[1], bdk_ref[g])

            raw, done = first(0), None
            for g in range(quads):
                upcoming = first(g + 1) if g + 1 < quads else None
                fresh = second(g, raw)
                if done is not None:
                    third(g - 1, done)
                raw, done = upcoming, fresh
            third(quads - 1, done)

        dk_ref[krows, :] = sk_ref[...].astype(bf16)
        dv_ref[krows, :] = sv_ref[...].astype(bf16)

    scale = HEAD_SCALE

    @pl.loop(0, tiles)
    def _(r):
        rows = pl.ds(pl.multiple_of(r * WIN, WIN), WIN)
        part = dot((dq_ref[rows, :] * scale).astype(bf16), wq_ref[...], NT)
        part = part + dot(dk_ref[rows, :], wk_ref[...], NT)
        part = part + dot(dv_ref[rows, :], wv_ref[...], NT)

        @pl.when(pl.program_id(0) == 0)
        def _():
            out_ref[rows, :] = one_ref[rows, :] + part

        @pl.when(pl.program_id(0) > 0)
        def _():
            out_ref[rows, :] += part

def attend_back(lo, nw, q, k, v, g, lse, delta, ds, pk, segc, segk, wq, wk, wv, grad_one, width=1024):
    length, lanes = q.shape
    quads = width // QUAD
    slots = pk.shape[0]
    tall = pl.BlockSpec((length, width), lambda i: (0, i))
    short = pl.BlockSpec((slots, width), lambda i: (0, i))
    wt = pl.BlockSpec((lanes, width), lambda i: (0, i))

    def whole(shape):
        return pl.BlockSpec(shape, lambda i: (0, 0))

    smem = pl.BlockSpec(memory_space=pltpu.SMEM)
    return pl.pallas_call(
        back_kernel,
        grid=(lanes // width,),
        out_shape=jax.ShapeDtypeStruct((length, lanes), f32),
        in_specs=[smem, smem, tall, tall, tall, tall, tall, tall, tall, short, whole(segc.shape), whole(segk.shape), wt, wt, wt, whole(grad_one.shape)],
        out_specs=whole((length, lanes)),
        scratch_shapes=[pltpu.VMEM((length, width), f32), pltpu.VMEM((length, width), bf16), pltpu.VMEM((length, width), bf16),
                        pltpu.VMEM((quads, 256, 256), bf16), pltpu.VMEM((quads, 256, 256), bf16),
                        pltpu.VMEM((KC, width), f32), pltpu.VMEM((KC, width), f32)],
        compiler_params=pltpu.CompilerParams(vmem_limit_bytes=58 << 20),
        name="attend_back",
    )(lo, nw, q, k, v, g, lse, delta, ds, pk, segc, segk, wq, wk, wv, grad_one)


def mean_of(x):
    return jnp.mean(x, axis=-1, keepdims=True)


def norm_kernel(att_ref, tok_ref, wout_ref, gain_ref, hat_ref, inv_ref, low_ref):
    x = tok_ref[...].astype(f32) + dot(att_ref[...], wout_ref[...])
    centred = x - mean_of(x)
    inv = lax.rsqrt(mean_of(centred * centred) + epsilon_norm)
    hat = centred * inv
    hat_ref[...] = hat
    inv_ref[...] = jnp.broadcast_to(inv, inv_ref.shape)
    low_ref[...] = (gain_ref[...] * hat).astype(bf16)


def first_norm(att, tokens, w_out, gain):
    length, lanes = att.shape
    tall = pl.BlockSpec((WIN, lanes), lambda i: (i, 0))
    return pl.pallas_call(
        norm_kernel,
        grid=(length // WIN,),
        out_shape=(
            jax.ShapeDtypeStruct((length, lanes), f32),
            jax.ShapeDtypeStruct((length, 128), f32),
            jax.ShapeDtypeStruct((length, lanes), bf16),
        ),
        in_specs=[
            tall,
            tall,
            pl.BlockSpec((lanes, lanes), lambda i: (0, 0)),
            pl.BlockSpec((1, lanes), lambda i: (0, 0)),
        ],
        out_specs=(tall, pl.BlockSpec((WIN, 128), lambda i: (i, 0)), tall),
        compiler_params=pltpu.CompilerParams(vmem_limit_bytes=40 << 20),
        name="first_norm",
    )(att, tokens, w_out, gain)


def gelu_pair(x):
    t = 1.0 / (1.0 + (0.3275911 * 0.7071067811865476) * jnp.abs(x))
    bell = jnp.exp(-0.5 * (x * x))
    poly = t * (0.127414796 + t * (-0.142248368 + t * (0.7107068705 + t * (-0.7265760135 + t * 0.5307027145))))
    tail = poly * bell
    phi = jnp.where(x < 0.0, tail, 1.0 - tail)
    return x * phi, phi + x * (0.3989422804014327 * bell)


HID = 512


def ffn_kernel(low_ref, w_in_ref, w_back_ref, start_ref, sum_ref, slope_ref):
    length = low_ref.shape[0]
    tiles = length // WIN
    spans = [slice(r * WIN, (r + 1) * WIN) for r in range(tiles)]

    @pl.when(pl.program_id(0) == 0)
    def _():
        sum_ref[...] = start_ref[...]

    def first(r):
        return dot(low_ref[spans[r], :], w_in_ref[...], NT)

    def second(r, x):
        act, slope = gelu_pair(x)
        slope_ref[spans[r], :] = slope.astype(bf16)
        return act.astype(bf16)

    raw, done = first(0), None
    for r in range(tiles + 1):
        upcoming = first(r + 1) if r + 1 < tiles else None
        fresh = second(r, raw) if r < tiles else None
        if done is not None:
            sum_ref[spans[r - 1], :] += dot(done, w_back_ref[...])
        raw, done = upcoming, fresh


def ffn_forward(low, w_in, w_back, start):
    length, lanes = low.shape
    hidden = w_in.shape[0]

    def whole(shape):
        return pl.BlockSpec(shape, lambda i: (0, 0))

    wt = pl.BlockSpec((HID, lanes), lambda i: (i, 0))
    return pl.pallas_call(
        ffn_kernel,
        grid=(hidden // HID,),
        out_shape=(jax.ShapeDtypeStruct((length, lanes), f32), jax.ShapeDtypeStruct((length, hidden), bf16)),
        in_specs=[whole(low.shape), wt, wt, whole(start.shape)],
        out_specs=(whole((length, lanes)), pl.BlockSpec((length, HID), lambda i: (0, i))),
        compiler_params=pltpu.CompilerParams(vmem_limit_bytes=48 << 20),
        name="ffn_forward",
    )(low, w_in, w_back, start)


def ffn_back_kernel(
    sum_ref, cot_ref, gain_two_ref, gain_one_ref, w_in_ref, w_back_ref, slope_ref, hat_ref, inv_ref, w_out_ref,
    layer_ref, one_ref, att_ref, acc_ref, low_ref,
):
    length = sum_ref.shape[0]
    tiles = length // WIN
    spans = [slice(r * WIN, (r + 1) * WIN) for r in range(tiles)]

    @pl.when(pl.program_id(0) == 0)
    def _():
        for rows in spans:
            x = sum_ref[rows, :]
            centred = x - mean_of(x)
            inv = lax.rsqrt(mean_of(centred * centred) + epsilon_norm)
            hat = centred * inv
            layer_ref[rows, :] = (gain_two_ref[...] * hat).astype(bf16)
            pull = cot_ref[rows, :].astype(f32) * gain_two_ref[...]
            grad = inv * (pull - mean_of(pull) - hat * mean_of(pull * hat))
            acc_ref[rows, :] = grad
            low_ref[rows, :] = grad.astype(bf16)

    def first(r):
        return dot(low_ref[spans[r], :], w_back_ref[...], NT)

    def second(r, x):
        return (x * slope_ref[spans[r], :].astype(f32)).astype(bf16)

    raw, done = first(0), None
    for r in range(tiles + 1):
        upcoming = first(r + 1) if r + 1 < tiles else None
        fresh = second(r, raw) if r < tiles else None
        if done is not None:
            acc_ref[spans[r - 1], :] += dot(done, w_in_ref[...])
        raw, done = upcoming, fresh

    @pl.when(pl.program_id(0) == pl.num_programs(0) - 1)
    def _():
        for rows in spans:
            pull = acc_ref[rows, :] * gain_one_ref[...]
            hat = hat_ref[rows, :]
            grad = inv_ref[rows, 0:1] * (pull - mean_of(pull) - hat * mean_of(pull * hat))
            one_ref[rows, :] = grad
            att_ref[rows, :] = dot(grad.astype(bf16), w_out_ref[...], NT).astype(bf16)


def ffn_backward(total, cot, gain_two, gain_one, w_in, w_back, slope, hat, inv, w_out):
    length, lanes = total.shape
    hidden = w_in.shape[0]

    def whole(array):
        return pl.BlockSpec(array.shape, lambda i: (0, 0))

    wt = pl.BlockSpec((HID, lanes), lambda i: (i, 0))
    outs = (
        jax.ShapeDtypeStruct((length, lanes), bf16),
        jax.ShapeDtypeStruct((length, lanes), f32),
        jax.ShapeDtypeStruct((length, lanes), bf16),
    )
    return pl.pallas_call(
        ffn_back_kernel,
        grid=(hidden // HID,),
        out_shape=outs,
        in_specs=[
            whole(total), whole(cot), whole(gain_two), whole(gain_one), wt, wt,
            pl.BlockSpec((length, HID), lambda i: (0, i)), whole(hat), whole(inv), whole(w_out),
        ],
        out_specs=tuple(whole(o) for o in outs),
        scratch_shapes=[pltpu.VMEM((length, lanes), f32), pltpu.VMEM((length, lanes), bf16)],
        compiler_params=pltpu.CompilerParams(vmem_limit_bytes=60 << 20),
        name="ffn_backward",
    )(total, cot, gain_two, gain_one, w_in, w_back, slope, hat, inv, w_out)


def gather_weights(w_in, w_back):
    copies = lax.axis_size("dp")
    part = w_in.shape[1] // copies
    place = lax.axis_index("dp") * part
    mine_in = lax.dynamic_slice_in_dim(w_in, place, part, 1).T
    mine_back = lax.dynamic_slice_in_dim(w_back, place, part, 0)
    return (
        lax.all_gather(mine_in, ("dp", "mp"), axis=0, tiled=True),
        lax.all_gather(mine_back, ("dp", "mp"), axis=0, tiled=True),
    )


def on_device(
    tokens, segment_ids, w_query, w_key, w_value, w_out, gain_one, gain_two, w_in, w_back,
    prefix_master, moment_one, moment_two, cotangent,
):
    all_in, all_back = gather_weights(w_in, w_back)
    prefix_low = prefix_master.astype(bf16)
    prefix_keys, prefix_vals = prefix_low[0], prefix_low[1]
    first_gain, second_gain = gain_one[None, :], gain_two[None, :]

    queries = (jnp.dot(tokens, w_query, preferred_element_type=f32) * HEAD_SCALE).astype(bf16)
    keys_own = jnp.dot(tokens, w_key, preferred_element_type=f32).astype(bf16)
    values_own = jnp.dot(tokens, w_value, preferred_element_type=f32).astype(bf16)
    lo, nw, segc, segk = windows(segment_ids[0])
    attended, lse = attend(lo, nw, queries, keys_own, values_own, prefix_keys, prefix_vals, segc, segk)
    hat, inv, normed_low = first_norm(attended, tokens, w_out, first_gain)
    total, slope = ffn_forward(normed_low, all_in, all_back, first_gain * hat)
    layer_output, grad_one, grad_att = ffn_backward(
        total, cotangent, second_gain, first_gain, all_in, all_back, slope, hat, inv, w_out
    )
    delta, ds_prefix, dpk, dpv = prefix_back(queries, grad_att, attended, lse, prefix_keys, prefix_vals)
    prefix_grad = lax.psum(jnp.stack([dpk, dpv]), ("dp", "mp"))
    input_grad = attend_back(
        lo, nw, queries, keys_own, values_own, grad_att, lse, delta, ds_prefix, prefix_keys, segc, segk,
        w_query, w_key, w_value, grad_one,
    )
    new_first = beta_one * moment_one + (1.0 - beta_one) * prefix_grad
    new_second = beta_two * moment_two + (1.0 - beta_two) * prefix_grad * prefix_grad
    first_hat = new_first / (1.0 - beta_one**STEP)
    second_hat = new_second / (1.0 - beta_two**STEP)
    new_master = prefix_master * (1.0 - learn_rate * weight_decay) - learn_rate * first_hat / (
        jnp.sqrt(second_hat) + epsilon_adam
    )
    return (layer_output, input_grad, new_master, new_first, new_second, new_master.astype(bf16))


def solution(mesh):
    rows = P(("dp", "mp"), None)
    return jax.shard_map(
        on_device,
        mesh=mesh,
        in_specs=(rows, rows, P(), P(), P(), P(), P(), P(), P(None, "mp"), P("mp", None), P(), P(), P(), rows),
        out_specs=(rows, rows, P(), P(), P(), P()),
        check_vma=False,
    )
```

```python
import functools

import jax
import jax.numpy as jnp
from jax import lax
from jax.experimental import pallas as pl
from jax.experimental.pallas import tpu as pltpu
from jax.sharding import PartitionSpec as P

f32, bf16 = jnp.float32, jnp.bfloat16
STEP = 5
epsilon_norm = 1e-05
learn_rate = 1.0
weight_decay = 0.01
beta_one = 0.9
beta_two = 0.999
epsilon_adam = 1e-08
HEAD_SCALE = 0.125
NEG = -1e30
WIN = 256
KC = 64
QUAD = 256
SAFE = 60.0
ITEMS = 64
VMEM = 60 << 20
NN = (((1,), (0,)), ((), ()))
NT = (((1,), (1,)), ((), ()))
TN = (((0,), (0,)), ((), ()))


def dot(a, b, d=NN):
    return lax.dot_general(a, b, d, preferred_element_type=f32)


def vm():
    return pl.BlockSpec(memory_space=pltpu.VMEM)


def sm():
    return pl.BlockSpec(memory_space=pltpu.SMEM)


def hbm():
    return pl.BlockSpec(memory_space=pl.ANY)


def cost(flops, moved=8 << 20):
    return pl.CostEstimate(flops=flops, bytes_accessed=moved, transcendentals=0)


def block_diag(piece):
    lane = lax.broadcasted_iota(jnp.int32, piece.shape, 1) // 64
    zero = jnp.zeros_like(piece)
    return jnp.concatenate([jnp.where(lane == h, piece, zero) for h in range(4)], axis=0)


def diag_of(full):
    lane = lax.broadcasted_iota(jnp.int32, (KC, 128), 1) < 64
    left = jnp.where(lane, full[0:64, 0:128], full[64:128, 0:128])
    right = jnp.where(lane, full[128:192, 128:256], full[192:256, 128:256])
    return jnp.concatenate([left, right], axis=1)


def head_ones():
    row = lax.broadcasted_iota(jnp.int32, (QUAD, QUAD), 0) // 64
    lane = lax.broadcasted_iota(jnp.int32, (QUAD, QUAD), 1) // 64
    return jnp.where(row == lane, 1.0, 0.0).astype(bf16)


def head_sum(x, ones):
    high = x.astype(bf16)
    return dot(high, ones) + dot((x - high.astype(f32)).astype(bf16), ones)


def head_max(x):
    lane = lax.broadcasted_iota(jnp.int32, x.shape, 1) < 64
    a = jnp.max(jnp.where(lane, x, NEG), axis=1, keepdims=True)
    b = jnp.max(jnp.where(lane, NEG, x), axis=1, keepdims=True)
    return jnp.where(lane, a, b)


def windows(seg):
    length = seg.shape[0]
    by = seg.reshape(length // KC, KC)
    first, last = by[:, 0], by[:, -1]
    lo = jnp.sum((seg[None, :] < first[:, None]).astype(jnp.int32), axis=1)
    hi = jnp.sum((seg[None, :] <= last[:, None]).astype(jnp.int32), axis=1)
    lo = lo // 16 * 16
    nw = (hi - lo + WIN - 1) // WIN
    segc = jnp.broadcast_to(seg[:, None], (length, 128))
    segk = jnp.concatenate([by, by], axis=1)
    return lo, nw, segc, segk


def list_items(lo_ref, nw_ref, chunk_ref, row_ref, length):
    def chunk(c, count):
        def one(w, count):
            chunk_ref[count] = c
            row_ref[count] = lo_ref[c] + w * WIN
            return count + 1

        return lax.fori_loop(0, nw_ref[c], one, count)

    count = lax.fori_loop(0, length // KC, chunk, 0)
    for n in range(2):
        chunk_ref[count + n] = 0
        row_ref[count + n] = length
    return count


def item_at(n, chunk_ref, row_ref, segc_ref, segk_ref, length):
    c, nominal = chunk_ref[n], row_ref[n]
    start = pl.multiple_of(jnp.minimum(nominal, length - WIN), 16)
    rows = pl.ds(start, WIN)
    keys = pl.ds(pl.multiple_of(c * KC, KC), KC)
    row_id = lax.broadcasted_iota(jnp.int32, (WIN, 128), 0) + start
    keep = jnp.logical_and(segc_ref[rows, :] == segk_ref[pl.ds(c, 1), :], row_id >= nominal)
    bias = jnp.where(keep, 0.0, NEG)
    return rows, keys, jnp.concatenate([bias, bias], axis=1)


def staged(units, first, second, third):
    raw, done = first(units[0]), None
    for n in range(len(units) + 1):
        upcoming = first(units[n + 1]) if n + 1 < len(units) else None
        fresh = second(units[n], raw) if n < len(units) else None
        if done is not None:
            third(units[n - 1], done)
        raw, done = upcoming, fresh


def attend_kernel(
    lo_ref, nw_ref, x_ref, wq_hbm, wk_hbm, wv_hbm, pk_ref, pv_ref, segc_ref, segk_ref,
    q_hbm, k_hbm, v_hbm, att_ref, lse_ref,
    w_ref, q_ref, k_ref, v_ref, l_ref, acc_ref, chunk_ref, row_ref, in_sems, out_sems,
):
    length, lanes = x_ref.shape
    parts = [slice(g * QUAD, (g + 1) * QUAD) for g in range(lanes // QUAD)]
    spans = [slice(r * WIN, (r + 1) * WIN) for r in range(length // WIN)]
    loads = [pltpu.make_async_copy(w, w_ref.at[n], in_sems.at[n]) for n, w in enumerate((wq_hbm, wk_hbm, wv_hbm))]
    stores = [
        pltpu.make_async_copy(a, b, out_sems.at[n])
        for n, (a, b) in enumerate(((q_ref, q_hbm), (k_ref, k_hbm), (v_ref, v_hbm)))
    ]
    for load in loads:
        load.start()
    count = list_items(lo_ref, nw_ref, chunk_ref, row_ref, length)
    ones = head_ones()
    tops = []
    for n, out_ref in enumerate((q_ref, k_ref, v_ref)):
        loads[n].wait()
        top = []
        for cols in parts:
            value = dot(x_ref[...], w_ref[n, :, cols])
            value = (value * HEAD_SCALE if n == 0 else value).astype(bf16)
            out_ref[:, cols] = value
            if n < 2:
                size = dot(value * value, ones)
                size = jnp.max(size, axis=0, keepdims=True)
                if n == 1:
                    extra = pk_ref[:, cols]
                    size = jnp.maximum(size, jnp.max(dot(extra * extra, ones), axis=0, keepdims=True))
                top.append(size)
        tops.append(top)
        stores[n].start()
    bound = jnp.max(jnp.concatenate([a * b for a, b in zip(tops[0], tops[1])], axis=1))
    safe = bound < SAFE * SAFE
    pairs = (count + 1) // 2

    def item(n):
        return item_at(n, chunk_ref, row_ref, segc_ref, segk_ref, length)

    def sweep(shift):
        bdk = [block_diag(pk_ref[:, cols]) for cols in parts]
        bdv = [block_diag(pv_ref[:, cols]) for cols in parts]
        ids = range(len(parts))

        def moved(s, rows, cols):
            return s if shift is None else s - shift[rows, cols]

        def start_third(unit, p):
            rows, g = unit
            l_ref[rows, parts[g]] = p
            acc_ref[rows, parts[g]] = dot(p.astype(bf16), bdv[g])

        staged(
            [(rows, g) for g in ids for rows in spans],
            lambda u: dot(q_ref[u[0], parts[u[1]]], bdk[u[1]], NT),
            lambda u, s: jnp.exp(moved(s, u[0], parts[u[1]])),
            start_third,
        )

        @pl.loop(0, pairs)
        def _(n):
            def third(unit, p):
                (rows, keys, _), g = unit
                l_ref[rows, parts[g]] += p
                acc_ref[rows, parts[g]] += dot(p.astype(bf16), block_diag(v_ref[keys, parts[g]]))

            staged(
                [(one, g) for one in (item(2 * n), item(2 * n + 1)) for g in ids],
                lambda u: dot(q_ref[u[0][0], parts[u[1]]], block_diag(k_ref[u[0][1], parts[u[1]]]), NT),
                lambda u, s: jnp.exp(moved(s, u[0][0], parts[u[1]]) + u[0][2]),
                third,
            )

        for rows in spans:
            for cols in parts:
                total = head_sum(l_ref[rows, cols], ones)
                att_ref[rows, cols] = (acc_ref[rows, cols] / total).astype(bf16)
                low = jnp.log(total)
                lse_ref[rows, cols] = low if shift is None else low + shift[rows, cols]

    @pl.when(safe)
    def _():
        sweep(None)

    @pl.when(jnp.logical_not(safe))
    def _():
        for cols in parts:
            bdk = block_diag(pk_ref[:, cols])
            for rows in spans:
                lse_ref[rows, cols] = dot(q_ref[rows, cols], bdk, NT)

        @pl.loop(0, count)
        def _(n):
            rows, keys, bias = item(n)
            for cols in parts:
                s = dot(q_ref[rows, cols], block_diag(k_ref[keys, cols]), NT) + bias
                lse_ref[rows, cols] = jnp.maximum(lse_ref[rows, cols], s)

        @pl.loop(0, length // WIN)
        def _(r):
            rows = pl.ds(pl.multiple_of(r * WIN, WIN), WIN)
            for t in range(lanes // 128):
                cols = slice(t * 128, (t + 1) * 128)
                lse_ref[rows, cols] = head_max(lse_ref[rows, cols])

        sweep(lse_ref)

    for store in stores:
        store.wait()


def attend(lo, nw, x, wq, wk, wv, pk, pv, segc, segk):
    length, lanes = x.shape
    low = jax.ShapeDtypeStruct((length, lanes), bf16)
    wide = jax.ShapeDtypeStruct((length, lanes), f32)
    return pl.pallas_call(
        attend_kernel,
        out_shape=(low, low, low, low, wide),
        in_specs=[sm(), sm(), vm(), hbm(), hbm(), hbm(), vm(), vm(), vm(), vm()],
        out_specs=(hbm(), hbm(), hbm(), vm(), vm()),
        scratch_shapes=[pltpu.VMEM((3, lanes, lanes), bf16)]
        + [pltpu.VMEM((length, lanes), bf16)] * 3
        + [pltpu.VMEM((length, lanes), f32)] * 2
        + [pltpu.SMEM((ITEMS,), jnp.int32)] * 2
        + [pltpu.SemaphoreType.DMA((3,))] * 2,
        compiler_params=pltpu.CompilerParams(vmem_limit_bytes=VMEM),
        cost_estimate=cost(24 * length * lanes * lanes),
        name="attend",
    )(lo, nw, x, wq, wk, wv, pk, pv, segc, segk)


def attend_back_kernel(
    lo_ref, nw_ref, q_ref, k_ref, v_ref, g_ref, lse_ref, delta_ref, ds_ref, pk_ref, segc_ref, segk_ref,
    dq_ref, dk_ref, dv_ref, dq_acc, dk_acc, dv_acc, chunk_ref, row_ref,
):
    length, lanes = q_ref.shape
    parts = [slice(g * QUAD, (g + 1) * QUAD) for g in range(lanes // QUAD)]
    spans = [slice(r * WIN, (r + 1) * WIN) for r in range(length // WIN)]
    count = list_items(lo_ref, nw_ref, chunk_ref, row_ref, length)
    for cols in parts:
        bdk = block_diag(pk_ref[:, cols])
        for rows in spans:
            dq_acc[rows, cols] = dot(ds_ref[rows, cols], bdk)
    dk_acc[...] = jnp.zeros_like(dk_acc)
    dv_acc[...] = jnp.zeros_like(dv_acc)
    ids = range(len(parts))

    @pl.loop(0, (count + 1) // 2)
    def _(n):
        def first(unit):
            (rows, keys, _), g = unit
            cols = parts[g]
            s = dot(q_ref[rows, cols], block_diag(k_ref[keys, cols]), NT)
            return s, dot(g_ref[rows, cols], block_diag(v_ref[keys, cols]), NT)

        def second(unit, pair):
            (rows, _, bias), g = unit
            cols = parts[g]
            p = jnp.exp(pair[0] + bias - lse_ref[rows, cols])
            return p.astype(bf16), (p * (pair[1] - delta_ref[rows, cols])).astype(bf16)

        def third(unit, pair):
            (rows, keys, _), g = unit
            cols = parts[g]
            dv_acc[keys, cols] += diag_of(dot(pair[0], g_ref[rows, cols], TN))
            dk_acc[keys, cols] += diag_of(dot(pair[1], q_ref[rows, cols], TN))
            dq_acc[rows, cols] += dot(pair[1], block_diag(k_ref[keys, cols]))

        items = [item_at(2 * n + i, chunk_ref, row_ref, segc_ref, segk_ref, length) for i in range(2)]
        staged([(one, g) for one in items for g in ids], first, second, third)

    for rows in spans:
        dq_ref[rows, :] = (dq_acc[rows, :] * HEAD_SCALE).astype(bf16)
        dk_ref[rows, :] = dk_acc[rows, :].astype(bf16)
        dv_ref[rows, :] = dv_acc[rows, :].astype(bf16)


def part_of(array, width, part):
    return pl.BlockSpec((array.shape[0], width), lambda i: (0, part))


def whole_of(array):
    return pl.BlockSpec(array.shape, lambda i: (0, 0))


def attend_back(lo, nw, q, k, v, g, lse, delta, ds, pk, segc, segk, width, part):
    length = q.shape[0]
    return pl.pallas_call(
        attend_back_kernel,
        grid=(1,),
        out_shape=(jax.ShapeDtypeStruct((length, width), bf16),) * 3,
        in_specs=[sm(), sm()]
        + [part_of(a, width, part) for a in (q, k, v, g, lse, delta, ds, pk)]
        + [whole_of(segc), whole_of(segk)],
        out_specs=(pl.BlockSpec((length, width), lambda i: (0, 0)),) * 3,
        scratch_shapes=[pltpu.VMEM((length, width), f32)] * 3 + [pltpu.SMEM((ITEMS,), jnp.int32)] * 2,
        compiler_params=pltpu.CompilerParams(vmem_limit_bytes=VMEM),
        cost_estimate=cost(length * width * 30000),
        name="attend_back",
    )(lo, nw, q, k, v, g, lse, delta, ds, pk, segc, segk)


HID = 512


def mean_of(x):
    return jnp.mean(x, axis=-1, keepdims=True)


def centre(x):
    centred = x - mean_of(x)
    inv = lax.rsqrt(mean_of(centred * centred) + epsilon_norm)
    return centred * inv, inv


def pull_norm(pull, hat, inv):
    return inv * (pull - mean_of(pull) - hat * mean_of(pull * hat))


def gelu_pair(x):
    t = 1.0 / (1.0 + (0.3275911 * 0.7071067811865476) * jnp.abs(x))
    bell = jnp.exp(-0.5 * (x * x))
    poly = t * (0.127414796 + t * (-0.142248368 + t * (0.7107068705 + t * (-0.7265760135 + t * 0.5307027145))))
    tail = poly * bell
    phi = jnp.where(x < 0.0, tail, 1.0 - tail)
    return x * phi, phi + x * (0.3989422804014327 * bell)


def blocks_of(pieces):
    blocks, block, room = [], [], HID
    for piece in pieces:
        row = 0
        while row < piece.shape[1]:
            rows = min(room, piece.shape[1] - row)
            block.append((piece, row, rows))
            row, room = row + rows, room - rows
            if room == 0:
                blocks.append(block)
                block, room = [], HID
    return blocks


def most_of(pieces):
    return max(len(block) for block in blocks_of(pieces))


def block_copies(block, buffer, sems, slot):
    copies, place = [], 0
    for n, (piece, row, rows) in enumerate(block):
        source = piece.at[:, row : row + rows]
        copies.append(pltpu.make_async_copy(source, buffer.at[slot, :, place : place + rows], sems.at[slot, n]))
        place += rows
    return copies


def begin(copies):
    for copy in copies:
        copy.start()


def finish(copies):
    for copy in copies:
        copy.wait()


def forward_block(low_ref, weights, sum_ref, slope_ref, cols):
    def second(rows, x):
        act, slope = gelu_pair(x)
        slope_ref[rows, cols] = slope.astype(bf16)
        return act.astype(bf16)

    def third(rows, act):
        sum_ref[rows, :] += dot(act, weights[1])

    spans = [slice(r, r + WIN) for r in range(0, low_ref.shape[0], WIN)]
    staged(spans, lambda rows: dot(low_ref[rows, :], weights[0], NT), second, third)


def ffn_kernel(*refs, count):
    att_ref, tok_ref, w_out_ref, gain_ref = refs[:4]
    blocks = blocks_of(refs[4 : 4 + count])
    hat_ref, inv_ref, low_ref, sum_ref, slope_ref, buffer, sems = refs[4 + count :]
    copies = [block_copies(block, buffer, sems, b % 2) for b, block in enumerate(blocks)]
    begin(copies[0])

    def second(rows, x):
        hat, inv = centre(tok_ref[rows, :].astype(f32) + x)
        hat_ref[rows, :] = hat
        inv_ref[rows, :] = jnp.broadcast_to(inv, (WIN, 128))
        normed = gain_ref[...] * hat
        sum_ref[rows, :] = normed
        low_ref[rows, :] = normed.astype(bf16)

    spans = [slice(r, r + WIN) for r in range(0, att_ref.shape[0], WIN)]
    staged(spans, lambda rows: dot(att_ref[rows, :], w_out_ref[...]), second, lambda rows, x: None)
    for b in range(len(blocks)):
        if b + 1 < len(blocks):
            begin(copies[b + 1])
        finish(copies[b])
        forward_block(low_ref, buffer.at[b % 2], sum_ref, slope_ref, slice(b * HID, (b + 1) * HID))


def ffn_forward(att, tokens, w_out, gain, pieces):
    length, lanes = att.shape
    hidden = sum(piece.shape[1] for piece in pieces)
    wide = jax.ShapeDtypeStruct((length, lanes), f32)
    return pl.pallas_call(
        functools.partial(ffn_kernel, count=len(pieces)),
        out_shape=(
            wide,
            jax.ShapeDtypeStruct((length, 128), f32),
            jax.ShapeDtypeStruct((length, lanes), bf16),
            wide,
            jax.ShapeDtypeStruct((length, hidden), bf16),
        ),
        in_specs=[vm()] * 4 + [hbm()] * len(pieces),
        out_specs=(vm(),) * 5,
        scratch_shapes=[pltpu.VMEM((2, 2, HID, lanes), bf16), pltpu.SemaphoreType.DMA((2, most_of(pieces)))],
        compiler_params=pltpu.CompilerParams(vmem_limit_bytes=VMEM),
        cost_estimate=cost(4 * length * lanes * (hidden + lanes)),
        name="ffn_forward",
    )(att, tokens, w_out, gain, *pieces)


def more_kernel(low_ref, start_ref, *refs, count):
    blocks = blocks_of(refs[:count])
    sum_ref, slope_ref, buffer, sems = refs[count:]
    copies = [block_copies(block, buffer, sems, b % 2) for b, block in enumerate(blocks)]
    begin(copies[0])
    sum_ref[...] = start_ref[...]
    for b in range(len(blocks)):
        if b + 1 < len(blocks):
            begin(copies[b + 1])
        finish(copies[b])
        forward_block(low_ref, buffer.at[b % 2], sum_ref, slope_ref, slice(b * HID, (b + 1) * HID))


def ffn_more(low, start, pieces):
    length, lanes = low.shape
    hidden = sum(piece.shape[1] for piece in pieces)
    return pl.pallas_call(
        functools.partial(more_kernel, count=len(pieces)),
        out_shape=(jax.ShapeDtypeStruct((length, lanes), f32), jax.ShapeDtypeStruct((length, hidden), bf16)),
        in_specs=[vm()] * 2 + [hbm()] * len(pieces),
        out_specs=(vm(),) * 2,
        scratch_shapes=[pltpu.VMEM((2, 2, HID, lanes), bf16), pltpu.SemaphoreType.DMA((2, most_of(pieces)))],
        compiler_params=pltpu.CompilerParams(vmem_limit_bytes=VMEM),
        cost_estimate=cost(4 * length * lanes * hidden),
        name="ffn_more",
    )(low, start, *pieces)


def middle_kernel(*refs, early, late, groups):
    low_ref, inv_ref, gain_two_ref, gain_one_ref, pk_ref, pv_ref = refs[:6]
    sum_hbm, cot_hbm, hat_hbm, w_out_hbm, q_hbm, att_hbm, lse_hbm = refs[6:13]
    slopes = refs[13 : 13 + groups]
    pieces = refs[13 + groups : 13 + groups + early + late]
    refs = refs[13 + groups + early + late :]
    (layer_hbm, one_hbm, g_hbm, delta_hbm, ds_hbm, dpk_ref, dpv_ref) = refs[:7]
    (
        acc_ref, cot_ref, hat_ref, w_out_ref, q_ref, att_ref, lse_ref, layer_ref, one_ref, g_ref, delta_ref, ds_ref,
        grad_ref, late_ref, buffer, sbuf, sems, ssems, in_sems, out_sems,
    ) = refs[7:]
    length, lanes = low_ref.shape
    spans = [slice(r, r + WIN) for r in range(0, length, WIN)]
    parts = [slice(c, c + QUAD) for c in range(0, lanes, QUAD)]
    first_blocks, last_blocks = blocks_of(pieces[:early]), blocks_of(pieces[early:])
    order = last_blocks + first_blocks + last_blocks
    copies = [block_copies(block, buffer, sems, n % 2) for n, block in enumerate(order)]
    skip = len(last_blocks)
    slabs = [slope.at[:, c : c + HID] for slope in slopes for c in range(0, slope.shape[1], HID)]
    for n, source in enumerate(slabs, skip):
        copies[n].append(pltpu.make_async_copy(source, sbuf.at[n % 2], ssems.at[n % 2]))
    sources = (sum_hbm, cot_hbm, hat_hbm, w_out_hbm, q_hbm, att_hbm, lse_hbm)
    places = (acc_ref, cot_ref, hat_ref, w_out_ref, q_ref, att_ref, lse_ref)
    loads = [pltpu.make_async_copy(a, b, in_sems.at[n]) for n, (a, b) in enumerate(zip(sources, places))]
    results = (layer_ref, one_ref, g_ref, delta_ref, ds_ref)
    targets = (layer_hbm, one_hbm, g_hbm, delta_hbm, ds_hbm)
    stores = [pltpu.make_async_copy(a, b, out_sems.at[n]) for n, (a, b) in enumerate(zip(results, targets))]
    begin(copies[0])
    begin(loads[:1])

    def enter(n):
        if n + 1 < len(order):
            begin(copies[n + 1])
        if n == 0:
            finish(loads[:1])
            begin(loads[1:])
        finish(copies[n])
        return buffer.at[n % 2]

    for n in range(skip):
        forward_block(low_ref, enter(n), acc_ref, late_ref, slice(n * HID, (n + 1) * HID))

    finish(loads[1:3])
    for n in range(skip, len(order)):
        weights = enter(n)
        past = n - skip - len(first_blocks)

        def first(rows):
            if n == skip:
                hat, inv = centre(acc_ref[rows, :])
                layer_ref[rows, :] = (gain_two_ref[...] * hat).astype(bf16)
                grad = pull_norm(cot_ref[rows, :].astype(f32) * gain_two_ref[...], hat, inv)
                acc_ref[rows, :] = grad
                grad_ref[rows, :] = grad.astype(bf16)
            return dot(grad_ref[rows, :], weights[1], NT)

        def second(rows, x):
            slope = sbuf[n % 2, rows, :] if past < 0 else late_ref[rows, past * HID : (past + 1) * HID]
            return (x * slope.astype(f32)).astype(bf16)

        def third(rows, x):
            acc_ref[rows, :] += dot(x, weights[0])

        staged(spans, first, second, third)
        if n == skip:
            begin(stores[:1])
    finish(loads[3:])

    def first(rows):
        grad = pull_norm(acc_ref[rows, :] * gain_one_ref[...], hat_ref[rows, :], inv_ref[rows, 0:1])
        one_ref[rows, :] = grad
        return grad.astype(bf16)

    def second(rows, grad):
        g_ref[rows, :] = dot(grad, w_out_ref[...], NT).astype(bf16)

    staged(spans, first, second, lambda rows, x: None)
    begin(stores[1:3])

    ones = head_ones()
    sums = {}

    def first(unit):
        g, rows = unit
        cols = parts[g]
        up = g_ref[rows, cols]
        delta = head_sum(up.astype(f32) * att_ref[rows, cols].astype(f32), ones)
        return dot(q_ref[rows, cols], block_diag(pk_ref[:, cols]), NT), dot(up, block_diag(pv_ref[:, cols]), NT), delta

    def second(unit, three):
        g, rows = unit
        cols = parts[g]
        delta_ref[rows, cols] = three[2]
        p = jnp.exp(three[0] - lse_ref[rows, cols])
        ds = (p * (three[1] - three[2])).astype(bf16)
        ds_ref[rows, cols] = ds
        return p.astype(bf16), ds

    def third(unit, pair):
        g, rows = unit
        cols = parts[g]
        dpv, dpk = diag_of(dot(pair[0], g_ref[rows, cols], TN)), diag_of(dot(pair[1], q_ref[rows, cols], TN))
        if rows.start:
            dpv, dpk = sums[g][0] + dpv, sums[g][1] + dpk
        sums[g] = (dpv, dpk)
        if rows.stop == length:
            dpv_ref[:, cols], dpk_ref[:, cols] = dpv, dpk

    staged([(g, rows) for g in range(len(parts)) for rows in spans], first, second, third)
    begin(stores[3:])
    finish(stores)


def middle(low, inv, gain_two, gain_one, pk, pv, total, cot, hat, w_out, q, att, lse, slopes, early, late):
    length, lanes = low.shape
    slots = pk.shape[0]
    late_units = sum(piece.shape[1] for piece in late)
    tall = (length, lanes)
    small = jax.ShapeDtypeStruct((slots, lanes), f32)
    holds = [f32, bf16, f32, None, bf16, bf16, f32, bf16, f32, bf16, f32, bf16, bf16]
    return pl.pallas_call(
        functools.partial(middle_kernel, early=len(early), late=len(late), groups=len(slopes)),
        out_shape=tuple(jax.ShapeDtypeStruct(tall, t) for t in (bf16, f32, bf16, f32, bf16)) + (small, small),
        in_specs=[vm()] * 6 + [hbm()] * (7 + len(slopes) + len(early) + len(late)),
        out_specs=(hbm(),) * 5 + (vm(), vm()),
        scratch_shapes=[pltpu.VMEM((lanes, lanes), bf16) if t is None else pltpu.VMEM(tall, t) for t in holds]
        + [
            pltpu.VMEM((length, late_units), bf16),
            pltpu.VMEM((2, 2, HID, lanes), bf16),
            pltpu.VMEM((2, length, HID), bf16),
            pltpu.SemaphoreType.DMA((2, most_of(early + late))),
            pltpu.SemaphoreType.DMA((2,)),
            pltpu.SemaphoreType.DMA((7,)),
            pltpu.SemaphoreType.DMA((5,)),
        ],
        compiler_params=pltpu.CompilerParams(vmem_limit_bytes=VMEM),
        cost_estimate=cost(40 * length * lanes * lanes),
        name="middle",
    )(low, inv, gain_two, gain_one, pk, pv, total, cot, hat, w_out, q, att, lse, *slopes, *early, *late)


def project_kernel(*refs, halves):
    grads, weights, one_ref, out_ref = refs[: 3 * halves], refs[3 * halves : 6 * halves], refs[-2], refs[-1]
    total = one_ref[...]
    for grad, weight in zip(grads, weights):
        total = total + dot(grad[...], weight[...], NT)
    out_ref[...] = total


def project_back(grads, weights, grad_one):
    length, lanes = grad_one.shape
    halves = len(grads)
    width = lanes // halves
    flat = [grad for half in grads for grad in half]
    slabs = [pl.BlockSpec((lanes, width), lambda i, n=n: (0, n)) for n in range(halves) for _ in range(3)]
    tall = pl.BlockSpec((WIN, lanes), lambda i: (i, 0))
    return pl.pallas_call(
        functools.partial(project_kernel, halves=halves),
        grid=(length // WIN,),
        out_shape=jax.ShapeDtypeStruct((length, lanes), f32),
        in_specs=[pl.BlockSpec((WIN, width), lambda i: (i, 0)) for _ in flat] + slabs + [tall],
        out_specs=tall,
        compiler_params=pltpu.CompilerParams(vmem_limit_bytes=VMEM),
        cost_estimate=cost(6 * length * lanes * lanes),
        name="project_back",
    )(*flat, *(list(weights) * halves), grad_one)


def swap(x, axis, bit):
    return lax.ppermute(x, axis, [(i, i ^ bit) for i in range(lax.axis_size(axis))])


def swap_two(x, one, two):
    if one[0] == two[0]:
        return swap(x, one[0], one[1] | two[1])
    wide = {"dp": lax.axis_size("mp"), "mp": 1}
    mask = one[1] * wide[one[0]] + two[1] * wide[two[0]]
    count = lax.axis_size("dp") * lax.axis_size("mp")
    return lax.ppermute(x, ("dp", "mp"), [(i, i ^ mask) for i in range(count)])


def gather_plain(w_in, w_back):
    both = jnp.stack([w_in.T, w_back])
    part = both.shape[1] // lax.axis_size("dp")
    mine = lax.dynamic_slice_in_dim(both, lax.axis_index("dp") * part, part, 1)
    return lax.all_gather(mine, ("dp", "mp"), axis=1, tiled=True)


def own_weights(w_in, w_back):
    both = jnp.stack([w_in.T, w_back])
    half = both.shape[1] // 2
    dp = lax.axis_index("dp")
    own = lax.dynamic_slice_in_dim(both, lax.rem(dp, 2) * half, half, 1)
    unit = half // 2
    mine = lax.dynamic_slice_in_dim(own, dp // 2 * unit, unit, 1)
    return both, own, mine


def after(x, *others):
    return lax.optimization_barrier((x, *others))[0]


def with_other(pieces):
    return [each for piece in pieces for each in (piece, swap(piece, "dp", 1))]


def sum_everywhere(x):
    core = lax.rem(lax.axis_index("dp"), 2)
    half = x.shape[0] // 2
    keep = lax.dynamic_slice_in_dim(x, core * half, half, 0)
    give = lax.dynamic_slice_in_dim(x, (1 - core) * half, half, 0)
    part = keep + swap(give, "dp", 1)
    bits = [(axis, 1 << n) for axis in ("dp", "mp") for n in range(lax.axis_size(axis).bit_length() - 1)][1:]
    bits = sorted(bits, key=lambda pair: pair[1] if pair[0] == "mp" else 1)
    for n in range(0, len(bits), 2):
        low = part.astype(bf16)
        pairs = bits[n : n + 2]
        near = swap(low, *pairs[0]).astype(f32) + low.astype(f32)
        if len(pairs) == 2:
            far = swap(low, *pairs[1])
            both = swap_two(low, pairs[0], pairs[1])
            near = near + (far.astype(f32) + both.astype(f32))
        part = near
    other = swap(part, "dp", 1)
    return jnp.where(core == 0, jnp.concatenate([part, other]), jnp.concatenate([other, part]))


def on_device(
    tokens, segment_ids, w_query, w_key, w_value, w_out, gain_one, gain_two, w_in, w_back,
    prefix_master, moment_one, moment_two, cotangent,
):
    stepwise = lax.axis_size("dp") == 4 and lax.axis_size("mp") == 8
    if stepwise:
        both, own, mine = own_weights(w_in, w_back)
        unit = mine.shape[1]
        z_two, z_three = swap(mine, "mp", 4), swap(mine, "mp", 6)
        z_one, x_own = swap(own, "mp", 2), swap(own, "mp", 1)
    prefix_low = prefix_master.astype(bf16)
    prefix_keys, prefix_vals = prefix_low[0], prefix_low[1]
    first_gain, second_gain = gain_one[None, :], gain_two[None, :]
    lo, nw, segc, segk = windows(segment_ids[0])
    queries, keys_own, values_own, attended, lse = attend(
        lo, nw, tokens, w_query, w_key, w_value, prefix_keys, prefix_vals, segc, segk
    )
    if stepwise:
        z_one, z_two, x_own, attended = lax.optimization_barrier((z_one, z_two, x_own, attended))
        x_two, y_two = swap(z_two, "mp", 1), swap(z_two, "dp", 2)
        x_one = swap(z_one[:, :unit], "mp", 1)
        normed = ffn_forward(attended, tokens, w_out, first_gain, [both])
        z_one, z_three, x_two, *normed = lax.optimization_barrier((z_one, z_three, x_two, *normed))
        x_three, y_three = swap(z_three, "mp", 1), swap(z_three, "dp", 2)
        yx_two = swap(x_two, "dp", 2)
        hat, inv, normed_low, total, slope = normed
        more = with_other([z_one, x_own])
        total, slope_more = ffn_more(normed_low, total, more)
        x_three, z_one, total = lax.optimization_barrier((x_three, z_one, total))
        yx_three = swap(x_three, "dp", 2)
        x_last = swap(z_one[:, unit:], "mp", 1)
        early = [both] + more
        slopes = [slope, slope_more]
        late = with_other([z_two, x_two, y_two, x_one, z_three, y_three, yx_two, x_three, x_last, yx_three])
    else:
        every = gather_plain(w_in, w_back)
        cut = every.shape[1] * 3 // 8
        early, late = [every[:, :cut]], [every[:, cut:]]
        hat, inv, normed_low, total, slope = ffn_forward(attended, tokens, w_out, first_gain, early)
        slopes = [slope]
    layer_output, grad_one, grad_att, delta, ds_prefix, dpk, dpv = middle(
        normed_low, inv, second_gain, first_gain, prefix_keys, prefix_vals,
        total, cotangent, hat, w_out, queries, attended, lse, slopes, early, late,
    )
    prefix_grad = sum_everywhere(jnp.stack([dpk, dpv]))
    halves = 2
    width = tokens.shape[1] // halves
    grads = [
        attend_back(
            lo, nw, queries, keys_own, values_own, grad_att, lse, delta, ds_prefix, prefix_keys, segc, segk, width, part
        )
        for part in range(halves)
    ]
    input_grad = project_back(grads, (w_query, w_key, w_value), grad_one)
    new_first = beta_one * moment_one + (1.0 - beta_one) * prefix_grad
    new_second = beta_two * moment_two + (1.0 - beta_two) * prefix_grad * prefix_grad
    first_hat = new_first / (1.0 - beta_one**STEP)
    second_hat = new_second / (1.0 - beta_two**STEP)
    new_master = prefix_master * (1.0 - learn_rate * weight_decay) - learn_rate * first_hat / (
        jnp.sqrt(second_hat) + epsilon_adam
    )
    return (layer_output, input_grad, new_master, new_first, new_second, new_master.astype(bf16))


def solution(mesh):
    rows = P(("dp", "mp"), None)
    return jax.shard_map(
        on_device,
        mesh=mesh,
        in_specs=(rows, rows, P(), P(), P(), P(), P(), P(), P(None, "mp"), P("mp", None), P(), P(), P(), rows),
        out_specs=(rows, rows, P(), P(), P(), P()),
        check_vma=False,
    )
```

```python
import functools

import jax
import jax.numpy as jnp
from jax import lax
from jax.experimental import pallas as pl
from jax.experimental.pallas import tpu as pltpu
from jax.sharding import PartitionSpec as P

f32, bf16 = jnp.float32, jnp.bfloat16
STEP = 5
epsilon_norm = 1e-05
learn_rate = 1.0
weight_decay = 0.01
beta_one = 0.9
beta_two = 0.999
epsilon_adam = 1e-08
HEAD_SCALE = 0.125
NEG = -1e30
WIN = 256
KC = 64
QUAD = 256
LEAST, MOST = 1e-25, 1e30
ITEMS = 64
VMEM = 60 << 20
NN = (((1,), (0,)), ((), ()))
NT = (((1,), (1,)), ((), ()))
TN = (((0,), (0,)), ((), ()))


def dot(a, b, d=NN):
    return lax.dot_general(a, b, d, preferred_element_type=f32)


def vm():
    return pl.BlockSpec(memory_space=pltpu.VMEM)


def sm():
    return pl.BlockSpec(memory_space=pltpu.SMEM)


def hbm():
    return pl.BlockSpec(memory_space=pl.ANY)


def cost(flops, moved=8 << 20):
    return pl.CostEstimate(flops=4 * flops, bytes_accessed=moved, transcendentals=0)


def part_of(array, width, part):
    return pl.BlockSpec((array.shape[0], width), lambda i: (0, part))


def whole_of(array):
    return pl.BlockSpec(array.shape, lambda i: (0, 0))


def block_diag(piece):
    lane = lax.broadcasted_iota(jnp.int32, piece.shape, 1) // 64
    zero = jnp.zeros_like(piece)
    return jnp.concatenate([jnp.where(lane == h, piece, zero) for h in range(4)], axis=0)


def diag_of(full):
    lane = lax.broadcasted_iota(jnp.int32, (KC, 128), 1) < 64
    left = jnp.where(lane, full[0:64, 0:128], full[64:128, 0:128])
    right = jnp.where(lane, full[128:192, 128:256], full[192:256, 128:256])
    return jnp.concatenate([left, right], axis=1)


def head_ones():
    row = lax.broadcasted_iota(jnp.int32, (QUAD, QUAD), 0) // 64
    lane = lax.broadcasted_iota(jnp.int32, (QUAD, QUAD), 1) // 64
    return jnp.where(row == lane, 1.0, 0.0).astype(bf16)


def head_sum(x, ones):
    high = x.astype(bf16)
    return dot(high, ones) + dot((x - high.astype(f32)).astype(bf16), ones)


def head_max(x):
    lane = lax.broadcasted_iota(jnp.int32, x.shape, 1) < 64
    a = jnp.max(jnp.where(lane, x, NEG), axis=1, keepdims=True)
    b = jnp.max(jnp.where(lane, NEG, x), axis=1, keepdims=True)
    return jnp.where(lane, a, b)


def windows(seg):
    length = seg.shape[0]
    by = seg.reshape(length // KC, KC)
    first, last = by[:, 0], by[:, -1]
    lo = jnp.sum((seg[None, :] < first[:, None]).astype(jnp.int32), axis=1)
    hi = jnp.sum((seg[None, :] <= last[:, None]).astype(jnp.int32), axis=1)
    lo = lo // 16 * 16
    nw = (hi - lo + WIN - 1) // WIN
    segc = jnp.broadcast_to(seg[:, None], (length, 128))
    segk = jnp.concatenate([by, by], axis=1)
    return lo, nw, segc, segk


def list_items(lo_ref, nw_ref, chunk_ref, row_ref, length):
    def chunk(c, count):
        def one(w, count):
            chunk_ref[count] = c
            row_ref[count] = lo_ref[c] + w * WIN
            return count + 1

        return lax.fori_loop(0, nw_ref[c], one, count)

    count = lax.fori_loop(0, length // KC, chunk, 0)
    for n in range(2):
        chunk_ref[count + n] = 0
        row_ref[count + n] = length
    return count


def item_at(n, chunk_ref, row_ref, segc_ref, segk_ref, length):
    c, nominal = chunk_ref[n], row_ref[n]
    start = pl.multiple_of(jnp.minimum(nominal, length - WIN), 16)
    rows = pl.ds(start, WIN)
    keys = pl.ds(pl.multiple_of(c * KC, KC), KC)
    row_id = lax.broadcasted_iota(jnp.int32, (WIN, 128), 0) + start
    keep = jnp.logical_and(segc_ref[rows, :] == segk_ref[pl.ds(c, 1), :], row_id >= nominal)
    bias = jnp.where(keep, 0.0, NEG)
    return rows, keys, jnp.concatenate([bias, bias], axis=1)


def staged(units, first, second, third):
    raw, done = first(units[0]), None
    for n in range(len(units) + 1):
        upcoming = first(units[n + 1]) if n + 1 < len(units) else None
        fresh = second(units[n], raw) if n < len(units) else None
        if done is not None:
            third(units[n - 1], done)
        raw, done = upcoming, fresh


def attend_columns(count, q_ref, k_ref, v_ref, pk_ref, pv_ref, att_ref, lse_ref, l_ref, acc_ref, item, ones):
    length, width = att_ref.shape
    parts = [slice(c, c + QUAD) for c in range(0, width, QUAD)]
    spans = [slice(r, r + WIN) for r in range(0, length, WIN)]
    ids = range(len(parts))

    def sweep(shift):
        bdk = [block_diag(pk_ref[:, cols]) for cols in parts]
        bdv = [block_diag(pv_ref[:, cols]) for cols in parts]

        def moved(s, rows, cols):
            return s if shift is None else s - shift[rows, cols]

        def start_third(unit, p):
            rows, g = unit
            l_ref[rows, parts[g]] = p
            acc_ref[rows, parts[g]] = dot(p.astype(bf16), bdv[g])

        staged(
            [(rows, g) for g in ids for rows in spans],
            lambda u: dot(q_ref[u[0], parts[u[1]]], bdk[u[1]], NT),
            lambda u, s: jnp.exp(moved(s, u[0], parts[u[1]])),
            start_third,
        )

        @pl.loop(0, (count + 1) // 2)
        def _(n):
            def third(unit, p):
                (rows, keys, _), g = unit
                l_ref[rows, parts[g]] += p
                acc_ref[rows, parts[g]] += dot(p.astype(bf16), block_diag(v_ref[keys, parts[g]]))

            staged(
                [(one, g) for one in (item(2 * n), item(2 * n + 1)) for g in ids],
                lambda u: dot(q_ref[u[0][0], parts[u[1]]], block_diag(k_ref[u[0][1], parts[u[1]]]), NT),
                lambda u, s: jnp.exp(moved(s, u[0][0], parts[u[1]]) + u[0][2]),
                third,
            )

        least, most = [], []
        for rows in spans:
            for cols in parts:
                total = head_sum(l_ref[rows, cols], ones)
                att_ref[rows, cols] = (acc_ref[rows, cols] / total).astype(bf16)
                low = jnp.log(total)
                lse_ref[rows, cols] = low if shift is None else low + shift[rows, cols]
                least.append(jnp.min(total, axis=0, keepdims=True))
                most.append(jnp.max(total, axis=0, keepdims=True))
        return jnp.min(functools.reduce(jnp.minimum, least)), jnp.max(functools.reduce(jnp.maximum, most))

    least, most = sweep(None)

    @pl.when(jnp.logical_not(jnp.logical_and(least > LEAST, most < MOST)))
    def _():
        for cols in parts:
            bdk = block_diag(pk_ref[:, cols])
            for rows in spans:
                lse_ref[rows, cols] = dot(q_ref[rows, cols], bdk, NT)

        @pl.loop(0, count)
        def _(n):
            rows, keys, bias = item(n)
            for cols in parts:
                s = dot(q_ref[rows, cols], block_diag(k_ref[keys, cols]), NT) + bias
                lse_ref[rows, cols] = jnp.maximum(lse_ref[rows, cols], s)

        @pl.loop(0, length // WIN)
        def _(r):
            rows = pl.ds(pl.multiple_of(r * WIN, WIN), WIN)
            for c in range(0, width, 128):
                cols = slice(c, c + 128)
                lse_ref[rows, cols] = head_max(lse_ref[rows, cols])

        sweep(lse_ref)


def attend_first_kernel(
    lo_ref, nw_ref, x_ref, wq_hbm, wk_hbm, wv_hbm, pk_ref, pv_ref, segc_ref, segk_ref,
    q_hbm, k_hbm, v_hbm, att_ref, lse_ref,
    w_ref, q_ref, k_ref, v_ref, l_ref, acc_ref, chunk_ref, row_ref, in_sems, out_sems,
):
    length, lanes = x_ref.shape
    loads = [pltpu.make_async_copy(w, w_ref.at[n], in_sems.at[n]) for n, w in enumerate((wq_hbm, wk_hbm, wv_hbm))]
    stores = [
        pltpu.make_async_copy(a, b, out_sems.at[n])
        for n, (a, b) in enumerate(((q_ref, q_hbm), (k_ref, k_hbm), (v_ref, v_hbm)))
    ]
    for load in loads:
        load.start()
    count = list_items(lo_ref, nw_ref, chunk_ref, row_ref, length)
    for n, out_ref in enumerate((q_ref, k_ref, v_ref)):
        loads[n].wait()
        for c in range(0, lanes, QUAD):
            value = dot(x_ref[...], w_ref[n, :, c : c + QUAD])
            out_ref[:, c : c + QUAD] = (value * HEAD_SCALE if n == 0 else value).astype(bf16)
        stores[n].start()

    def item(n):
        return item_at(n, chunk_ref, row_ref, segc_ref, segk_ref, length)

    attend_columns(
        count, q_ref, k_ref, v_ref, pk_ref, pv_ref, att_ref, lse_ref, l_ref, acc_ref, item, head_ones()
    )
    for store in stores:
        store.wait()


def attend_rest_kernel(
    lo_ref, nw_ref, q_ref, k_ref, v_ref, pk_ref, pv_ref, segc_ref, segk_ref,
    att_ref, lse_ref, l_ref, acc_ref, chunk_ref, row_ref,
):
    length = q_ref.shape[0]
    count = list_items(lo_ref, nw_ref, chunk_ref, row_ref, length)

    def item(n):
        return item_at(n, chunk_ref, row_ref, segc_ref, segk_ref, length)

    attend_columns(
        count, q_ref, k_ref, v_ref, pk_ref, pv_ref, att_ref, lse_ref, l_ref, acc_ref, item, head_ones()
    )


def attend_first(lo, nw, x, wq, wk, wv, pk, pv, segc, segk, width):
    length, lanes = x.shape
    low = jax.ShapeDtypeStruct((length, lanes), bf16)
    return pl.pallas_call(
        attend_first_kernel,
        out_shape=(low, low, low, jax.ShapeDtypeStruct((length, width), bf16), jax.ShapeDtypeStruct((length, width), f32)),
        in_specs=[sm(), sm(), vm(), hbm(), hbm(), hbm(), vm(), vm(), vm(), vm()],
        out_specs=(hbm(), hbm(), hbm(), vm(), vm()),
        scratch_shapes=[pltpu.VMEM((3, lanes, lanes), bf16)]
        + [pltpu.VMEM((length, lanes), bf16)] * 3
        + [pltpu.VMEM((length, width), f32)] * 2
        + [pltpu.SMEM((ITEMS,), jnp.int32)] * 2
        + [pltpu.SemaphoreType.DMA((3,))] * 2,
        compiler_params=pltpu.CompilerParams(vmem_limit_bytes=VMEM),
        cost_estimate=cost(16 * length * lanes * lanes),
        name="attend_first",
    )(lo, nw, x, wq, wk, wv, pk, pv, segc, segk)


def attend_rest(lo, nw, q, k, v, pk, pv, segc, segk, width, part):
    length = q.shape[0]
    return pl.pallas_call(
        attend_rest_kernel,
        grid=(1,),
        out_shape=(jax.ShapeDtypeStruct((length, width), bf16), jax.ShapeDtypeStruct((length, width), f32)),
        in_specs=[sm(), sm()] + [part_of(a, width, part) for a in (q, k, v, pk, pv)] + [whole_of(segc), whole_of(segk)],
        out_specs=(pl.BlockSpec((length, width), lambda i: (0, 0)),) * 2,
        scratch_shapes=[pltpu.VMEM((length, width), f32)] * 2 + [pltpu.SMEM((ITEMS,), jnp.int32)] * 2,
        compiler_params=pltpu.CompilerParams(vmem_limit_bytes=VMEM),
        cost_estimate=cost(16000 * length * width),
        name="attend_rest",
    )(lo, nw, q, k, v, pk, pv, segc, segk)


def attend_back_kernel(
    lo_ref, nw_ref, q_ref, k_ref, v_ref, g_ref, lse_ref, delta_ref, ds_ref, pk_ref, segc_ref, segk_ref,
    dq_ref, dk_ref, dv_ref, dq_acc, dk_acc, dv_acc, chunk_ref, row_ref,
):
    length, lanes = q_ref.shape
    parts = [slice(g * QUAD, (g + 1) * QUAD) for g in range(lanes // QUAD)]
    spans = [slice(r * WIN, (r + 1) * WIN) for r in range(length // WIN)]
    count = list_items(lo_ref, nw_ref, chunk_ref, row_ref, length)
    for cols in parts:
        bdk = block_diag(pk_ref[:, cols])
        for rows in spans:
            dq_acc[rows, cols] = dot(ds_ref[rows, cols], bdk)
    dk_acc[...] = jnp.zeros_like(dk_acc)
    dv_acc[...] = jnp.zeros_like(dv_acc)
    ids = range(len(parts))

    @pl.loop(0, (count + 1) // 2)
    def _(n):
        def first(unit):
            (rows, keys, _), g = unit
            cols = parts[g]
            s = dot(q_ref[rows, cols], block_diag(k_ref[keys, cols]), NT)
            return s, dot(g_ref[rows, cols], block_diag(v_ref[keys, cols]), NT)

        def second(unit, pair):
            (rows, _, bias), g = unit
            cols = parts[g]
            p = jnp.exp(pair[0] + bias - lse_ref[rows, cols])
            return p.astype(bf16), (p * (pair[1] - delta_ref[rows, cols])).astype(bf16)

        def third(unit, pair):
            (rows, keys, _), g = unit
            cols = parts[g]
            dv_acc[keys, cols] += diag_of(dot(pair[0], g_ref[rows, cols], TN))
            dk_acc[keys, cols] += diag_of(dot(pair[1], q_ref[rows, cols], TN))
            dq_acc[rows, cols] += dot(pair[1], block_diag(k_ref[keys, cols]))

        items = [item_at(2 * n + i, chunk_ref, row_ref, segc_ref, segk_ref, length) for i in range(2)]
        staged([(one, g) for one in items for g in ids], first, second, third)

    for rows in spans:
        dq_ref[rows, :] = (dq_acc[rows, :] * HEAD_SCALE).astype(bf16)
        dk_ref[rows, :] = dk_acc[rows, :].astype(bf16)
        dv_ref[rows, :] = dv_acc[rows, :].astype(bf16)


def attend_back(lo, nw, q, k, v, g, lse, delta, ds, pk, segc, segk, width, part):
    length = q.shape[0]
    return pl.pallas_call(
        attend_back_kernel,
        grid=(1,),
        out_shape=(jax.ShapeDtypeStruct((length, width), bf16),) * 3,
        in_specs=[sm(), sm()]
        + [part_of(a, width, part) for a in (q, k, v, g)]
        + [whole_of(lse)]
        + [part_of(a, width, part) for a in (delta, ds, pk)]
        + [whole_of(segc), whole_of(segk)],
        out_specs=(pl.BlockSpec((length, width), lambda i: (0, 0)),) * 3,
        scratch_shapes=[pltpu.VMEM((length, width), f32)] * 3 + [pltpu.SMEM((ITEMS,), jnp.int32)] * 2,
        compiler_params=pltpu.CompilerParams(vmem_limit_bytes=VMEM),
        cost_estimate=cost(length * width * 30000),
        name="attend_back",
    )(lo, nw, q, k, v, g, lse, delta, ds, pk, segc, segk)


HID = 512


def mean_of(x):
    return jnp.mean(x, axis=-1, keepdims=True)


def centre(x):
    centred = x - mean_of(x)
    inv = lax.rsqrt(mean_of(centred * centred) + epsilon_norm)
    return centred * inv, inv


def pull_norm(pull, hat, inv):
    return inv * (pull - mean_of(pull) - hat * mean_of(pull * hat))


def gelu_pair(x):
    t = 1.0 / (1.0 + (0.3275911 * 0.7071067811865476) * jnp.abs(x))
    bell = jnp.exp(-0.5 * (x * x))
    poly = t * (0.127414796 + t * (-0.142248368 + t * (0.7107068705 + t * (-0.7265760135 + t * 0.5307027145))))
    tail = poly * bell
    phi = jnp.where(x < 0.0, tail, 1.0 - tail)
    return x * phi, phi + x * (0.3989422804014327 * bell)


def blocks_of(pieces):
    blocks, block, room = [], [], HID
    for piece in pieces:
        row = 0
        while row < piece.shape[1]:
            rows = min(room, piece.shape[1] - row)
            block.append((piece, row, rows))
            row, room = row + rows, room - rows
            if room == 0:
                blocks.append(block)
                block, room = [], HID
    return blocks


def most_of(pieces):
    return max(len(block) for block in blocks_of(pieces))


def block_copies(block, buffer, sems, slot):
    copies, place = [], 0
    for n, (piece, row, rows) in enumerate(block):
        source = piece.at[:, row : row + rows]
        copies.append(pltpu.make_async_copy(source, buffer.at[slot, :, place : place + rows], sems.at[slot, n]))
        place += rows
    return copies


def begin(copies):
    for copy in copies:
        copy.start()


def finish(copies):
    for copy in copies:
        copy.wait()


def forward_block(low_ref, weights, sum_ref, slope_ref, cols):
    def second(rows, x):
        act, slope = gelu_pair(x)
        slope_ref[rows, cols] = slope.astype(bf16)
        return act.astype(bf16)

    def third(rows, act):
        sum_ref[rows, :] += dot(act, weights[1])

    spans = [slice(r, r + WIN) for r in range(0, low_ref.shape[0], WIN)]
    staged(spans, lambda rows: dot(low_ref[rows, :], weights[0], NT), second, third)


def ffn_kernel(*refs, halves, count):
    atts, (tok_ref, w_out_ref, gain_ref), refs = refs[:halves], refs[halves : halves + 3], refs[halves + 3 :]
    blocks = blocks_of(refs[:count])
    hat_ref, inv_ref, low_ref, sum_ref, slope_ref, buffer, sems = refs[count:]
    width = atts[0].shape[1]
    copies = [block_copies(block, buffer, sems, b % 2) for b, block in enumerate(blocks)]
    begin(copies[0])

    def second(rows, x):
        hat, inv = centre(tok_ref[rows, :].astype(f32) + x)
        hat_ref[rows, :] = hat
        inv_ref[rows, :] = jnp.broadcast_to(inv, (WIN, 128))
        normed = gain_ref[...] * hat
        sum_ref[rows, :] = normed
        low_ref[rows, :] = normed.astype(bf16)

    def first(rows):
        return sum(dot(att_ref[rows, :], w_out_ref[n * width : (n + 1) * width, :]) for n, att_ref in enumerate(atts))

    spans = [slice(r, r + WIN) for r in range(0, tok_ref.shape[0], WIN)]
    staged(spans, first, second, lambda rows, x: None)
    for b in range(len(blocks)):
        if b + 1 < len(blocks):
            begin(copies[b + 1])
        finish(copies[b])
        forward_block(low_ref, buffer.at[b % 2], sum_ref, slope_ref, slice(b * HID, (b + 1) * HID))


def ffn_forward(att, tokens, w_out, gain, pieces):
    length, lanes = tokens.shape
    hidden = sum(piece.shape[1] for piece in pieces)
    wide = jax.ShapeDtypeStruct((length, lanes), f32)
    return pl.pallas_call(
        functools.partial(ffn_kernel, halves=len(att), count=len(pieces)),
        out_shape=(
            wide,
            jax.ShapeDtypeStruct((length, 128), f32),
            jax.ShapeDtypeStruct((length, lanes), bf16),
            wide,
            jax.ShapeDtypeStruct((length, hidden), bf16),
        ),
        in_specs=[vm()] * (len(att) + 3) + [hbm()] * len(pieces),
        out_specs=(vm(),) * 5,
        scratch_shapes=[pltpu.VMEM((2, 2, HID, lanes), bf16), pltpu.SemaphoreType.DMA((2, most_of(pieces)))],
        compiler_params=pltpu.CompilerParams(vmem_limit_bytes=VMEM),
        cost_estimate=cost(4 * length * lanes * (hidden + lanes)),
        name="ffn_forward",
    )(*att, tokens, w_out, gain, *pieces)


def more_kernel(low_ref, start_ref, *refs, count):
    blocks = blocks_of(refs[:count])
    sum_ref, slope_ref, buffer, sems = refs[count:]
    copies = [block_copies(block, buffer, sems, b % 2) for b, block in enumerate(blocks)]
    begin(copies[0])
    sum_ref[...] = start_ref[...]
    for b in range(len(blocks)):
        if b + 1 < len(blocks):
            begin(copies[b + 1])
        finish(copies[b])
        forward_block(low_ref, buffer.at[b % 2], sum_ref, slope_ref, slice(b * HID, (b + 1) * HID))


def ffn_more(low, start, pieces):
    length, lanes = low.shape
    hidden = sum(piece.shape[1] for piece in pieces)
    return pl.pallas_call(
        functools.partial(more_kernel, count=len(pieces)),
        out_shape=(jax.ShapeDtypeStruct((length, lanes), f32), jax.ShapeDtypeStruct((length, hidden), bf16)),
        in_specs=[vm()] * 2 + [hbm()] * len(pieces),
        out_specs=(vm(),) * 2,
        scratch_shapes=[pltpu.VMEM((2, 2, HID, lanes), bf16), pltpu.SemaphoreType.DMA((2, most_of(pieces)))],
        compiler_params=pltpu.CompilerParams(vmem_limit_bytes=VMEM),
        cost_estimate=cost(4 * length * lanes * hidden),
        name="ffn_more",
    )(low, start, *pieces)


def middle_kernel(*refs, halves, early, late, groups):
    low_ref, inv_ref, gain_two_ref, gain_one_ref, pk_ref, pv_ref = refs[:6]
    sum_hbm, cot_hbm, hat_hbm, w_out_hbm, q_hbm = refs[6:11]
    seen, refs = refs[11 : 11 + 2 * halves], refs[11 + 2 * halves :]
    slopes, pieces, refs = refs[:groups], refs[groups : groups + early + late], refs[groups + early + late :]
    (layer_hbm, one_hbm, g_hbm, delta_hbm, ds_hbm, dpk_ref, dpv_ref) = refs[:7]
    (
        acc_ref, cot_ref, hat_ref, w_out_ref, q_ref, att_ref, lse_ref, layer_ref, one_ref, g_ref, delta_ref, ds_ref,
        grad_ref, late_ref, buffer, sbuf, sems, ssems, in_sems, out_sems,
    ) = refs[7:]
    length, lanes = low_ref.shape
    spans = [slice(r, r + WIN) for r in range(0, length, WIN)]
    parts = [slice(c, c + QUAD) for c in range(0, lanes, QUAD)]
    first_blocks, last_blocks = blocks_of(pieces[:early]), blocks_of(pieces[early:])
    order = last_blocks + first_blocks + last_blocks
    copies = [block_copies(block, buffer, sems, n % 2) for n, block in enumerate(order)]
    skip = len(last_blocks)
    slabs = [slope.at[:, c : c + HID] for slope in slopes for c in range(0, slope.shape[1], HID)]
    for n, source in enumerate(slabs, skip):
        copies[n].append(pltpu.make_async_copy(source, sbuf.at[n % 2], ssems.at[n % 2]))
    sources = (sum_hbm, cot_hbm, hat_hbm, w_out_hbm, q_hbm, *seen)
    places = [acc_ref, cot_ref, hat_ref, w_out_ref, q_ref]
    for n in range(halves):
        cols = slice(n * (lanes // halves), (n + 1) * (lanes // halves))
        places += [att_ref.at[:, cols], lse_ref.at[:, cols]]
    loads = [pltpu.make_async_copy(a, b, in_sems.at[n]) for n, (a, b) in enumerate(zip(sources, places))]
    results = (layer_ref, one_ref, g_ref, delta_ref, ds_ref)
    targets = (layer_hbm, one_hbm, g_hbm, delta_hbm, ds_hbm)
    stores = [pltpu.make_async_copy(a, b, out_sems.at[n]) for n, (a, b) in enumerate(zip(results, targets))]
    begin(copies[0])
    begin(loads[:1])

    def enter(n):
        if n + 1 < len(order):
            begin(copies[n + 1])
        if n == 0:
            finish(loads[:1])
            begin(loads[1:])
        finish(copies[n])
        return buffer.at[n % 2]

    for n in range(skip):
        forward_block(low_ref, enter(n), acc_ref, late_ref, slice(n * HID, (n + 1) * HID))

    finish(loads[1:3])
    for n in range(skip, len(order)):
        weights = enter(n)
        past = n - skip - len(first_blocks)

        def first(rows):
            if n == skip:
                hat, inv = centre(acc_ref[rows, :])
                layer_ref[rows, :] = (gain_two_ref[...] * hat).astype(bf16)
                grad = pull_norm(cot_ref[rows, :].astype(f32) * gain_two_ref[...], hat, inv)
                acc_ref[rows, :] = grad
                grad_ref[rows, :] = grad.astype(bf16)
            return dot(grad_ref[rows, :], weights[1], NT)

        def second(rows, x):
            slope = sbuf[n % 2, rows, :] if past < 0 else late_ref[rows, past * HID : (past + 1) * HID]
            return (x * slope.astype(f32)).astype(bf16)

        def third(rows, x):
            acc_ref[rows, :] += dot(x, weights[0])

        staged(spans, first, second, third)
        if n == skip:
            begin(stores[:1])
    finish(loads[3:])

    def first(rows):
        grad = pull_norm(acc_ref[rows, :] * gain_one_ref[...], hat_ref[rows, :], inv_ref[rows, 0:1])
        one_ref[rows, :] = grad
        return grad.astype(bf16)

    def second(rows, grad):
        g_ref[rows, :] = dot(grad, w_out_ref[...], NT).astype(bf16)

    staged(spans, first, second, lambda rows, x: None)
    begin(stores[1:3])

    ones = head_ones()
    sums = {}

    def first(unit):
        g, rows = unit
        cols = parts[g]
        up = g_ref[rows, cols]
        delta = head_sum(up.astype(f32) * att_ref[rows, cols].astype(f32), ones)
        return dot(q_ref[rows, cols], block_diag(pk_ref[:, cols]), NT), dot(up, block_diag(pv_ref[:, cols]), NT), delta

    def second(unit, three):
        g, rows = unit
        cols = parts[g]
        delta_ref[rows, cols] = three[2]
        p = jnp.exp(three[0] - lse_ref[rows, cols])
        ds = (p * (three[1] - three[2])).astype(bf16)
        ds_ref[rows, cols] = ds
        return p.astype(bf16), ds

    def third(unit, pair):
        g, rows = unit
        cols = parts[g]
        dpv, dpk = diag_of(dot(pair[0], g_ref[rows, cols], TN)), diag_of(dot(pair[1], q_ref[rows, cols], TN))
        if rows.start:
            dpv, dpk = sums[g][0] + dpv, sums[g][1] + dpk
        sums[g] = (dpv, dpk)
        if rows.stop == length:
            dpv_ref[:, cols], dpk_ref[:, cols] = dpv, dpk

    staged([(g, rows) for g in range(len(parts)) for rows in spans], first, second, third)
    begin(stores[3:])
    finish(stores)


def middle(low, inv, gain_two, gain_one, pk, pv, total, cot, hat, w_out, q, seen, slopes, early, late):
    length, lanes = low.shape
    slots = pk.shape[0]
    late_units = sum(piece.shape[1] for piece in late)
    flat = [each for pair in seen for each in pair]
    tall = (length, lanes)
    small = jax.ShapeDtypeStruct((slots, lanes), f32)
    holds = [f32, bf16, f32, None, bf16, bf16, f32, bf16, f32, bf16, f32, bf16, bf16]
    return pl.pallas_call(
        functools.partial(middle_kernel, halves=len(seen), early=len(early), late=len(late), groups=len(slopes)),
        out_shape=tuple(jax.ShapeDtypeStruct(tall, t) for t in (bf16, f32, bf16, f32, bf16)) + (small, small),
        in_specs=[vm()] * 6 + [hbm()] * (5 + 2 * len(seen) + len(slopes) + len(early) + len(late)),
        out_specs=(hbm(),) * 5 + (vm(), vm()),
        scratch_shapes=[pltpu.VMEM((lanes, lanes), bf16) if t is None else pltpu.VMEM(tall, t) for t in holds]
        + [
            pltpu.VMEM((length, late_units), bf16),
            pltpu.VMEM((2, 2, HID, lanes), bf16),
            pltpu.VMEM((2, length, HID), bf16),
            pltpu.SemaphoreType.DMA((2, most_of(early + late))),
            pltpu.SemaphoreType.DMA((2,)),
            pltpu.SemaphoreType.DMA((5 + len(flat),)),
            pltpu.SemaphoreType.DMA((5,)),
        ],
        compiler_params=pltpu.CompilerParams(vmem_limit_bytes=VMEM),
        cost_estimate=cost(40 * length * lanes * lanes),
        name="middle",
    )(low, inv, gain_two, gain_one, pk, pv, total, cot, hat, w_out, q, *flat, *slopes, *early, *late)


def project_kernel(*refs, halves):
    grads, weights, one_ref, out_ref = refs[: 3 * halves], refs[3 * halves : 6 * halves], refs[-2], refs[-1]
    total = one_ref[...]
    for grad, weight in zip(grads, weights):
        total = total + dot(grad[...], weight[...], NT)
    out_ref[...] = total


def project_back(grads, weights, grad_one):
    length, lanes = grad_one.shape
    halves = len(grads)
    width = lanes // halves
    flat = [grad for half in grads for grad in half]
    slabs = [pl.BlockSpec((lanes, width), lambda i, n=n: (0, n)) for n in range(halves) for _ in range(3)]
    tall = pl.BlockSpec((WIN, lanes), lambda i: (i, 0))
    return pl.pallas_call(
        functools.partial(project_kernel, halves=halves),
        grid=(length // WIN,),
        out_shape=jax.ShapeDtypeStruct((length, lanes), f32),
        in_specs=[pl.BlockSpec((WIN, width), lambda i: (i, 0)) for _ in flat] + slabs + [tall],
        out_specs=tall,
        compiler_params=pltpu.CompilerParams(vmem_limit_bytes=VMEM),
        cost_estimate=cost(6 * length * lanes * lanes),
        name="project_back",
    )(*flat, *(list(weights) * halves), grad_one)


def swap(x, axis, bit):
    return lax.ppermute(x, axis, [(i, i ^ bit) for i in range(lax.axis_size(axis))])


def swap_two(x, one, two):
    if one[0] == two[0]:
        return swap(x, one[0], one[1] | two[1])
    wide = {"dp": lax.axis_size("mp"), "mp": 1}
    mask = one[1] * wide[one[0]] + two[1] * wide[two[0]]
    count = lax.axis_size("dp") * lax.axis_size("mp")
    return lax.ppermute(x, ("dp", "mp"), [(i, i ^ mask) for i in range(count)])


def gather_plain(w_in, w_back):
    both = jnp.stack([w_in.T, w_back])
    part = both.shape[1] // lax.axis_size("dp")
    mine = lax.dynamic_slice_in_dim(both, lax.axis_index("dp") * part, part, 1)
    return lax.all_gather(mine, ("dp", "mp"), axis=1, tiled=True)


def own_weights(w_in, w_back):
    both = jnp.stack([w_in.T, w_back])
    half = both.shape[1] // 2
    dp = lax.axis_index("dp")
    own = lax.dynamic_slice_in_dim(both, lax.rem(dp, 2) * half, half, 1)
    unit = half // 2
    mine = lax.dynamic_slice_in_dim(own, dp // 2 * unit, unit, 1)
    rest = lax.dynamic_slice_in_dim(own, (1 - dp // 2) * unit, unit, 1)
    return both, own, mine, rest


def with_other(pieces):
    return [each for piece in pieces for each in (piece, swap(piece, "dp", 1))]


def sum_everywhere(x):
    core = lax.rem(lax.axis_index("dp"), 2)
    half = x.shape[0] // 2
    keep = lax.dynamic_slice_in_dim(x, core * half, half, 0)
    give = lax.dynamic_slice_in_dim(x, (1 - core) * half, half, 0)
    part = keep + swap(give, "dp", 1)
    bits = [(axis, 1 << n) for axis in ("dp", "mp") for n in range(lax.axis_size(axis).bit_length() - 1)][1:]
    bits = sorted(bits, key=lambda pair: pair[1] if pair[0] == "mp" else 1)
    for n in range(0, len(bits), 2):
        low = part.astype(bf16)
        pairs = bits[n : n + 2]
        near = swap(low, *pairs[0]).astype(f32) + low.astype(f32)
        if len(pairs) == 2:
            far = swap(low, *pairs[1])
            both = swap_two(low, pairs[0], pairs[1])
            near = near + (far.astype(f32) + both.astype(f32))
        part = near
    other = swap(part, "dp", 1)
    return jnp.where(core == 0, jnp.concatenate([part, other]), jnp.concatenate([other, part]))


def on_device(
    tokens, segment_ids, w_query, w_key, w_value, w_out, gain_one, gain_two, w_in, w_back,
    prefix_master, moment_one, moment_two, cotangent,
):
    stepwise = lax.axis_size("dp") == 4 and lax.axis_size("mp") == 8
    prefix_low = prefix_master.astype(bf16)
    prefix_keys, prefix_vals = prefix_low[0], prefix_low[1]
    first_gain, second_gain = gain_one[None, :], gain_two[None, :]
    lo, nw, segc, segk = windows(segment_ids[0])
    halves = 2
    width = tokens.shape[1] // halves
    if stepwise:
        both, own, mine, rest = own_weights(w_in, w_back)
        z_two, z_three = swap(mine, "mp", 4), swap(mine, "mp", 6)
        z_one, z_last, x_own = swap(mine, "mp", 2), swap(rest, "mp", 2), swap(own, "mp", 1)
    queries, keys_own, values_own, *first = attend_first(
        lo, nw, tokens, w_query, w_key, w_value, prefix_keys, prefix_vals, segc, segk, width
    )
    if stepwise:
        z_one, z_two, queries, keys_own, values_own = lax.optimization_barrier(
            (z_one, z_two, queries, keys_own, values_own)
        )
        x_two, y_two, x_one = swap(z_two, "mp", 1), swap(z_two, "dp", 2), swap(z_one, "mp", 1)
    seen = [first] + [
        attend_rest(lo, nw, queries, keys_own, values_own, prefix_keys, prefix_vals, segc, segk, width, part)
        for part in range(1, halves)
    ]
    attended = [pair[0] for pair in seen]
    if stepwise:
        x_two, y_two, z_three, z_last, x_own, z_one, *attended = lax.optimization_barrier(
            (x_two, y_two, z_three, z_last, x_own, z_one, *attended)
        )
        x_three, y_three, yx_two = swap(z_three, "mp", 1), swap(z_three, "dp", 2), swap(x_two, "dp", 2)
        more = with_other([x_own, z_one, z_last])
        hat, inv, normed_low, total, slope = ffn_forward(attended, tokens, w_out, first_gain, [both])
        x_three, y_three, x_one, z_last, yx_two, *rows = lax.optimization_barrier(
            (x_three, y_three, x_one, z_last, yx_two, normed_low, total, *more)
        )
        yx_three, x_last = swap(x_three, "dp", 2), swap(z_last, "mp", 1)
        normed_low, total, *more = rows
        late = with_other([z_two, x_two, y_two, x_one, z_three, x_three, y_three, yx_two])
        total, slope_more = ffn_more(normed_low, total, more)
        late, total, yx_three, x_last = lax.optimization_barrier((late, total, yx_three, x_last))
        early, slopes = [both] + more, [slope, slope_more]
        late = late + with_other([x_last, yx_three])
    else:
        every = gather_plain(w_in, w_back)
        cut = every.shape[1] * 3 // 8
        early, late = [every[:, :cut]], [every[:, cut:]]
        hat, inv, normed_low, total, slope = ffn_forward(attended, tokens, w_out, first_gain, early)
        slopes = [slope]
    layer_output, grad_one, grad_att, delta, ds_prefix, dpk, dpv = middle(
        normed_low, inv, second_gain, first_gain, prefix_keys, prefix_vals,
        total, cotangent, hat, w_out, queries, seen, slopes, early, late,
    )
    prefix_grad = sum_everywhere(jnp.stack([dpk, dpv]))
    grads = [
        attend_back(
            lo, nw, queries, keys_own, values_own, grad_att, lse, delta, ds_prefix, prefix_keys, segc, segk, width, part
        )
        for part, (_, lse) in enumerate(seen)
    ]
    input_grad = project_back(grads, (w_query, w_key, w_value), grad_one)
    new_first = beta_one * moment_one + (1.0 - beta_one) * prefix_grad
    new_second = beta_two * moment_two + (1.0 - beta_two) * prefix_grad * prefix_grad
    first_hat = new_first / (1.0 - beta_one**STEP)
    second_hat = new_second / (1.0 - beta_two**STEP)
    new_master = prefix_master * (1.0 - learn_rate * weight_decay) - learn_rate * first_hat / (
        jnp.sqrt(second_hat) + epsilon_adam
    )
    return (layer_output, input_grad, new_master, new_first, new_second, new_master.astype(bf16))


def solution(mesh):
    rows = P(("dp", "mp"), None)
    return jax.shard_map(
        on_device,
        mesh=mesh,
        in_specs=(rows, rows, P(), P(), P(), P(), P(), P(), P(None, "mp"), P("mp", None), P(), P(), P(), rows),
        out_specs=(rows, rows, P(), P(), P(), P()),
        check_vma=False,
    )
```

```python
import functools

import jax
import jax.numpy as jnp
from jax import lax
from jax.experimental import pallas as pl
from jax.experimental.pallas import tpu as pltpu
from jax.sharding import PartitionSpec as P

f32, bf16 = jnp.float32, jnp.bfloat16
STEP = 5
epsilon_norm = 1e-05
learn_rate = 1.0
weight_decay = 0.01
beta_one = 0.9
beta_two = 0.999
epsilon_adam = 1e-08
HEAD_SCALE = 0.125
NEG = -1e30
WIN = 256
KC = 64
QUAD = 256
LEAST, MOST = 1e-25, 1e30
ITEMS = 64
VMEM = 60 << 20
NN = (((1,), (0,)), ((), ()))
NT = (((1,), (1,)), ((), ()))
TN = (((0,), (0,)), ((), ()))


def dot(a, b, d=NN):
    return lax.dot_general(a, b, d, preferred_element_type=f32)


def vm():
    return pl.BlockSpec(memory_space=pltpu.VMEM)


def sm():
    return pl.BlockSpec(memory_space=pltpu.SMEM)


def hbm():
    return pl.BlockSpec(memory_space=pl.ANY)


def cost(flops, moved=8 << 20):
    return pl.CostEstimate(flops=4 * flops, bytes_accessed=moved, transcendentals=0)


def part_of(array, width, part):
    return pl.BlockSpec((array.shape[0], width), lambda i: (0, part))


def whole_of(array):
    return pl.BlockSpec(array.shape, lambda i: (0, 0))


def block_diag(piece):
    lane = lax.broadcasted_iota(jnp.int32, piece.shape, 1) // 64
    zero = jnp.zeros_like(piece)
    return jnp.concatenate([jnp.where(lane == h, piece, zero) for h in range(4)], axis=0)


def diag_of(full):
    lane = lax.broadcasted_iota(jnp.int32, (KC, 128), 1) < 64
    left = jnp.where(lane, full[0:64, 0:128], full[64:128, 0:128])
    right = jnp.where(lane, full[128:192, 128:256], full[192:256, 128:256])
    return jnp.concatenate([left, right], axis=1)


def head_ones():
    row = lax.broadcasted_iota(jnp.int32, (QUAD, QUAD), 0) // 64
    lane = lax.broadcasted_iota(jnp.int32, (QUAD, QUAD), 1) // 64
    return jnp.where(row == lane, 1.0, 0.0).astype(bf16)


def head_sum(x, ones):
    high = x.astype(bf16)
    return dot(high, ones) + dot((x - high.astype(f32)).astype(bf16), ones)


def head_max(x):
    lane = lax.broadcasted_iota(jnp.int32, x.shape, 1) < 64
    a = jnp.max(jnp.where(lane, x, NEG), axis=1, keepdims=True)
    b = jnp.max(jnp.where(lane, NEG, x), axis=1, keepdims=True)
    return jnp.where(lane, a, b)


def windows(seg):
    length = seg.shape[0]
    by = seg.reshape(length // KC, KC)
    first, last = by[:, 0], by[:, -1]
    lo = jnp.sum((seg[None, :] < first[:, None]).astype(jnp.int32), axis=1)
    hi = jnp.sum((seg[None, :] <= last[:, None]).astype(jnp.int32), axis=1)
    lo = lo // 16 * 16
    nw = (hi - lo + WIN - 1) // WIN
    segc = jnp.broadcast_to(seg[:, None], (length, 128))
    segk = jnp.concatenate([by, by], axis=1)
    return lo, nw, segc, segk


def list_items(lo_ref, nw_ref, chunk_ref, row_ref, length):
    def chunk(c, count):
        def one(w, count):
            chunk_ref[count] = c
            row_ref[count] = lo_ref[c] + w * WIN
            return count + 1

        return lax.fori_loop(0, nw_ref[c], one, count)

    count = lax.fori_loop(0, length // KC, chunk, 0)
    for n in range(2):
        chunk_ref[count + n] = 0
        row_ref[count + n] = length
    return count


def item_at(n, chunk_ref, row_ref, segc_ref, segk_ref, length):
    c, nominal = chunk_ref[n], row_ref[n]
    start = pl.multiple_of(jnp.minimum(nominal, length - WIN), 16)
    rows = pl.ds(start, WIN)
    keys = pl.ds(pl.multiple_of(c * KC, KC), KC)
    row_id = lax.broadcasted_iota(jnp.int32, (WIN, 128), 0) + start
    keep = jnp.logical_and(segc_ref[rows, :] == segk_ref[pl.ds(c, 1), :], row_id >= nominal)
    bias = jnp.where(keep, 0.0, NEG)
    return rows, keys, jnp.concatenate([bias, bias], axis=1)


def staged(units, first, second, third):
    raw, done = first(units[0]), None
    for n in range(len(units) + 1):
        upcoming = first(units[n + 1]) if n + 1 < len(units) else None
        fresh = second(units[n], raw) if n < len(units) else None
        if done is not None:
            third(units[n - 1], done)
        raw, done = upcoming, fresh


def attend_columns(count, q_ref, k_ref, v_ref, pk_ref, pv_ref, att_ref, lse_ref, l_ref, acc_ref, item, ones):
    length, width = att_ref.shape
    parts = [slice(c, c + QUAD) for c in range(0, width, QUAD)]
    spans = [slice(r, r + WIN) for r in range(0, length, WIN)]
    ids = range(len(parts))

    def sweep(shift):
        bdk = [block_diag(pk_ref[:, cols]) for cols in parts]
        bdv = [block_diag(pv_ref[:, cols]) for cols in parts]

        def moved(s, rows, cols):
            return s if shift is None else s - shift[rows, cols]

        def start_third(unit, p):
            rows, g = unit
            l_ref[rows, parts[g]] = p
            acc_ref[rows, parts[g]] = dot(p.astype(bf16), bdv[g])

        staged(
            [(rows, g) for g in ids for rows in spans],
            lambda u: dot(q_ref[u[0], parts[u[1]]], bdk[u[1]], NT),
            lambda u, s: jnp.exp(moved(s, u[0], parts[u[1]])),
            start_third,
        )

        @pl.loop(0, (count + 1) // 2)
        def _(n):
            def third(unit, p):
                (rows, keys, _), g = unit
                l_ref[rows, parts[g]] += p
                acc_ref[rows, parts[g]] += dot(p.astype(bf16), block_diag(v_ref[keys, parts[g]]))

            staged(
                [(one, g) for one in (item(2 * n), item(2 * n + 1)) for g in ids],
                lambda u: dot(q_ref[u[0][0], parts[u[1]]], block_diag(k_ref[u[0][1], parts[u[1]]]), NT),
                lambda u, s: jnp.exp(moved(s, u[0][0], parts[u[1]]) + u[0][2]),
                third,
            )

        least, most = [], []
        for rows in spans:
            for cols in parts:
                total = head_sum(l_ref[rows, cols], ones)
                att_ref[rows, cols] = (acc_ref[rows, cols] / total).astype(bf16)
                low = jnp.log(total)
                lse_ref[rows, cols] = low if shift is None else low + shift[rows, cols]
                least.append(jnp.min(total, axis=0, keepdims=True))
                most.append(jnp.max(total, axis=0, keepdims=True))
        return jnp.min(functools.reduce(jnp.minimum, least)), jnp.max(functools.reduce(jnp.maximum, most))

    least, most = sweep(None)

    @pl.when(jnp.logical_not(jnp.logical_and(least > LEAST, most < MOST)))
    def _():
        for cols in parts:
            bdk = block_diag(pk_ref[:, cols])
            for rows in spans:
                lse_ref[rows, cols] = dot(q_ref[rows, cols], bdk, NT)

        @pl.loop(0, count)
        def _(n):
            rows, keys, bias = item(n)
            for cols in parts:
                s = dot(q_ref[rows, cols], block_diag(k_ref[keys, cols]), NT) + bias
                lse_ref[rows, cols] = jnp.maximum(lse_ref[rows, cols], s)

        @pl.loop(0, length // WIN)
        def _(r):
            rows = pl.ds(pl.multiple_of(r * WIN, WIN), WIN)
            for c in range(0, width, 128):
                cols = slice(c, c + 128)
                lse_ref[rows, cols] = head_max(lse_ref[rows, cols])

        sweep(lse_ref)


def attend_first_kernel(
    lo_ref, nw_ref, x_ref, wq_hbm, wk_hbm, wv_hbm, pk_ref, pv_ref, segc_ref, segk_ref,
    q_hbm, k_hbm, v_hbm, att_ref, lse_ref,
    w_ref, q_ref, k_ref, v_ref, l_ref, acc_ref, chunk_ref, row_ref, in_sems, out_sems,
):
    length, lanes = x_ref.shape
    loads = [pltpu.make_async_copy(w, w_ref.at[n], in_sems.at[n]) for n, w in enumerate((wq_hbm, wk_hbm, wv_hbm))]
    stores = [
        pltpu.make_async_copy(a, b, out_sems.at[n])
        for n, (a, b) in enumerate(((q_ref, q_hbm), (k_ref, k_hbm), (v_ref, v_hbm)))
    ]
    for load in loads:
        load.start()
    count = list_items(lo_ref, nw_ref, chunk_ref, row_ref, length)
    for n, out_ref in enumerate((q_ref, k_ref, v_ref)):
        loads[n].wait()
        for c in range(0, lanes, QUAD):
            value = dot(x_ref[...], w_ref[n, :, c : c + QUAD])
            out_ref[:, c : c + QUAD] = (value * HEAD_SCALE if n == 0 else value).astype(bf16)
        stores[n].start()

    def item(n):
        return item_at(n, chunk_ref, row_ref, segc_ref, segk_ref, length)

    attend_columns(
        count, q_ref, k_ref, v_ref, pk_ref, pv_ref, att_ref, lse_ref, l_ref, acc_ref, item, head_ones()
    )
    for store in stores:
        store.wait()


def attend_rest_kernel(
    lo_ref, nw_ref, q_ref, k_ref, v_ref, pk_ref, pv_ref, segc_ref, segk_ref,
    att_ref, lse_ref, l_ref, acc_ref, chunk_ref, row_ref,
):
    length = q_ref.shape[0]
    count = list_items(lo_ref, nw_ref, chunk_ref, row_ref, length)

    def item(n):
        return item_at(n, chunk_ref, row_ref, segc_ref, segk_ref, length)

    attend_columns(
        count, q_ref, k_ref, v_ref, pk_ref, pv_ref, att_ref, lse_ref, l_ref, acc_ref, item, head_ones()
    )


def attend_first(lo, nw, x, wq, wk, wv, pk, pv, segc, segk, width):
    length, lanes = x.shape
    low = jax.ShapeDtypeStruct((length, lanes), bf16)
    return pl.pallas_call(
        attend_first_kernel,
        out_shape=(low, low, low, jax.ShapeDtypeStruct((length, width), bf16), jax.ShapeDtypeStruct((length, width), f32)),
        in_specs=[sm(), sm(), vm(), hbm(), hbm(), hbm(), vm(), vm(), vm(), vm()],
        out_specs=(hbm(), hbm(), hbm(), vm(), vm()),
        scratch_shapes=[pltpu.VMEM((3, lanes, lanes), bf16)]
        + [pltpu.VMEM((length, lanes), bf16)] * 3
        + [pltpu.VMEM((length, width), f32)] * 2
        + [pltpu.SMEM((ITEMS,), jnp.int32)] * 2
        + [pltpu.SemaphoreType.DMA((3,))] * 2,
        compiler_params=pltpu.CompilerParams(vmem_limit_bytes=VMEM),
        cost_estimate=cost(16 * length * lanes * lanes),
        name="attend_first",
    )(lo, nw, x, wq, wk, wv, pk, pv, segc, segk)


def attend_rest(lo, nw, q, k, v, pk, pv, segc, segk, width, part):
    length = q.shape[0]
    return pl.pallas_call(
        attend_rest_kernel,
        grid=(1,),
        out_shape=(jax.ShapeDtypeStruct((length, width), bf16), jax.ShapeDtypeStruct((length, width), f32)),
        in_specs=[sm(), sm()] + [part_of(a, width, part) for a in (q, k, v, pk, pv)] + [whole_of(segc), whole_of(segk)],
        out_specs=(pl.BlockSpec((length, width), lambda i: (0, 0)),) * 2,
        scratch_shapes=[pltpu.VMEM((length, width), f32)] * 2 + [pltpu.SMEM((ITEMS,), jnp.int32)] * 2,
        compiler_params=pltpu.CompilerParams(vmem_limit_bytes=VMEM),
        cost_estimate=cost(16000 * length * width),
        name="attend_rest",
    )(lo, nw, q, k, v, pk, pv, segc, segk)


def attend_back_kernel(*refs, halves):
    lo_ref, nw_ref, pk_ref, segc_ref, segk_ref = refs[:5]
    sources, refs = refs[5 : 11 + halves], refs[11 + halves :]
    (
        dq_hbm, dk_hbm, dv_hbm,
        q_ref, k_ref, v_ref, g_ref, delta_ref, ds_ref, lse_ref,
        dq_acc, dk_acc, dv_acc, dq_ref, dk_ref, dv_ref, chunk_ref, row_ref, in_sems, out_sems,
    ) = refs
    length, lanes = q_ref.shape
    parts = [slice(g * QUAD, (g + 1) * QUAD) for g in range(lanes // QUAD)]
    spans = [slice(r * WIN, (r + 1) * WIN) for r in range(length // WIN)]
    places = [ds_ref, q_ref, k_ref, v_ref, g_ref, delta_ref]
    for n in range(halves):
        places.append(lse_ref.at[:, n * (lanes // halves) : (n + 1) * (lanes // halves)])
    loads = [pltpu.make_async_copy(a, b, in_sems.at[n]) for n, (a, b) in enumerate(zip(sources, places))]
    for load in loads:
        load.start()
    count = list_items(lo_ref, nw_ref, chunk_ref, row_ref, length)
    dk_acc[...] = jnp.zeros_like(dk_acc)
    dv_acc[...] = jnp.zeros_like(dv_acc)
    loads[0].wait()
    for cols in parts:
        bdk = block_diag(pk_ref[:, cols])
        for rows in spans:
            dq_acc[rows, cols] = dot(ds_ref[rows, cols], bdk)
    for load in loads[1:]:
        load.wait()
    ids = range(len(parts))

    @pl.loop(0, (count + 1) // 2)
    def _(n):
        def first(unit):
            (rows, keys, _), g = unit
            cols = parts[g]
            s = dot(q_ref[rows, cols], block_diag(k_ref[keys, cols]), NT)
            return s, dot(g_ref[rows, cols], block_diag(v_ref[keys, cols]), NT)

        def second(unit, pair):
            (rows, _, bias), g = unit
            cols = parts[g]
            p = jnp.exp(pair[0] + bias - lse_ref[rows, cols])
            return p.astype(bf16), (p * (pair[1] - delta_ref[rows, cols])).astype(bf16)

        def third(unit, pair):
            (rows, keys, _), g = unit
            cols = parts[g]
            dv_acc[keys, cols] += diag_of(dot(pair[0], g_ref[rows, cols], TN))
            dk_acc[keys, cols] += diag_of(dot(pair[1], q_ref[rows, cols], TN))
            dq_acc[rows, cols] += dot(pair[1], block_diag(k_ref[keys, cols]))

        items = [item_at(2 * n + i, chunk_ref, row_ref, segc_ref, segk_ref, length) for i in range(2)]
        staged([(one, g) for one in items for g in ids], first, second, third)

    stores = []
    ends = ((dq_acc, dq_ref, dq_hbm, HEAD_SCALE), (dk_acc, dk_ref, dk_hbm, 1.0), (dv_acc, dv_ref, dv_hbm, 1.0))
    for n, (acc, low, target, scale) in enumerate(ends):
        low[...] = (acc[...] * scale).astype(bf16)
        stores.append(pltpu.make_async_copy(low, target, out_sems.at[n]))
        stores[n].start()
    for store in stores:
        store.wait()


def attend_back(lo, nw, q, k, v, g, lse, delta, ds, pk, segc, segk):
    length, lanes = q.shape
    tall = (length, lanes)
    return pl.pallas_call(
        functools.partial(attend_back_kernel, halves=len(lse)),
        out_shape=(jax.ShapeDtypeStruct(tall, bf16),) * 3,
        in_specs=[sm(), sm(), vm(), vm(), vm()] + [hbm()] * (6 + len(lse)),
        out_specs=(hbm(),) * 3,
        scratch_shapes=[pltpu.VMEM(tall, t) for t in (bf16, bf16, bf16, bf16, f32, bf16, f32)]
        + [pltpu.VMEM(tall, f32)] * 3
        + [pltpu.VMEM(tall, bf16)] * 3
        + [pltpu.SMEM((ITEMS,), jnp.int32)] * 2
        + [pltpu.SemaphoreType.DMA((6 + len(lse),)), pltpu.SemaphoreType.DMA((3,))],
        compiler_params=pltpu.CompilerParams(vmem_limit_bytes=VMEM),
        cost_estimate=cost(length * lanes * 30000),
        name="attend_back",
    )(lo, nw, pk, segc, segk, ds, q, k, v, g, delta, *lse)


HID = 512


def mean_of(x):
    return jnp.mean(x, axis=-1, keepdims=True)


def centre(x):
    centred = x - mean_of(x)
    inv = lax.rsqrt(mean_of(centred * centred) + epsilon_norm)
    return centred * inv, inv


def pull_norm(pull, hat, inv):
    return inv * (pull - mean_of(pull) - hat * mean_of(pull * hat))


def gelu_pair(x):
    phi = 0.5 + 0.5 * lax.erf(x * 0.7071067811865476)
    bell = 0.3989422804014327 * jnp.exp(-0.5 * (x * x))
    return x * phi, phi + x * bell


def blocks_of(pieces):
    blocks, block, room = [], [], HID
    for piece in pieces:
        row = 0
        while row < piece.shape[1]:
            rows = min(room, piece.shape[1] - row)
            block.append((piece, row, rows))
            row, room = row + rows, room - rows
            if room == 0:
                blocks.append(block)
                block, room = [], HID
    return blocks


def most_of(pieces):
    return max(len(block) for block in blocks_of(pieces))


def block_copies(block, buffer, sems, slot):
    copies, place = [], 0
    for n, (piece, row, rows) in enumerate(block):
        source = piece.at[:, row : row + rows]
        copies.append(pltpu.make_async_copy(source, buffer.at[slot, :, place : place + rows], sems.at[slot, n]))
        place += rows
    return copies


def begin(copies):
    for copy in copies:
        copy.start()


def finish(copies):
    for copy in copies:
        copy.wait()


def forward_block(low_ref, weights, sum_ref, slope_ref, cols):
    def second(rows, x):
        act, slope = gelu_pair(x)
        slope_ref[rows, cols] = slope.astype(bf16)
        return act.astype(bf16)

    def third(rows, act):
        sum_ref[rows, :] += dot(act, weights[1])

    spans = [slice(r, r + WIN) for r in range(0, low_ref.shape[0], WIN)]
    staged(spans, lambda rows: dot(low_ref[rows, :], weights[0], NT), second, third)


def ffn_kernel(*refs, halves, count):
    atts, (tok_ref, w_out_ref, gain_ref), refs = refs[:halves], refs[halves : halves + 3], refs[halves + 3 :]
    blocks = blocks_of(refs[:count])
    hat_ref, inv_ref, low_ref, sum_ref, slope_ref, buffer, sems = refs[count:]
    width = atts[0].shape[1]
    copies = [block_copies(block, buffer, sems, b % 2) for b, block in enumerate(blocks)]
    begin(copies[0])

    def second(rows, x):
        hat, inv = centre(tok_ref[rows, :].astype(f32) + x)
        hat_ref[rows, :] = hat
        inv_ref[rows, :] = jnp.broadcast_to(inv, (WIN, 128))
        normed = gain_ref[...] * hat
        sum_ref[rows, :] = normed
        low_ref[rows, :] = normed.astype(bf16)

    def first(rows):
        return sum(dot(att_ref[rows, :], w_out_ref[n * width : (n + 1) * width, :]) for n, att_ref in enumerate(atts))

    spans = [slice(r, r + WIN) for r in range(0, tok_ref.shape[0], WIN)]
    staged(spans, first, second, lambda rows, x: None)
    for b in range(len(blocks)):
        if b + 1 < len(blocks):
            begin(copies[b + 1])
        finish(copies[b])
        forward_block(low_ref, buffer.at[b % 2], sum_ref, slope_ref, slice(b * HID, (b + 1) * HID))


def ffn_forward(att, tokens, w_out, gain, pieces):
    length, lanes = tokens.shape
    hidden = sum(piece.shape[1] for piece in pieces)
    wide = jax.ShapeDtypeStruct((length, lanes), f32)
    return pl.pallas_call(
        functools.partial(ffn_kernel, halves=len(att), count=len(pieces)),
        out_shape=(
            wide,
            jax.ShapeDtypeStruct((length, 128), f32),
            jax.ShapeDtypeStruct((length, lanes), bf16),
            wide,
            jax.ShapeDtypeStruct((length, hidden), bf16),
        ),
        in_specs=[vm()] * (len(att) + 3) + [hbm()] * len(pieces),
        out_specs=(vm(),) * 5,
        scratch_shapes=[pltpu.VMEM((2, 2, HID, lanes), bf16), pltpu.SemaphoreType.DMA((2, most_of(pieces)))],
        compiler_params=pltpu.CompilerParams(vmem_limit_bytes=VMEM),
        cost_estimate=cost(4 * length * lanes * (hidden + lanes)),
        name="ffn_forward",
    )(*att, tokens, w_out, gain, *pieces)


def more_kernel(low_ref, start_ref, *refs, count):
    blocks = blocks_of(refs[:count])
    sum_ref, slope_ref, buffer, sems = refs[count:]
    copies = [block_copies(block, buffer, sems, b % 2) for b, block in enumerate(blocks)]
    begin(copies[0])
    sum_ref[...] = start_ref[...]
    for b in range(len(blocks)):
        if b + 1 < len(blocks):
            begin(copies[b + 1])
        finish(copies[b])
        forward_block(low_ref, buffer.at[b % 2], sum_ref, slope_ref, slice(b * HID, (b + 1) * HID))


def ffn_more(low, start, pieces):
    length, lanes = low.shape
    hidden = sum(piece.shape[1] for piece in pieces)
    return pl.pallas_call(
        functools.partial(more_kernel, count=len(pieces)),
        out_shape=(jax.ShapeDtypeStruct((length, lanes), f32), jax.ShapeDtypeStruct((length, hidden), bf16)),
        in_specs=[vm()] * 2 + [hbm()] * len(pieces),
        out_specs=(vm(),) * 2,
        scratch_shapes=[pltpu.VMEM((2, 2, HID, lanes), bf16), pltpu.SemaphoreType.DMA((2, most_of(pieces)))],
        compiler_params=pltpu.CompilerParams(vmem_limit_bytes=VMEM),
        cost_estimate=cost(4 * length * lanes * hidden),
        name="ffn_more",
    )(low, start, *pieces)


def middle_kernel(*refs, halves, early, late, groups):
    low_ref, inv_ref, gain_two_ref, gain_one_ref, pk_ref, pv_ref = refs[:6]
    sum_hbm, cot_hbm, hat_hbm, w_out_hbm, q_hbm = refs[6:11]
    seen, refs = refs[11 : 11 + 2 * halves], refs[11 + 2 * halves :]
    slopes, pieces, refs = refs[:groups], refs[groups : groups + early + late], refs[groups + early + late :]
    (layer_hbm, one_hbm, g_hbm, delta_hbm, ds_hbm, dpk_ref, dpv_ref) = refs[:7]
    (
        acc_ref, cot_ref, hat_ref, w_out_ref, q_ref, att_ref, lse_ref, layer_ref, one_ref, g_ref, delta_ref, ds_ref,
        grad_ref, late_ref, buffer, sbuf, sems, ssems, in_sems, out_sems,
    ) = refs[7:]
    length, lanes = low_ref.shape
    spans = [slice(r, r + WIN) for r in range(0, length, WIN)]
    parts = [slice(c, c + QUAD) for c in range(0, lanes, QUAD)]
    first_blocks, last_blocks = blocks_of(pieces[:early]), blocks_of(pieces[early:])
    order = last_blocks + first_blocks + last_blocks
    copies = [block_copies(block, buffer, sems, n % 2) for n, block in enumerate(order)]
    skip = len(last_blocks)
    slabs = [slope.at[:, c : c + HID] for slope in slopes for c in range(0, slope.shape[1], HID)]
    for n, source in enumerate(slabs, skip):
        copies[n].append(pltpu.make_async_copy(source, sbuf.at[n % 2], ssems.at[n % 2]))
    sources = (sum_hbm, cot_hbm, hat_hbm, w_out_hbm, q_hbm, *seen)
    places = [acc_ref, cot_ref, hat_ref, w_out_ref, q_ref]
    for n in range(halves):
        cols = slice(n * (lanes // halves), (n + 1) * (lanes // halves))
        places += [att_ref.at[:, cols], lse_ref.at[:, cols]]
    loads = [pltpu.make_async_copy(a, b, in_sems.at[n]) for n, (a, b) in enumerate(zip(sources, places))]
    results = (layer_ref, one_ref, g_ref, delta_ref, ds_ref)
    targets = (layer_hbm, one_hbm, g_hbm, delta_hbm, ds_hbm)
    stores = [pltpu.make_async_copy(a, b, out_sems.at[n]) for n, (a, b) in enumerate(zip(results, targets))]
    begin(copies[0])
    begin(loads[:1])

    def enter(n):
        if n + 1 < len(order):
            begin(copies[n + 1])
        if n == 0:
            finish(loads[:1])
            begin(loads[1:])
        finish(copies[n])
        return buffer.at[n % 2]

    for n in range(skip):
        forward_block(low_ref, enter(n), acc_ref, late_ref, slice(n * HID, (n + 1) * HID))

    finish(loads[1:3])
    for n in range(skip, len(order)):
        weights = enter(n)
        past = n - skip - len(first_blocks)

        def first(rows):
            if n == skip:
                hat, inv = centre(acc_ref[rows, :])
                layer_ref[rows, :] = (gain_two_ref[...] * hat).astype(bf16)
                grad = pull_norm(cot_ref[rows, :].astype(f32) * gain_two_ref[...], hat, inv)
                acc_ref[rows, :] = grad
                grad_ref[rows, :] = grad.astype(bf16)
            return dot(grad_ref[rows, :], weights[1], NT)

        def second(rows, x):
            slope = sbuf[n % 2, rows, :] if past < 0 else late_ref[rows, past * HID : (past + 1) * HID]
            return (x * slope.astype(f32)).astype(bf16)

        def third(rows, x):
            acc_ref[rows, :] += dot(x, weights[0])

        staged(spans, first, second, third)
        if n == skip:
            begin(stores[:1])
    finish(loads[3:])

    def first(rows):
        grad = pull_norm(acc_ref[rows, :] * gain_one_ref[...], hat_ref[rows, :], inv_ref[rows, 0:1])
        one_ref[rows, :] = grad
        return grad.astype(bf16)

    def second(rows, grad):
        g_ref[rows, :] = dot(grad, w_out_ref[...], NT).astype(bf16)

    staged(spans, first, second, lambda rows, x: None)
    begin(stores[1:3])

    ones = head_ones()
    sums = {}

    def first(unit):
        g, rows = unit
        cols = parts[g]
        up = g_ref[rows, cols]
        delta = head_sum(up.astype(f32) * att_ref[rows, cols].astype(f32), ones)
        return dot(q_ref[rows, cols], block_diag(pk_ref[:, cols]), NT), dot(up, block_diag(pv_ref[:, cols]), NT), delta

    def second(unit, three):
        g, rows = unit
        cols = parts[g]
        delta_ref[rows, cols] = three[2]
        p = jnp.exp(three[0] - lse_ref[rows, cols])
        ds = (p * (three[1] - three[2])).astype(bf16)
        ds_ref[rows, cols] = ds
        return p.astype(bf16), ds

    def third(unit, pair):
        g, rows = unit
        cols = parts[g]
        dpv, dpk = diag_of(dot(pair[0], g_ref[rows, cols], TN)), diag_of(dot(pair[1], q_ref[rows, cols], TN))
        if rows.start:
            dpv, dpk = sums[g][0] + dpv, sums[g][1] + dpk
        sums[g] = (dpv, dpk)
        if rows.stop == length:
            dpv_ref[:, cols], dpk_ref[:, cols] = dpv, dpk

    staged([(g, rows) for g in range(len(parts)) for rows in spans], first, second, third)
    begin(stores[3:])
    finish(stores)


def middle(low, inv, gain_two, gain_one, pk, pv, total, cot, hat, w_out, q, seen, slopes, early, late):
    length, lanes = low.shape
    slots = pk.shape[0]
    late_units = sum(piece.shape[1] for piece in late)
    flat = [each for pair in seen for each in pair]
    tall = (length, lanes)
    small = jax.ShapeDtypeStruct((slots, lanes), f32)
    holds = [f32, bf16, f32, None, bf16, bf16, f32, bf16, f32, bf16, f32, bf16, bf16]
    return pl.pallas_call(
        functools.partial(middle_kernel, halves=len(seen), early=len(early), late=len(late), groups=len(slopes)),
        out_shape=tuple(jax.ShapeDtypeStruct(tall, t) for t in (bf16, f32, bf16, f32, bf16)) + (small, small),
        in_specs=[vm()] * 6 + [hbm()] * (5 + 2 * len(seen) + len(slopes) + len(early) + len(late)),
        out_specs=(hbm(),) * 5 + (vm(), vm()),
        scratch_shapes=[pltpu.VMEM((lanes, lanes), bf16) if t is None else pltpu.VMEM(tall, t) for t in holds]
        + [
            pltpu.VMEM((length, late_units), bf16),
            pltpu.VMEM((2, 2, HID, lanes), bf16),
            pltpu.VMEM((2, length, HID), bf16),
            pltpu.SemaphoreType.DMA((2, most_of(early + late))),
            pltpu.SemaphoreType.DMA((2,)),
            pltpu.SemaphoreType.DMA((5 + len(flat),)),
            pltpu.SemaphoreType.DMA((5,)),
        ],
        compiler_params=pltpu.CompilerParams(vmem_limit_bytes=VMEM),
        cost_estimate=cost(40 * length * lanes * lanes),
        name="middle",
    )(low, inv, gain_two, gain_one, pk, pv, total, cot, hat, w_out, q, *flat, *slopes, *early, *late)


def project_kernel(dq_hbm, dk_hbm, dv_hbm, wq_hbm, wk_hbm, wv_hbm, one_hbm, out_hbm, grads, weights, out_ref, *sems):
    length, lanes = out_ref.shape
    spans = [slice(r, r + WIN) for r in range(0, length, WIN)]
    grad_sems, weight_sems, one_sem, out_sems = sems
    loads = []
    for n, (grad, weight) in enumerate(((dq_hbm, wq_hbm), (dk_hbm, wk_hbm), (dv_hbm, wv_hbm))):
        loads.append(
            (
                pltpu.make_async_copy(grad, grads.at[n], grad_sems.at[n]),
                pltpu.make_async_copy(weight, weights.at[n], weight_sems.at[n]),
            )
        )
        begin(loads[n])
        if n == 0:
            one = pltpu.make_async_copy(one_hbm, out_ref, one_sem.at[0])
            one.start()
    stores = [
        pltpu.make_async_copy(out_ref.at[rows, :], out_hbm.at[rows, :], out_sems.at[r]) for r, rows in enumerate(spans)
    ]
    finish(loads[0])
    first = [dot(grads[0, rows, :], weights[0], NT) for rows in spans[:1]]
    one.wait()
    out_ref[spans[0], :] += first[0]
    for rows in spans[1:]:
        out_ref[rows, :] += dot(grads[0, rows, :], weights[0], NT)
    finish(loads[1])
    finish(loads[2])
    for r, rows in enumerate(spans):
        more = dot(grads[1, rows, :], weights[1], NT) + dot(grads[2, rows, :], weights[2], NT)
        out_ref[rows, :] += more
        stores[r].start()
    finish(stores)


def project_back(grads, weights, grad_one):
    length, lanes = grad_one.shape
    return pl.pallas_call(
        project_kernel,
        out_shape=jax.ShapeDtypeStruct((length, lanes), f32),
        in_specs=[hbm()] * 7,
        out_specs=hbm(),
        scratch_shapes=[
            pltpu.VMEM((3, length, lanes), bf16),
            pltpu.VMEM((3, lanes, lanes), bf16),
            pltpu.VMEM((length, lanes), f32),
            pltpu.SemaphoreType.DMA((3,)),
            pltpu.SemaphoreType.DMA((3,)),
            pltpu.SemaphoreType.DMA((1,)),
            pltpu.SemaphoreType.DMA((length // WIN,)),
        ],
        compiler_params=pltpu.CompilerParams(vmem_limit_bytes=VMEM),
        cost_estimate=cost(6 * length * lanes * lanes),
        name="project_back",
    )(*grads, *weights, grad_one)


def swap(x, axis, bit):
    return lax.ppermute(x, axis, [(i, i ^ bit) for i in range(lax.axis_size(axis))])


def swap_two(x, one, two):
    if one[0] == two[0]:
        return swap(x, one[0], one[1] | two[1])
    wide = {"dp": lax.axis_size("mp"), "mp": 1}
    mask = one[1] * wide[one[0]] + two[1] * wide[two[0]]
    count = lax.axis_size("dp") * lax.axis_size("mp")
    return lax.ppermute(x, ("dp", "mp"), [(i, i ^ mask) for i in range(count)])


def gather_plain(w_in, w_back):
    both = jnp.stack([w_in.T, w_back])
    part = both.shape[1] // lax.axis_size("dp")
    mine = lax.dynamic_slice_in_dim(both, lax.axis_index("dp") * part, part, 1)
    return lax.all_gather(mine, ("dp", "mp"), axis=1, tiled=True)


def own_weights(w_in, w_back):
    both = jnp.stack([w_in.T, w_back])
    half = both.shape[1] // 2
    dp = lax.axis_index("dp")
    own = lax.dynamic_slice_in_dim(both, lax.rem(dp, 2) * half, half, 1)
    unit = half // 2
    mine = lax.dynamic_slice_in_dim(own, dp // 2 * unit, unit, 1)
    rest = lax.dynamic_slice_in_dim(own, (1 - dp // 2) * unit, unit, 1)
    return both, own, mine, rest


def with_other(pieces):
    return [each for piece in pieces for each in (piece, swap(piece, "dp", 1))]


def sum_everywhere(x, between):
    core = lax.rem(lax.axis_index("dp"), 2)
    half = x.shape[0] // 2
    keep = lax.dynamic_slice_in_dim(x, core * half, half, 0)
    give = lax.dynamic_slice_in_dim(x, (1 - core) * half, half, 0)
    part = keep + swap(give, "dp", 1)
    bits = [(axis, 1 << n) for axis in ("dp", "mp") for n in range(lax.axis_size(axis).bit_length() - 1)][1:]
    bits = sorted(bits, key=lambda pair: pair[1] if pair[0] == "mp" else 1)
    done = None
    for n in range(0, len(bits), 2):
        low = part.astype(bf16)
        pairs = bits[n : n + 2]
        came = [swap(low, *pair) for pair in pairs]
        if len(pairs) == 2:
            came.append(swap_two(low, *pairs))
        if between:
            done = between.pop(0)(done)
            came, done = lax.optimization_barrier((came, done))
        part = low.astype(f32) + came[0].astype(f32)
        if len(pairs) == 2:
            part = part + (came[1].astype(f32) + came[2].astype(f32))
    while between:
        done = between.pop(0)(done)
    other = swap(part, "dp", 1)
    return jnp.where(core == 0, jnp.concatenate([part, other]), jnp.concatenate([other, part])), done


def on_device(
    tokens, segment_ids, w_query, w_key, w_value, w_out, gain_one, gain_two, w_in, w_back,
    prefix_master, moment_one, moment_two, cotangent,
):
    stepwise = lax.axis_size("dp") == 4 and lax.axis_size("mp") == 8
    prefix_low = prefix_master.astype(bf16)
    prefix_keys, prefix_vals = prefix_low[0], prefix_low[1]
    first_gain, second_gain = gain_one[None, :], gain_two[None, :]
    lo, nw, segc, segk = windows(segment_ids[0])
    halves = 2
    width = tokens.shape[1] // halves
    if stepwise:
        both, own, mine, rest = own_weights(w_in, w_back)
        z_two, z_one, x_own = swap(mine, "mp", 4), swap(mine, "mp", 2), swap(own, "mp", 1)
    queries, keys_own, values_own, *first = attend_first(
        lo, nw, tokens, w_query, w_key, w_value, prefix_keys, prefix_vals, segc, segk, width
    )
    if stepwise:
        z_one, z_two, mine, rest, queries, keys_own, values_own = lax.optimization_barrier(
            (z_one, z_two, mine, rest, queries, keys_own, values_own)
        )
        z_three, z_last = swap(mine, "mp", 6), swap(rest, "mp", 2)
        x_two, y_two, x_one = swap(z_two, "mp", 1), swap(z_two, "dp", 2), swap(z_one, "mp", 1)
    seen = [first] + [
        attend_rest(lo, nw, queries, keys_own, values_own, prefix_keys, prefix_vals, segc, segk, width, part)
        for part in range(1, halves)
    ]
    attended = [pair[0] for pair in seen]
    if stepwise:
        x_two, y_two, z_three, z_last, x_own, z_one, *attended = lax.optimization_barrier(
            (x_two, y_two, z_three, z_last, x_own, z_one, *attended)
        )
        x_three, y_three, yx_two = swap(z_three, "mp", 1), swap(z_three, "dp", 2), swap(x_two, "dp", 2)
        more = with_other([x_own, z_one, z_last])
        hat, inv, normed_low, total, slope = ffn_forward(attended, tokens, w_out, first_gain, [both])
        x_three, y_three, x_one, z_last, yx_two, *rows = lax.optimization_barrier(
            (x_three, y_three, x_one, z_last, yx_two, normed_low, total, *more)
        )
        yx_three, x_last = swap(x_three, "dp", 2), swap(z_last, "mp", 1)
        normed_low, total, *more = rows
        late = with_other([z_two, x_two, y_two, x_one, z_three, x_three, y_three, yx_two])
        total, slope_more = ffn_more(normed_low, total, more)
        late, total, yx_three, x_last = lax.optimization_barrier((late, total, yx_three, x_last))
        early, slopes = [both] + more, [slope, slope_more]
        late = late + with_other([x_last, yx_three])
    else:
        every = gather_plain(w_in, w_back)
        cut = every.shape[1] * 3 // 8
        early, late = [every[:, :cut]], [every[:, cut:]]
        hat, inv, normed_low, total, slope = ffn_forward(attended, tokens, w_out, first_gain, early)
        slopes = [slope]
    layer_output, grad_one, grad_att, delta, ds_prefix, dpk, dpv = middle(
        normed_low, inv, second_gain, first_gain, prefix_keys, prefix_vals,
        total, cotangent, hat, w_out, queries, seen, slopes, early, late,
    )
    logs = [lse for _, lse in seen]
    prefix_grad, input_grad = sum_everywhere(
        jnp.stack([dpk, dpv]),
        [
            lambda _: attend_back(
                lo, nw, queries, keys_own, values_own, grad_att, logs, delta, ds_prefix, prefix_keys, segc, segk
            ),
            lambda grads: project_back(grads, (w_query, w_key, w_value), grad_one),
        ],
    )
    new_first = beta_one * moment_one + (1.0 - beta_one) * prefix_grad
    new_second = beta_two * moment_two + (1.0 - beta_two) * prefix_grad * prefix_grad
    first_hat = new_first / (1.0 - beta_one**STEP)
    second_hat = new_second / (1.0 - beta_two**STEP)
    new_master = prefix_master * (1.0 - learn_rate * weight_decay) - learn_rate * first_hat / (
        jnp.sqrt(second_hat) + epsilon_adam
    )
    return (layer_output, input_grad, new_master, new_first, new_second, new_master.astype(bf16))


def solution(mesh):
    rows = P(("dp", "mp"), None)
    return jax.shard_map(
        on_device,
        mesh=mesh,
        in_specs=(rows, rows, P(), P(), P(), P(), P(), P(), P(None, "mp"), P("mp", None), P(), P(), P(), rows),
        out_specs=(rows, rows, P(), P(), P(), P()),
        check_vma=False,
    )
```

```python
import functools

import jax
import jax.numpy as jnp
from jax import lax
from jax.experimental import pallas as pl
from jax.experimental.pallas import tpu as pltpu
from jax.sharding import PartitionSpec as P

f32, bf16 = jnp.float32, jnp.bfloat16
STEP = 5
epsilon_norm = 1e-05
learn_rate = 1.0
weight_decay = 0.01
beta_one = 0.9
beta_two = 0.999
epsilon_adam = 1e-08
HEAD_SCALE = 0.125
NEG = -1e30
WIN = 256
KC = 64
QUAD = 256
LEAST, MOST = 1e-25, 1e30
ITEMS = 64
VMEM = 60 << 20
NN = (((1,), (0,)), ((), ()))
NT = (((1,), (1,)), ((), ()))
TN = (((0,), (0,)), ((), ()))


def dot(a, b, d=NN):
    return lax.dot_general(a, b, d, preferred_element_type=f32)


def vm():
    return pl.BlockSpec(memory_space=pltpu.VMEM)


def sm():
    return pl.BlockSpec(memory_space=pltpu.SMEM)


def hbm():
    return pl.BlockSpec(memory_space=pl.ANY)


def cost(flops, moved=8 << 20):
    return pl.CostEstimate(flops=4 * flops, bytes_accessed=moved, transcendentals=0)


def part_of(array, width, part):
    return pl.BlockSpec((array.shape[0], width), lambda i: (0, part))


def whole_of(array):
    return pl.BlockSpec(array.shape, lambda i: (0, 0))


def block_diag(piece):
    lane = lax.broadcasted_iota(jnp.int32, piece.shape, 1) // 64
    zero = jnp.zeros_like(piece)
    return jnp.concatenate([jnp.where(lane == h, piece, zero) for h in range(4)], axis=0)


def diag_of(full):
    lane = lax.broadcasted_iota(jnp.int32, (KC, 128), 1) < 64
    left = jnp.where(lane, full[0:64, 0:128], full[64:128, 0:128])
    right = jnp.where(lane, full[128:192, 128:256], full[192:256, 128:256])
    return jnp.concatenate([left, right], axis=1)


def head_ones():
    row = lax.broadcasted_iota(jnp.int32, (QUAD, QUAD), 0) // 64
    lane = lax.broadcasted_iota(jnp.int32, (QUAD, QUAD), 1) // 64
    return jnp.where(row == lane, 1.0, 0.0).astype(bf16)


def head_sum(x, ones):
    high = x.astype(bf16)
    return dot(high, ones) + dot((x - high.astype(f32)).astype(bf16), ones)


def head_max(x):
    lane = lax.broadcasted_iota(jnp.int32, x.shape, 1) < 64
    a = jnp.max(jnp.where(lane, x, NEG), axis=1, keepdims=True)
    b = jnp.max(jnp.where(lane, NEG, x), axis=1, keepdims=True)
    return jnp.where(lane, a, b)


def windows(seg):
    length = seg.shape[0]
    by = seg.reshape(length // KC, KC)
    first, last = by[:, 0], by[:, -1]
    lo = jnp.sum((seg[None, :] < first[:, None]).astype(jnp.int32), axis=1)
    hi = jnp.sum((seg[None, :] <= last[:, None]).astype(jnp.int32), axis=1)
    lo = lo // 16 * 16
    nw = (hi - lo + WIN - 1) // WIN
    segc = jnp.broadcast_to(seg[:, None], (length, 128))
    segk = jnp.concatenate([by, by], axis=1)
    return lo, nw, segc, segk


def list_items(lo_ref, nw_ref, chunk_ref, row_ref, length):
    def chunk(c, count):
        def one(w, count):
            chunk_ref[count] = c
            row_ref[count] = lo_ref[c] + w * WIN
            return count + 1

        return lax.fori_loop(0, nw_ref[c], one, count)

    count = lax.fori_loop(0, length // KC, chunk, 0)
    for n in range(2):
        chunk_ref[count + n] = 0
        row_ref[count + n] = length
    return count


def item_at(n, chunk_ref, row_ref, segc_ref, segk_ref, length):
    c, nominal = chunk_ref[n], row_ref[n]
    start = pl.multiple_of(jnp.minimum(nominal, length - WIN), 16)
    rows = pl.ds(start, WIN)
    keys = pl.ds(pl.multiple_of(c * KC, KC), KC)
    row_id = lax.broadcasted_iota(jnp.int32, (WIN, 128), 0) + start
    keep = jnp.logical_and(segc_ref[rows, :] == segk_ref[pl.ds(c, 1), :], row_id >= nominal)
    bias = jnp.where(keep, 0.0, NEG)
    return rows, keys, jnp.concatenate([bias, bias], axis=1)


def staged(units, first, second, third):
    raw, done = first(units[0]), None
    for n in range(len(units) + 1):
        upcoming = first(units[n + 1]) if n + 1 < len(units) else None
        fresh = second(units[n], raw) if n < len(units) else None
        if done is not None:
            third(units[n - 1], done)
        raw, done = upcoming, fresh


def join_copies(pieces, buffer, target, sems):
    copies, row = [], 0
    for n, piece in enumerate(pieces):
        rows = piece.shape[1]
        copies.append(pltpu.make_async_copy(piece, buffer.at[:, row : row + rows], sems.at[n]))
        row += rows
    return copies, [pltpu.make_async_copy(buffer, target, sems.at[len(pieces)])]


def begin(copies):
    for copy in copies:
        copy.start()


def finish(copies):
    for copy in copies:
        copy.wait()


def joined_shape(pieces):
    planes, _, lanes = pieces[0].shape
    return jax.ShapeDtypeStruct((planes, sum(piece.shape[1] for piece in pieces), lanes), pieces[0].dtype)


def attend_columns(count, q_ref, k_ref, v_ref, pk_ref, pv_ref, att_ref, lse_ref, l_ref, acc_ref, item, ones):
    length, width = att_ref.shape
    parts = [slice(c, c + QUAD) for c in range(0, width, QUAD)]
    spans = [slice(r, r + WIN) for r in range(0, length, WIN)]
    ids = range(len(parts))

    def sweep(shift):
        bdk = [block_diag(pk_ref[:, cols]) for cols in parts]
        bdv = [block_diag(pv_ref[:, cols]) for cols in parts]

        def moved(s, rows, cols):
            return s if shift is None else s - shift[rows, cols]

        def start_third(unit, p):
            rows, g = unit
            l_ref[rows, parts[g]] = p
            acc_ref[rows, parts[g]] = dot(p.astype(bf16), bdv[g])

        staged(
            [(rows, g) for g in ids for rows in spans],
            lambda u: dot(q_ref[u[0], parts[u[1]]], bdk[u[1]], NT),
            lambda u, s: jnp.exp(moved(s, u[0], parts[u[1]])),
            start_third,
        )

        @pl.loop(0, (count + 1) // 2)
        def _(n):
            def third(unit, p):
                (rows, keys, _), g = unit
                l_ref[rows, parts[g]] += p
                acc_ref[rows, parts[g]] += dot(p.astype(bf16), block_diag(v_ref[keys, parts[g]]))

            staged(
                [(one, g) for one in (item(2 * n), item(2 * n + 1)) for g in ids],
                lambda u: dot(q_ref[u[0][0], parts[u[1]]], block_diag(k_ref[u[0][1], parts[u[1]]]), NT),
                lambda u, s: jnp.exp(moved(s, u[0][0], parts[u[1]]) + u[0][2]),
                third,
            )

        least, most = [], []
        for rows in spans:
            for cols in parts:
                total = head_sum(l_ref[rows, cols], ones)
                att_ref[rows, cols] = (acc_ref[rows, cols] / total).astype(bf16)
                low = jnp.log(total)
                lse_ref[rows, cols] = low if shift is None else low + shift[rows, cols]
                least.append(jnp.min(total, axis=0, keepdims=True))
                most.append(jnp.max(total, axis=0, keepdims=True))
        return jnp.min(functools.reduce(jnp.minimum, least)), jnp.max(functools.reduce(jnp.maximum, most))

    least, most = sweep(None)

    @pl.when(jnp.logical_not(jnp.logical_and(least > LEAST, most < MOST)))
    def _():
        for cols in parts:
            bdk = block_diag(pk_ref[:, cols])
            for rows in spans:
                lse_ref[rows, cols] = dot(q_ref[rows, cols], bdk, NT)

        @pl.loop(0, count)
        def _(n):
            rows, keys, bias = item(n)
            for cols in parts:
                s = dot(q_ref[rows, cols], block_diag(k_ref[keys, cols]), NT) + bias
                lse_ref[rows, cols] = jnp.maximum(lse_ref[rows, cols], s)

        @pl.loop(0, length // WIN)
        def _(r):
            rows = pl.ds(pl.multiple_of(r * WIN, WIN), WIN)
            for c in range(0, width, 128):
                cols = slice(c, c + 128)
                lse_ref[rows, cols] = head_max(lse_ref[rows, cols])

        sweep(lse_ref)


def attend_first_kernel(
    lo_ref, nw_ref, x_ref, wq_hbm, wk_hbm, wv_hbm, pk_ref, pv_ref, segc_ref, segk_ref,
    q_hbm, k_hbm, v_hbm, att_ref, lse_ref,
    w_ref, q_ref, k_ref, v_ref, l_ref, acc_ref, chunk_ref, row_ref, in_sems, out_sems,
):
    length, lanes = x_ref.shape
    loads = [pltpu.make_async_copy(w, w_ref.at[n], in_sems.at[n]) for n, w in enumerate((wq_hbm, wk_hbm, wv_hbm))]
    stores = [
        pltpu.make_async_copy(a, b, out_sems.at[n])
        for n, (a, b) in enumerate(((q_ref, q_hbm), (k_ref, k_hbm), (v_ref, v_hbm)))
    ]
    for load in loads:
        load.start()
    count = list_items(lo_ref, nw_ref, chunk_ref, row_ref, length)
    for n, out_ref in enumerate((q_ref, k_ref, v_ref)):
        loads[n].wait()
        for c in range(0, lanes, QUAD):
            value = dot(x_ref[...], w_ref[n, :, c : c + QUAD])
            out_ref[:, c : c + QUAD] = (value * HEAD_SCALE if n == 0 else value).astype(bf16)
        stores[n].start()

    def item(n):
        return item_at(n, chunk_ref, row_ref, segc_ref, segk_ref, length)

    attend_columns(
        count, q_ref, k_ref, v_ref, pk_ref, pv_ref, att_ref, lse_ref, l_ref, acc_ref, item, head_ones()
    )
    for store in stores:
        store.wait()


def attend_rest_kernel(*refs, count):
    lo_ref, nw_ref, q_ref, k_ref, v_ref, pk_ref, pv_ref, segc_ref, segk_ref = refs[:9]
    pieces, refs = refs[9 : 9 + count], refs[9 + count :]
    att_ref, lse_ref, refs = refs[0], refs[1], refs[2:]
    arrive, leave = [], []
    if count:
        target, *refs, held, sems = refs
        arrive, leave = join_copies(pieces, held, target, sems)
    l_ref, acc_ref, chunk_ref, row_ref = refs
    begin(arrive)
    length = q_ref.shape[0]
    items = list_items(lo_ref, nw_ref, chunk_ref, row_ref, length)
    finish(arrive)
    begin(leave)

    def item(n):
        return item_at(n, chunk_ref, row_ref, segc_ref, segk_ref, length)

    attend_columns(
        items, q_ref, k_ref, v_ref, pk_ref, pv_ref, att_ref, lse_ref, l_ref, acc_ref, item, head_ones()
    )
    finish(leave)


def attend_first(lo, nw, x, wq, wk, wv, pk, pv, segc, segk, width):
    length, lanes = x.shape
    low = jax.ShapeDtypeStruct((length, lanes), bf16)
    return pl.pallas_call(
        attend_first_kernel,
        out_shape=(low, low, low, jax.ShapeDtypeStruct((length, width), bf16), jax.ShapeDtypeStruct((length, width), f32)),
        in_specs=[sm(), sm(), vm(), hbm(), hbm(), hbm(), vm(), vm(), vm(), vm()],
        out_specs=(hbm(), hbm(), hbm(), vm(), vm()),
        scratch_shapes=[pltpu.VMEM((3, lanes, lanes), bf16)]
        + [pltpu.VMEM((length, lanes), bf16)] * 3
        + [pltpu.VMEM((length, width), f32)] * 2
        + [pltpu.SMEM((ITEMS,), jnp.int32)] * 2
        + [pltpu.SemaphoreType.DMA((3,))] * 2,
        compiler_params=pltpu.CompilerParams(vmem_limit_bytes=VMEM),
        cost_estimate=cost(16 * length * lanes * lanes),
        name="attend_first",
    )(lo, nw, x, wq, wk, wv, pk, pv, segc, segk)


def attend_rest(lo, nw, q, k, v, pk, pv, segc, segk, width, part, pieces):
    length = q.shape[0]
    outs = [jax.ShapeDtypeStruct((length, width), bf16), jax.ShapeDtypeStruct((length, width), f32)]
    specs = [pl.BlockSpec((length, width), lambda i: (0, 0))] * 2
    scratch = [pltpu.VMEM((length, width), f32)] * 2 + [pltpu.SMEM((ITEMS,), jnp.int32)] * 2
    if pieces:
        held = joined_shape(pieces)
        outs.append(held)
        specs.append(hbm())
        scratch += [pltpu.VMEM(held.shape, held.dtype), pltpu.SemaphoreType.DMA((len(pieces) + 1,))]
    return pl.pallas_call(
        functools.partial(attend_rest_kernel, count=len(pieces)),
        grid=(1,),
        out_shape=tuple(outs),
        in_specs=[sm(), sm()]
        + [part_of(a, width, part) for a in (q, k, v, pk, pv)]
        + [whole_of(segc), whole_of(segk)]
        + [hbm()] * len(pieces),
        out_specs=tuple(specs),
        scratch_shapes=scratch,
        compiler_params=pltpu.CompilerParams(vmem_limit_bytes=VMEM),
        cost_estimate=cost(16000 * length * width),
        name="attend_rest",
    )(lo, nw, q, k, v, pk, pv, segc, segk, *pieces)


def attend_back_kernel(*refs, halves):
    lo_ref, nw_ref, pk_ref, segc_ref, segk_ref = refs[:5]
    sources, refs = refs[5 : 11 + halves], refs[11 + halves :]
    (
        dq_hbm, dk_hbm, dv_hbm,
        q_ref, k_ref, v_ref, g_ref, delta_ref, ds_ref, lse_ref,
        dq_acc, dk_acc, dv_acc, dq_ref, dk_ref, dv_ref, chunk_ref, row_ref, in_sems, out_sems,
    ) = refs
    length, lanes = q_ref.shape
    parts = [slice(g * QUAD, (g + 1) * QUAD) for g in range(lanes // QUAD)]
    spans = [slice(r * WIN, (r + 1) * WIN) for r in range(length // WIN)]
    places = [ds_ref, q_ref, k_ref, v_ref, g_ref, delta_ref]
    for n in range(halves):
        places.append(lse_ref.at[:, n * (lanes // halves) : (n + 1) * (lanes // halves)])
    loads = [pltpu.make_async_copy(a, b, in_sems.at[n]) for n, (a, b) in enumerate(zip(sources, places))]
    for load in loads:
        load.start()
    count = list_items(lo_ref, nw_ref, chunk_ref, row_ref, length)
    dk_acc[...] = jnp.zeros_like(dk_acc)
    dv_acc[...] = jnp.zeros_like(dv_acc)
    loads[0].wait()
    for cols in parts:
        bdk = block_diag(pk_ref[:, cols])
        for rows in spans:
            dq_acc[rows, cols] = dot(ds_ref[rows, cols], bdk)
    for load in loads[1:]:
        load.wait()
    ids = range(len(parts))

    @pl.loop(0, (count + 1) // 2)
    def _(n):
        def first(unit):
            (rows, keys, _), g = unit
            cols = parts[g]
            s = dot(q_ref[rows, cols], block_diag(k_ref[keys, cols]), NT)
            return s, dot(g_ref[rows, cols], block_diag(v_ref[keys, cols]), NT)

        def second(unit, pair):
            (rows, _, bias), g = unit
            cols = parts[g]
            p = jnp.exp(pair[0] + bias - lse_ref[rows, cols])
            return p.astype(bf16), (p * (pair[1] - delta_ref[rows, cols])).astype(bf16)

        def third(unit, pair):
            (rows, keys, _), g = unit
            cols = parts[g]
            dv_acc[keys, cols] += diag_of(dot(pair[0], g_ref[rows, cols], TN))
            dk_acc[keys, cols] += diag_of(dot(pair[1], q_ref[rows, cols], TN))
            dq_acc[rows, cols] += dot(pair[1], block_diag(k_ref[keys, cols]))

        items = [item_at(2 * n + i, chunk_ref, row_ref, segc_ref, segk_ref, length) for i in range(2)]
        staged([(one, g) for one in items for g in ids], first, second, third)

    stores = []
    ends = ((dq_acc, dq_ref, dq_hbm, HEAD_SCALE), (dk_acc, dk_ref, dk_hbm, 1.0), (dv_acc, dv_ref, dv_hbm, 1.0))
    for n, (acc, low, target, scale) in enumerate(ends):
        low[...] = (acc[...] * scale).astype(bf16)
        stores.append(pltpu.make_async_copy(low, target, out_sems.at[n]))
        stores[n].start()
    for store in stores:
        store.wait()


def attend_back(lo, nw, q, k, v, g, lse, delta, ds, pk, segc, segk):
    length, lanes = q.shape
    tall = (length, lanes)
    return pl.pallas_call(
        functools.partial(attend_back_kernel, halves=len(lse)),
        out_shape=(jax.ShapeDtypeStruct(tall, bf16),) * 3,
        in_specs=[sm(), sm(), vm(), vm(), vm()] + [hbm()] * (6 + len(lse)),
        out_specs=(hbm(),) * 3,
        scratch_shapes=[pltpu.VMEM(tall, t) for t in (bf16, bf16, bf16, bf16, f32, bf16, f32)]
        + [pltpu.VMEM(tall, f32)] * 3
        + [pltpu.VMEM(tall, bf16)] * 3
        + [pltpu.SMEM((ITEMS,), jnp.int32)] * 2
        + [pltpu.SemaphoreType.DMA((6 + len(lse),)), pltpu.SemaphoreType.DMA((3,))],
        compiler_params=pltpu.CompilerParams(vmem_limit_bytes=VMEM),
        cost_estimate=cost(length * lanes * 30000),
        name="attend_back",
    )(lo, nw, pk, segc, segk, ds, q, k, v, g, delta, *lse)


HID = 512


def mean_of(x):
    return jnp.mean(x, axis=-1, keepdims=True)


def centre(x):
    centred = x - mean_of(x)
    inv = lax.rsqrt(mean_of(centred * centred) + epsilon_norm)
    return centred * inv, inv


def pull_norm(pull, hat, inv):
    return inv * (pull - mean_of(pull) - hat * mean_of(pull * hat))


def gelu_pair(x):
    phi = 0.5 + 0.5 * lax.erf(x * 0.7071067811865476)
    bell = 0.3989422804014327 * jnp.exp(-0.5 * (x * x))
    return x * phi, phi + x * bell


def blocks_of(pieces):
    blocks, block, room = [], [], HID
    for piece in pieces:
        row = 0
        while row < piece.shape[1]:
            rows = min(room, piece.shape[1] - row)
            block.append((piece, row, rows))
            row, room = row + rows, room - rows
            if room == 0:
                blocks.append(block)
                block, room = [], HID
    return blocks


def most_of(pieces):
    return max(len(block) for block in blocks_of(pieces))


def block_copies(block, buffer, sems, slot):
    copies, place = [], 0
    for n, (piece, row, rows) in enumerate(block):
        source = piece.at[:, row : row + rows]
        copies.append(pltpu.make_async_copy(source, buffer.at[slot, :, place : place + rows], sems.at[slot, n]))
        place += rows
    return copies


def forward_block(low_ref, weights, sum_ref, slope_ref, cols):
    def second(rows, x):
        act, slope = gelu_pair(x)
        slope_ref[rows, cols] = slope.astype(bf16)
        return act.astype(bf16)

    def third(rows, act):
        sum_ref[rows, :] += dot(act, weights[1])

    spans = [slice(r, r + WIN) for r in range(0, low_ref.shape[0], WIN)]
    staged(spans, lambda rows: dot(low_ref[rows, :], weights[0], NT), second, third)


def ffn_kernel(*refs, halves, count, others):
    atts, (tok_ref, w_out_ref, gain_ref), refs = refs[:halves], refs[halves : halves + 3], refs[halves + 3 :]
    blocks, pieces, refs = blocks_of(refs[:count]), refs[count : count + others], refs[count + others :]
    hat_ref, inv_ref, low_ref, sum_ref, slope_ref, *refs = refs
    arrive, leave = [], []
    if others:
        target, *refs, held, join_sems = refs
        arrive, leave = join_copies(pieces, held, target, join_sems)
    buffer, sems = refs
    width = atts[0].shape[1]
    copies = [block_copies(block, buffer, sems, b % 2) for b, block in enumerate(blocks)]
    begin(copies[0])
    begin(arrive)

    def second(rows, x):
        hat, inv = centre(tok_ref[rows, :].astype(f32) + x)
        hat_ref[rows, :] = hat
        inv_ref[rows, :] = jnp.broadcast_to(inv, (WIN, 128))
        normed = gain_ref[...] * hat
        sum_ref[rows, :] = normed
        low_ref[rows, :] = normed.astype(bf16)

    def first(rows):
        return sum(dot(att_ref[rows, :], w_out_ref[n * width : (n + 1) * width, :]) for n, att_ref in enumerate(atts))

    spans = [slice(r, r + WIN) for r in range(0, tok_ref.shape[0], WIN)]
    staged(spans, first, second, lambda rows, x: None)
    finish(arrive)
    begin(leave)
    for b in range(len(blocks)):
        if b + 1 < len(blocks):
            begin(copies[b + 1])
        finish(copies[b])
        forward_block(low_ref, buffer.at[b % 2], sum_ref, slope_ref, slice(b * HID, (b + 1) * HID))
    finish(leave)


def ffn_forward(att, tokens, w_out, gain, pieces, others):
    length, lanes = tokens.shape
    hidden = sum(piece.shape[1] for piece in pieces)
    wide = jax.ShapeDtypeStruct((length, lanes), f32)
    outs = [
        wide,
        jax.ShapeDtypeStruct((length, 128), f32),
        jax.ShapeDtypeStruct((length, lanes), bf16),
        wide,
        jax.ShapeDtypeStruct((length, hidden), bf16),
    ]
    specs = [vm()] * 5
    scratch = [pltpu.VMEM((2, 2, HID, lanes), bf16), pltpu.SemaphoreType.DMA((2, most_of(pieces)))]
    if others:
        held = joined_shape(others)
        outs.append(held)
        specs.append(hbm())
        scratch += [pltpu.VMEM(held.shape, held.dtype), pltpu.SemaphoreType.DMA((len(others) + 1,))]
    return pl.pallas_call(
        functools.partial(ffn_kernel, halves=len(att), count=len(pieces), others=len(others)),
        out_shape=tuple(outs),
        in_specs=[vm()] * (len(att) + 3) + [hbm()] * (len(pieces) + len(others)),
        out_specs=tuple(specs),
        scratch_shapes=scratch,
        compiler_params=pltpu.CompilerParams(vmem_limit_bytes=VMEM),
        cost_estimate=cost(4 * length * lanes * (hidden + lanes)),
        name="ffn_forward",
    )(*att, tokens, w_out, gain, *pieces, *others)


def more_kernel(low_ref, start_ref, *refs, count):
    blocks = blocks_of(refs[:count])
    sum_ref, slope_ref, buffer, sems = refs[count:]
    copies = [block_copies(block, buffer, sems, b % 2) for b, block in enumerate(blocks)]
    begin(copies[0])
    sum_ref[...] = start_ref[...]
    for b in range(len(blocks)):
        if b + 1 < len(blocks):
            begin(copies[b + 1])
        finish(copies[b])
        forward_block(low_ref, buffer.at[b % 2], sum_ref, slope_ref, slice(b * HID, (b + 1) * HID))


def ffn_more(low, start, pieces):
    length, lanes = low.shape
    hidden = sum(piece.shape[1] for piece in pieces)
    return pl.pallas_call(
        functools.partial(more_kernel, count=len(pieces)),
        out_shape=(jax.ShapeDtypeStruct((length, lanes), f32), jax.ShapeDtypeStruct((length, hidden), bf16)),
        in_specs=[vm()] * 2 + [hbm()] * len(pieces),
        out_specs=(vm(),) * 2,
        scratch_shapes=[pltpu.VMEM((2, 2, HID, lanes), bf16), pltpu.SemaphoreType.DMA((2, most_of(pieces)))],
        compiler_params=pltpu.CompilerParams(vmem_limit_bytes=VMEM),
        cost_estimate=cost(4 * length * lanes * hidden),
        name="ffn_more",
    )(low, start, *pieces)


def middle_kernel(*refs, halves, early, late, groups):
    low_ref, inv_ref, gain_two_ref, gain_one_ref, pk_ref, pv_ref = refs[:6]
    sum_hbm, cot_hbm, hat_hbm, w_out_hbm, q_hbm = refs[6:11]
    seen, refs = refs[11 : 11 + 2 * halves], refs[11 + 2 * halves :]
    slopes, pieces, refs = refs[:groups], refs[groups : groups + early + late], refs[groups + early + late :]
    (layer_hbm, one_hbm, g_hbm, delta_hbm, ds_hbm, dpk_ref, dpv_ref) = refs[:7]
    (
        acc_ref, cot_ref, hat_ref, w_out_ref, q_ref, att_ref, lse_ref, layer_ref, one_ref, g_ref, delta_ref, ds_ref,
        grad_ref, late_ref, buffer, sbuf, sems, ssems, in_sems, out_sems,
    ) = refs[7:]
    length, lanes = low_ref.shape
    spans = [slice(r, r + WIN) for r in range(0, length, WIN)]
    parts = [slice(c, c + QUAD) for c in range(0, lanes, QUAD)]
    first_blocks, last_blocks = blocks_of(pieces[:early]), blocks_of(pieces[early:])
    order = last_blocks + first_blocks + last_blocks
    copies = [block_copies(block, buffer, sems, n % 2) for n, block in enumerate(order)]
    skip = len(last_blocks)
    slabs = [slope.at[:, c : c + HID] for slope in slopes for c in range(0, slope.shape[1], HID)]
    for n, source in enumerate(slabs, skip):
        copies[n].append(pltpu.make_async_copy(source, sbuf.at[n % 2], ssems.at[n % 2]))
    sources = (sum_hbm, cot_hbm, hat_hbm, w_out_hbm, q_hbm, *seen)
    places = [acc_ref, cot_ref, hat_ref, w_out_ref, q_ref]
    for n in range(halves):
        cols = slice(n * (lanes // halves), (n + 1) * (lanes // halves))
        places += [att_ref.at[:, cols], lse_ref.at[:, cols]]
    loads = [pltpu.make_async_copy(a, b, in_sems.at[n]) for n, (a, b) in enumerate(zip(sources, places))]
    results = (layer_ref, one_ref, g_ref, delta_ref, ds_ref)
    targets = (layer_hbm, one_hbm, g_hbm, delta_hbm, ds_hbm)
    stores = [pltpu.make_async_copy(a, b, out_sems.at[n]) for n, (a, b) in enumerate(zip(results, targets))]
    begin(copies[0])
    begin(loads[:1])

    def enter(n):
        if n + 1 < len(order):
            begin(copies[n + 1])
        if n == 0:
            finish(loads[:1])
            begin(loads[1:])
        finish(copies[n])
        return buffer.at[n % 2]

    for n in range(skip):
        forward_block(low_ref, enter(n), acc_ref, late_ref, slice(n * HID, (n + 1) * HID))

    finish(loads[1:3])
    for n in range(skip, len(order)):
        weights = enter(n)
        past = n - skip - len(first_blocks)

        def first(rows):
            if n == skip:
                hat, inv = centre(acc_ref[rows, :])
                layer_ref[rows, :] = (gain_two_ref[...] * hat).astype(bf16)
                grad = pull_norm(cot_ref[rows, :].astype(f32) * gain_two_ref[...], hat, inv)
                acc_ref[rows, :] = grad
                grad_ref[rows, :] = grad.astype(bf16)
            return dot(grad_ref[rows, :], weights[1], NT)

        def second(rows, x):
            slope = sbuf[n % 2, rows, :] if past < 0 else late_ref[rows, past * HID : (past + 1) * HID]
            return (x * slope.astype(f32)).astype(bf16)

        def third(rows, x):
            acc_ref[rows, :] += dot(x, weights[0])

        staged(spans, first, second, third)
        if n == skip:
            begin(stores[:1])
    finish(loads[3:])

    def first(rows):
        grad = pull_norm(acc_ref[rows, :] * gain_one_ref[...], hat_ref[rows, :], inv_ref[rows, 0:1])
        one_ref[rows, :] = grad
        return grad.astype(bf16)

    def second(rows, grad):
        g_ref[rows, :] = dot(grad, w_out_ref[...], NT).astype(bf16)

    staged(spans, first, second, lambda rows, x: None)
    begin(stores[1:3])

    ones = head_ones()
    sums = {}

    def first(unit):
        g, rows = unit
        cols = parts[g]
        up = g_ref[rows, cols]
        delta = head_sum(up.astype(f32) * att_ref[rows, cols].astype(f32), ones)
        return dot(q_ref[rows, cols], block_diag(pk_ref[:, cols]), NT), dot(up, block_diag(pv_ref[:, cols]), NT), delta

    def second(unit, three):
        g, rows = unit
        cols = parts[g]
        delta_ref[rows, cols] = three[2]
        p = jnp.exp(three[0] - lse_ref[rows, cols])
        ds = (p * (three[1] - three[2])).astype(bf16)
        ds_ref[rows, cols] = ds
        return p.astype(bf16), ds

    def third(unit, pair):
        g, rows = unit
        cols = parts[g]
        dpv, dpk = diag_of(dot(pair[0], g_ref[rows, cols], TN)), diag_of(dot(pair[1], q_ref[rows, cols], TN))
        if rows.start:
            dpv, dpk = sums[g][0] + dpv, sums[g][1] + dpk
        sums[g] = (dpv, dpk)
        if rows.stop == length:
            dpv_ref[:, cols], dpk_ref[:, cols] = dpv, dpk

    staged([(g, rows) for g in range(len(parts)) for rows in spans], first, second, third)
    begin(stores[3:])
    finish(stores)


def middle(low, inv, gain_two, gain_one, pk, pv, total, cot, hat, w_out, q, seen, slopes, early, late):
    length, lanes = low.shape
    slots = pk.shape[0]
    late_units = sum(piece.shape[1] for piece in late)
    flat = [each for pair in seen for each in pair]
    tall = (length, lanes)
    small = jax.ShapeDtypeStruct((slots, lanes), f32)
    holds = [f32, bf16, f32, None, bf16, bf16, f32, bf16, f32, bf16, f32, bf16, bf16]
    return pl.pallas_call(
        functools.partial(middle_kernel, halves=len(seen), early=len(early), late=len(late), groups=len(slopes)),
        out_shape=tuple(jax.ShapeDtypeStruct(tall, t) for t in (bf16, f32, bf16, f32, bf16)) + (small, small),
        in_specs=[vm()] * 6 + [hbm()] * (5 + 2 * len(seen) + len(slopes) + len(early) + len(late)),
        out_specs=(hbm(),) * 5 + (vm(), vm()),
        scratch_shapes=[pltpu.VMEM((lanes, lanes), bf16) if t is None else pltpu.VMEM(tall, t) for t in holds]
        + [
            pltpu.VMEM((length, late_units), bf16),
            pltpu.VMEM((2, 2, HID, lanes), bf16),
            pltpu.VMEM((2, length, HID), bf16),
            pltpu.SemaphoreType.DMA((2, most_of(early + late))),
            pltpu.SemaphoreType.DMA((2,)),
            pltpu.SemaphoreType.DMA((5 + len(flat),)),
            pltpu.SemaphoreType.DMA((5,)),
        ],
        compiler_params=pltpu.CompilerParams(vmem_limit_bytes=VMEM),
        cost_estimate=cost(40 * length * lanes * lanes),
        name="middle",
    )(low, inv, gain_two, gain_one, pk, pv, total, cot, hat, w_out, q, *flat, *slopes, *early, *late)


def project_kernel(dq_hbm, dk_hbm, dv_hbm, wq_hbm, wk_hbm, wv_hbm, one_hbm, out_hbm, grads, weights, out_ref, *sems):
    length, lanes = out_ref.shape
    spans = [slice(r, r + WIN) for r in range(0, length, WIN)]
    grad_sems, weight_sems, one_sem, out_sems = sems
    loads = []
    for n, (grad, weight) in enumerate(((dq_hbm, wq_hbm), (dk_hbm, wk_hbm), (dv_hbm, wv_hbm))):
        loads.append(
            (
                pltpu.make_async_copy(grad, grads.at[n], grad_sems.at[n]),
                pltpu.make_async_copy(weight, weights.at[n], weight_sems.at[n]),
            )
        )
        begin(loads[n])
        if n == 0:
            one = pltpu.make_async_copy(one_hbm, out_ref, one_sem.at[0])
            one.start()
    stores = [
        pltpu.make_async_copy(out_ref.at[rows, :], out_hbm.at[rows, :], out_sems.at[r]) for r, rows in enumerate(spans)
    ]
    finish(loads[0])
    first = [dot(grads[0, rows, :], weights[0], NT) for rows in spans[:1]]
    one.wait()
    out_ref[spans[0], :] += first[0]
    for rows in spans[1:]:
        out_ref[rows, :] += dot(grads[0, rows, :], weights[0], NT)
    finish(loads[1])
    finish(loads[2])
    for r, rows in enumerate(spans):
        more = dot(grads[1, rows, :], weights[1], NT) + dot(grads[2, rows, :], weights[2], NT)
        out_ref[rows, :] += more
        stores[r].start()
    finish(stores)


def project_back(grads, weights, grad_one):
    length, lanes = grad_one.shape
    return pl.pallas_call(
        project_kernel,
        out_shape=jax.ShapeDtypeStruct((length, lanes), f32),
        in_specs=[hbm()] * 7,
        out_specs=hbm(),
        scratch_shapes=[
            pltpu.VMEM((3, length, lanes), bf16),
            pltpu.VMEM((3, lanes, lanes), bf16),
            pltpu.VMEM((length, lanes), f32),
            pltpu.SemaphoreType.DMA((3,)),
            pltpu.SemaphoreType.DMA((3,)),
            pltpu.SemaphoreType.DMA((1,)),
            pltpu.SemaphoreType.DMA((length // WIN,)),
        ],
        compiler_params=pltpu.CompilerParams(vmem_limit_bytes=VMEM),
        cost_estimate=cost(6 * length * lanes * lanes),
        name="project_back",
    )(*grads, *weights, grad_one)


def swap(x, axis, bit):
    return lax.ppermute(x, axis, [(i, i ^ bit) for i in range(lax.axis_size(axis))])


def swap_two(x, one, two):
    if one[0] == two[0]:
        return swap(x, one[0], one[1] | two[1])
    wide = {"dp": lax.axis_size("mp"), "mp": 1}
    mask = one[1] * wide[one[0]] + two[1] * wide[two[0]]
    count = lax.axis_size("dp") * lax.axis_size("mp")
    return lax.ppermute(x, ("dp", "mp"), [(i, i ^ mask) for i in range(count)])


def gather_plain(w_in, w_back):
    both = jnp.stack([w_in.T, w_back])
    part = both.shape[1] // lax.axis_size("dp")
    mine = lax.dynamic_slice_in_dim(both, lax.axis_index("dp") * part, part, 1)
    return lax.all_gather(mine, ("dp", "mp"), axis=1, tiled=True)


def own_weights(w_in, w_back):
    both = jnp.stack([w_in.T, w_back])
    half = both.shape[1] // 2
    dp = lax.axis_index("dp")
    own = lax.dynamic_slice_in_dim(both, lax.rem(dp, 2) * half, half, 1)
    unit = half // 2
    mine = lax.dynamic_slice_in_dim(own, dp // 2 * unit, unit, 1)
    rest = lax.dynamic_slice_in_dim(own, (1 - dp // 2) * unit, unit, 1)
    return both, own, mine, rest


def with_other(pieces):
    return [each for piece in pieces for each in (piece, swap(piece, "dp", 1))]


def sum_everywhere(x, between):
    core = lax.rem(lax.axis_index("dp"), 2)
    half = x.shape[0] // 2
    keep = lax.dynamic_slice_in_dim(x, core * half, half, 0)
    give = lax.dynamic_slice_in_dim(x, (1 - core) * half, half, 0)
    part = keep + swap(give, "dp", 1)
    bits = [(axis, 1 << n) for axis in ("dp", "mp") for n in range(lax.axis_size(axis).bit_length() - 1)][1:]
    bits = sorted(bits, key=lambda pair: pair[1] if pair[0] == "mp" else 1)
    done = None
    for n in range(0, len(bits), 2):
        low = part.astype(bf16)
        pairs = bits[n : n + 2]
        came = [swap(low, *pair) for pair in pairs]
        if len(pairs) == 2:
            came.append(swap_two(low, *pairs))
        if between:
            done = between.pop(0)(done)
            came, done = lax.optimization_barrier((came, done))
        part = low.astype(f32) + came[0].astype(f32)
        if len(pairs) == 2:
            part = part + (came[1].astype(f32) + came[2].astype(f32))
    while between:
        done = between.pop(0)(done)
    other = swap(part, "dp", 1)
    return jnp.where(core == 0, jnp.concatenate([part, other]), jnp.concatenate([other, part])), done


def on_device(
    tokens, segment_ids, w_query, w_key, w_value, w_out, gain_one, gain_two, w_in, w_back,
    prefix_master, moment_one, moment_two, cotangent,
):
    stepwise = lax.axis_size("dp") == 4 and lax.axis_size("mp") == 8
    prefix_low = prefix_master.astype(bf16)
    prefix_keys, prefix_vals = prefix_low[0], prefix_low[1]
    first_gain, second_gain = gain_one[None, :], gain_two[None, :]
    lo, nw, segc, segk = windows(segment_ids[0])
    halves = 2
    width = tokens.shape[1] // halves
    if stepwise:
        both, own, mine, rest = own_weights(w_in, w_back)
        z_two, z_one, x_own = swap(mine, "mp", 4), swap(mine, "mp", 2), swap(own, "mp", 1)
    queries, keys_own, values_own, *first = attend_first(
        lo, nw, tokens, w_query, w_key, w_value, prefix_keys, prefix_vals, segc, segk, width
    )
    if stepwise:
        z_one, z_two, x_own, mine, rest, queries, keys_own, values_own = lax.optimization_barrier(
            (z_one, z_two, x_own, mine, rest, queries, keys_own, values_own)
        )
        z_three, z_last = swap(mine, "mp", 6), swap(rest, "mp", 2)
        x_two, y_two, x_one = swap(z_two, "mp", 1), swap(z_two, "dp", 2), swap(z_one, "mp", 1)
    moved = [x_own, z_one] if stepwise else []
    *second, held = attend_rest(
        lo, nw, queries, keys_own, values_own, prefix_keys, prefix_vals, segc, segk, width, 1, moved
    ) + ((None,) if not moved else ())
    seen = [first, second]
    attended = [pair[0] for pair in seen]
    if stepwise:
        x_two, y_two, x_one, z_three, z_last, held, *attended = lax.optimization_barrier(
            (x_two, y_two, x_one, z_three, z_last, held, *attended)
        )
        x_three, y_three, yx_two = swap(z_three, "mp", 1), swap(z_three, "dp", 2), swap(x_two, "dp", 2)
        more = with_other([held, z_last])
        hat, inv, normed_low, total, slope, held = ffn_forward(
            attended, tokens, w_out, first_gain, [both], [z_two, x_two, y_two, x_one, z_three]
        )
        x_three, y_three, yx_two, held, more, normed_low, total = lax.optimization_barrier(
            (x_three, y_three, yx_two, held, more, normed_low, total)
        )
        yx_three, x_last = swap(x_three, "dp", 2), swap(z_last, "mp", 1)
        late = with_other([held, x_three, y_three])
        total, slope_more = ffn_more(normed_low, total, more)
        yx_three, x_last, yx_two, late, total = lax.optimization_barrier((yx_three, x_last, yx_two, late, total))
        early, slopes = [both] + more, [slope, slope_more]
        late = late + with_other([yx_two, x_last, yx_three])
    else:
        every = gather_plain(w_in, w_back)
        cut = every.shape[1] * 3 // 8
        early, late = [every[:, :cut]], [every[:, cut:]]
        hat, inv, normed_low, total, slope = ffn_forward(attended, tokens, w_out, first_gain, early, [])
        slopes = [slope]
    layer_output, grad_one, grad_att, delta, ds_prefix, dpk, dpv = middle(
        normed_low, inv, second_gain, first_gain, prefix_keys, prefix_vals,
        total, cotangent, hat, w_out, queries, seen, slopes, early, late,
    )
    logs = [lse for _, lse in seen]
    prefix_grad, input_grad = sum_everywhere(
        jnp.stack([dpk, dpv]),
        [
            lambda _: attend_back(
                lo, nw, queries, keys_own, values_own, grad_att, logs, delta, ds_prefix, prefix_keys, segc, segk
            ),
            lambda grads: project_back(grads, (w_query, w_key, w_value), grad_one),
        ],
    )
    new_first = beta_one * moment_one + (1.0 - beta_one) * prefix_grad
    new_second = beta_two * moment_two + (1.0 - beta_two) * prefix_grad * prefix_grad
    first_hat = new_first / (1.0 - beta_one**STEP)
    second_hat = new_second / (1.0 - beta_two**STEP)
    new_master = prefix_master * (1.0 - learn_rate * weight_decay) - learn_rate * first_hat / (
        jnp.sqrt(second_hat) + epsilon_adam
    )
    return (layer_output, input_grad, new_master, new_first, new_second, new_master.astype(bf16))


def solution(mesh):
    rows = P(("dp", "mp"), None)
    return jax.shard_map(
        on_device,
        mesh=mesh,
        in_specs=(rows, rows, P(), P(), P(), P(), P(), P(), P(None, "mp"), P("mp", None), P(), P(), P(), rows),
        out_specs=(rows, rows, P(), P(), P(), P()),
        check_vma=False,
    )
```

```python
import functools

import jax
import jax.numpy as jnp
from jax import lax
from jax.experimental import pallas as pl
from jax.experimental.pallas import tpu as pltpu
from jax.sharding import PartitionSpec as P

f32, bf16 = jnp.float32, jnp.bfloat16
STEP = 5
epsilon_norm = 1e-05
learn_rate = 1.0
weight_decay = 0.01
beta_one = 0.9
beta_two = 0.999
epsilon_adam = 1e-08
HEAD_SCALE = 0.125
NEG = -1e30
WIN = 256
KC = 64
QUAD = 256
LEAST, MOST = 1e-25, 1e30
ITEMS = 64
VMEM = 60 << 20
NN = (((1,), (0,)), ((), ()))
NT = (((1,), (1,)), ((), ()))
TN = (((0,), (0,)), ((), ()))


def dot(a, b, d=NN):
    return lax.dot_general(a, b, d, preferred_element_type=f32)


def vm():
    return pl.BlockSpec(memory_space=pltpu.VMEM)


def sm():
    return pl.BlockSpec(memory_space=pltpu.SMEM)


def hbm():
    return pl.BlockSpec(memory_space=pl.ANY)


def cost(flops, moved=8 << 20):
    return pl.CostEstimate(flops=4 * flops, bytes_accessed=moved, transcendentals=0)


def part_of(array, width, part):
    return pl.BlockSpec((array.shape[0], width), lambda i: (0, part))


def whole_of(array):
    return pl.BlockSpec(array.shape, lambda i: (0, 0))


def block_diag(piece):
    lane = lax.broadcasted_iota(jnp.int32, piece.shape, 1) // 64
    zero = jnp.zeros_like(piece)
    return jnp.concatenate([jnp.where(lane == h, piece, zero) for h in range(4)], axis=0)


def diag_of(full):
    lane = lax.broadcasted_iota(jnp.int32, (KC, 128), 1) < 64
    left = jnp.where(lane, full[0:64, 0:128], full[64:128, 0:128])
    right = jnp.where(lane, full[128:192, 128:256], full[192:256, 128:256])
    return jnp.concatenate([left, right], axis=1)


def head_ones():
    row = lax.broadcasted_iota(jnp.int32, (QUAD, QUAD), 0) // 64
    lane = lax.broadcasted_iota(jnp.int32, (QUAD, QUAD), 1) // 64
    return jnp.where(row == lane, 1.0, 0.0).astype(bf16)


def head_sum(x, ones):
    high = x.astype(bf16)
    return dot(high, ones) + dot((x - high.astype(f32)).astype(bf16), ones)


def head_max(x):
    lane = lax.broadcasted_iota(jnp.int32, x.shape, 1) < 64
    a = jnp.max(jnp.where(lane, x, NEG), axis=1, keepdims=True)
    b = jnp.max(jnp.where(lane, NEG, x), axis=1, keepdims=True)
    return jnp.where(lane, a, b)


def windows(seg):
    length = seg.shape[0]
    by = seg.reshape(length // KC, KC)
    first, last = by[:, 0], by[:, -1]
    lo = jnp.sum((seg[None, :] < first[:, None]).astype(jnp.int32), axis=1)
    hi = jnp.sum((seg[None, :] <= last[:, None]).astype(jnp.int32), axis=1)
    lo = lo // 16 * 16
    nw = (hi - lo + WIN - 1) // WIN
    segc = jnp.broadcast_to(seg[:, None], (length, 128))
    segk = jnp.concatenate([by, by], axis=1)
    return lo, nw, segc, segk


def list_items(lo_ref, nw_ref, chunk_ref, row_ref, length):
    def chunk(c, count):
        def one(w, count):
            chunk_ref[count] = c
            row_ref[count] = lo_ref[c] + w * WIN
            return count + 1

        return lax.fori_loop(0, nw_ref[c], one, count)

    count = lax.fori_loop(0, length // KC, chunk, 0)
    for n in range(2):
        chunk_ref[count + n] = 0
        row_ref[count + n] = length
    return count


def item_at(n, chunk_ref, row_ref, segc_ref, segk_ref, length):
    c, nominal = chunk_ref[n], row_ref[n]
    start = pl.multiple_of(jnp.minimum(nominal, length - WIN), 16)
    rows = pl.ds(start, WIN)
    keys = pl.ds(pl.multiple_of(c * KC, KC), KC)
    row_id = lax.broadcasted_iota(jnp.int32, (WIN, 128), 0) + start
    keep = jnp.logical_and(segc_ref[rows, :] == segk_ref[pl.ds(c, 1), :], row_id >= nominal)
    bias = jnp.where(keep, 0.0, NEG)
    return rows, keys, jnp.concatenate([bias, bias], axis=1)


def staged(units, first, second, third):
    raw, done = first(units[0]), None
    for n in range(len(units) + 1):
        upcoming = first(units[n + 1]) if n + 1 < len(units) else None
        fresh = second(units[n], raw) if n < len(units) else None
        if done is not None:
            third(units[n - 1], done)
        raw, done = upcoming, fresh


def join_copies(pieces, buffer, target, sems):
    copies, row = [], 0
    for n, piece in enumerate(pieces):
        rows = piece.shape[1]
        copies.append(pltpu.make_async_copy(piece, buffer.at[:, row : row + rows], sems.at[n]))
        row += rows
    return copies, [pltpu.make_async_copy(buffer, target, sems.at[len(pieces)])]


def begin(copies):
    for copy in copies:
        copy.start()


def finish(copies):
    for copy in copies:
        copy.wait()


def joined_shape(pieces):
    planes, _, lanes = pieces[0].shape
    return jax.ShapeDtypeStruct((planes, sum(piece.shape[1] for piece in pieces), lanes), pieces[0].dtype)


def attend_columns(count, q_ref, k_ref, v_ref, pk_ref, pv_ref, att_ref, lse_ref, l_ref, acc_ref, item):
    length, width = att_ref.shape
    parts = [slice(c, c + QUAD) for c in range(0, width, QUAD)]
    spans = [slice(r, r + WIN) for r in range(0, length, WIN)]
    ids = range(len(parts))
    ones = head_ones()
    bdk = [block_diag(pk_ref[:, cols]) for cols in parts]
    bdv = [block_diag(pv_ref[:, cols]) for cols in parts]

    def start_third(unit, p):
        rows, g = unit
        l_ref[rows, parts[g]] = p
        acc_ref[rows, parts[g]] = dot(p.astype(bf16), bdv[g])

    staged(
        [(rows, g) for g in ids for rows in spans],
        lambda u: dot(q_ref[u[0], parts[u[1]]], bdk[u[1]], NT),
        lambda u, s: jnp.exp(s),
        start_third,
    )

    @pl.loop(0, (count + 1) // 2)
    def _(n):
        def third(unit, p):
            (rows, keys, _), g = unit
            l_ref[rows, parts[g]] += p
            acc_ref[rows, parts[g]] += dot(p.astype(bf16), block_diag(v_ref[keys, parts[g]]))

        staged(
            [(one, g) for one in (item(2 * n), item(2 * n + 1)) for g in ids],
            lambda u: dot(q_ref[u[0][0], parts[u[1]]], block_diag(k_ref[u[0][1], parts[u[1]]]), NT),
            lambda u, s: jnp.exp(s + u[0][2]),
            third,
        )

    least, most = [], []
    for rows in spans:
        for cols in parts:
            total = head_sum(l_ref[rows, cols], ones)
            att_ref[rows, cols] = (acc_ref[rows, cols] / total).astype(bf16)
            lse_ref[rows, cols] = jnp.log(total)
            least.append(jnp.min(total, axis=0, keepdims=True))
            most.append(jnp.max(total, axis=0, keepdims=True))
    return functools.reduce(jnp.minimum, least), functools.reduce(jnp.maximum, most)


def attend_again_kernel(
    redo_ref, lo_ref, nw_ref, pk_ref, pv_ref, segc_ref, segk_ref, q_hbm, k_hbm, v_hbm, _a, _b, _c, _d,
    att_one, lse_one, att_two, lse_two,
    q_ref, k_ref, v_ref, part_pk, part_pv, att_ref, lse_ref, l_ref, acc_ref, chunk_ref, row_ref, sems,
):
    @pl.when(redo_ref[0] > 0)
    def _():
        length, width = att_ref.shape
        count = list_items(lo_ref, nw_ref, chunk_ref, row_ref, length)

        def item(n):
            return item_at(n, chunk_ref, row_ref, segc_ref, segk_ref, length)

        for part, (att_hbm, lse_hbm) in enumerate(((att_one, lse_one), (att_two, lse_two))):
            cols = slice(part * width, (part + 1) * width)
            loads = [
                pltpu.make_async_copy(a.at[:, cols], b, sems.at[n])
                for n, (a, b) in enumerate(((q_hbm, q_ref), (k_hbm, k_ref), (v_hbm, v_ref)))
            ]
            begin(loads)
            part_pk[...] = pk_ref[:, cols]
            part_pv[...] = pv_ref[:, cols]
            finish(loads)
            quads, tiles = width // QUAD, length // WIN

            def block(n):
                rows = pl.ds(pl.multiple_of(n // quads * WIN, WIN), WIN)
                return rows, pl.ds(pl.multiple_of(n % quads * QUAD, QUAD), QUAD)

            def entry(n):
                rows, keys, bias = item(n // quads)
                return rows, keys, bias, pl.ds(pl.multiple_of(n % quads * QUAD, QUAD), QUAD)

            @pl.loop(0, quads * tiles)
            def _(n):
                rows, quad = block(n)
                lse_ref[rows, quad] = dot(q_ref[rows, quad], block_diag(part_pk[:, quad]), NT)

            @pl.loop(0, quads * count)
            def _(n):
                rows, keys, bias, quad = entry(n)
                s = dot(q_ref[rows, quad], block_diag(k_ref[keys, quad]), NT) + bias
                lse_ref[rows, quad] = jnp.maximum(lse_ref[rows, quad], s)

            @pl.loop(0, 2 * quads * (length // KC))
            def _(n):
                rows = pl.ds(pl.multiple_of(n // (2 * quads) * KC, KC), KC)
                pair = pl.ds(pl.multiple_of(n % (2 * quads) * 128, 128), 128)
                lse_ref[rows, pair] = head_max(lse_ref[rows, pair])

            @pl.loop(0, quads * tiles)
            def _(n):
                rows, quad = block(n)
                p = jnp.exp(dot(q_ref[rows, quad], block_diag(part_pk[:, quad]), NT) - lse_ref[rows, quad])
                l_ref[rows, quad] = p
                acc_ref[rows, quad] = dot(p.astype(bf16), block_diag(part_pv[:, quad]))

            @pl.loop(0, quads * count)
            def _(n):
                rows, keys, bias, quad = entry(n)
                s = dot(q_ref[rows, quad], block_diag(k_ref[keys, quad]), NT)
                p = jnp.exp(s - lse_ref[rows, quad] + bias)
                l_ref[rows, quad] += p
                acc_ref[rows, quad] += dot(p.astype(bf16), block_diag(v_ref[keys, quad]))

            @pl.loop(0, quads * tiles)
            def _(n):
                rows, quad = block(n)
                total = head_sum(l_ref[rows, quad], head_ones())
                att_ref[rows, quad] = (acc_ref[rows, quad] / total).astype(bf16)
                lse_ref[rows, quad] += jnp.log(total)

            stores = [
                pltpu.make_async_copy(a, b, sems.at[n]) for n, (a, b) in enumerate(((att_ref, att_hbm), (lse_ref, lse_hbm)))
            ]
            begin(stores)
            finish(stores)


def attend_again(redo, lo, nw, pk, pv, segc, segk, q, k, v, first, second):
    length, width = first[0].shape
    slots = pk.shape[0]
    held = (*first, *second)
    return pl.pallas_call(
        attend_again_kernel,
        out_shape=tuple(jax.ShapeDtypeStruct(a.shape, a.dtype) for a in held),
        in_specs=[sm()] * 3 + [vm()] * 4 + [hbm()] * 7,
        out_specs=(hbm(),) * 4,
        input_output_aliases={10 + n: n for n in range(4)},
        scratch_shapes=[pltpu.VMEM((length, width), bf16)] * 3
        + [pltpu.VMEM((slots, width), bf16)] * 2
        + [pltpu.VMEM((length, width), t) for t in (bf16, f32, f32, f32)]
        + [pltpu.SMEM((ITEMS,), jnp.int32)] * 2
        + [pltpu.SemaphoreType.DMA((3,))],
        compiler_params=pltpu.CompilerParams(vmem_limit_bytes=VMEM),
        cost_estimate=cost(1 << 20, 1 << 20),
        name="attend_again",
    )(redo, lo, nw, pk, pv, segc, segk, q, k, v, *held)


def attend_first_kernel(
    lo_ref, nw_ref, x_ref, wq_hbm, wk_hbm, wv_hbm, pk_ref, pv_ref, segc_ref, segk_ref,
    q_hbm, k_hbm, v_hbm, att_ref, lse_ref, least_ref, most_ref,
    w_ref, q_ref, k_ref, v_ref, l_ref, acc_ref, chunk_ref, row_ref, in_sems, out_sems,
):
    length, lanes = x_ref.shape
    loads = [pltpu.make_async_copy(w, w_ref.at[n], in_sems.at[n]) for n, w in enumerate((wq_hbm, wk_hbm, wv_hbm))]
    stores = [
        pltpu.make_async_copy(a, b, out_sems.at[n])
        for n, (a, b) in enumerate(((q_ref, q_hbm), (k_ref, k_hbm), (v_ref, v_hbm)))
    ]
    for load in loads:
        load.start()
    count = list_items(lo_ref, nw_ref, chunk_ref, row_ref, length)
    for n, out_ref in enumerate((q_ref, k_ref, v_ref)):
        loads[n].wait()
        for c in range(0, lanes, QUAD):
            value = dot(x_ref[...], w_ref[n, :, c : c + QUAD])
            out_ref[:, c : c + QUAD] = (value * HEAD_SCALE if n == 0 else value).astype(bf16)
        stores[n].start()

    def item(n):
        return item_at(n, chunk_ref, row_ref, segc_ref, segk_ref, length)

    least_ref[...], most_ref[...] = attend_columns(
        count, q_ref, k_ref, v_ref, pk_ref, pv_ref, att_ref, lse_ref, l_ref, acc_ref, item
    )
    for store in stores:
        store.wait()


def attend_rest_kernel(*refs, count):
    lo_ref, nw_ref, q_ref, k_ref, v_ref, pk_ref, pv_ref, segc_ref, segk_ref = refs[:9]
    pieces, refs = refs[9 : 9 + count], refs[9 + count :]
    att_ref, lse_ref, least_ref, most_ref, *refs = refs
    arrive, leave = [], []
    if count:
        target, *refs, held, sems = refs
        arrive, leave = join_copies(pieces, held, target, sems)
    l_ref, acc_ref, chunk_ref, row_ref = refs
    begin(arrive)
    length = q_ref.shape[0]
    items = list_items(lo_ref, nw_ref, chunk_ref, row_ref, length)
    finish(arrive)
    begin(leave)

    def item(n):
        return item_at(n, chunk_ref, row_ref, segc_ref, segk_ref, length)

    least_ref[...], most_ref[...] = attend_columns(
        items, q_ref, k_ref, v_ref, pk_ref, pv_ref, att_ref, lse_ref, l_ref, acc_ref, item
    )
    finish(leave)


def attended_shapes(length, width):
    shape, lane = (length, width), jax.ShapeDtypeStruct((1, QUAD), f32)
    return [jax.ShapeDtypeStruct(shape, bf16), jax.ShapeDtypeStruct(shape, f32), lane, lane]


def attend_first(lo, nw, x, wq, wk, wv, pk, pv, segc, segk, width):
    length, lanes = x.shape
    low = jax.ShapeDtypeStruct((length, lanes), bf16)
    return pl.pallas_call(
        attend_first_kernel,
        out_shape=(low, low, low, *attended_shapes(length, width)),
        in_specs=[sm(), sm(), vm(), hbm(), hbm(), hbm(), vm(), vm(), vm(), vm()],
        out_specs=(hbm(), hbm(), hbm(), vm(), vm(), vm(), vm()),
        scratch_shapes=[pltpu.VMEM((3, lanes, lanes), bf16)]
        + [pltpu.VMEM((length, lanes), bf16)] * 3
        + [pltpu.VMEM((length, width), f32)] * 2
        + [pltpu.SMEM((ITEMS,), jnp.int32)] * 2
        + [pltpu.SemaphoreType.DMA((3,))] * 2,
        compiler_params=pltpu.CompilerParams(vmem_limit_bytes=VMEM),
        cost_estimate=cost(16 * length * lanes * lanes),
        name="attend_first",
    )(lo, nw, x, wq, wk, wv, pk, pv, segc, segk)


def attend_rest(lo, nw, q, k, v, pk, pv, segc, segk, width, part, pieces):
    length = q.shape[0]
    outs = attended_shapes(length, width)
    specs = [whole_of(each) for each in outs]
    scratch = [pltpu.VMEM((length, width), f32)] * 2 + [pltpu.SMEM((ITEMS,), jnp.int32)] * 2
    if pieces:
        held = joined_shape(pieces)
        outs.append(held)
        specs.append(hbm())
        scratch += [pltpu.VMEM(held.shape, held.dtype), pltpu.SemaphoreType.DMA((len(pieces) + 1,))]
    return pl.pallas_call(
        functools.partial(attend_rest_kernel, count=len(pieces)),
        grid=(1,),
        out_shape=tuple(outs),
        in_specs=[sm(), sm()]
        + [part_of(a, width, part) for a in (q, k, v, pk, pv)]
        + [whole_of(segc), whole_of(segk)]
        + [hbm()] * len(pieces),
        out_specs=tuple(specs),
        scratch_shapes=scratch,
        compiler_params=pltpu.CompilerParams(vmem_limit_bytes=VMEM),
        cost_estimate=cost(16000 * length * width),
        name="attend_rest",
    )(lo, nw, q, k, v, pk, pv, segc, segk, *pieces)


def attend_back_kernel(*refs, halves):
    lo_ref, nw_ref, pk_ref, segc_ref, segk_ref = refs[:5]
    sources, refs = refs[5 : 11 + halves], refs[11 + halves :]
    (
        dq_hbm, dk_hbm, dv_hbm,
        q_ref, k_ref, v_ref, g_ref, delta_ref, ds_ref, lse_ref,
        dq_acc, dk_acc, dv_acc, dq_ref, dk_ref, dv_ref, chunk_ref, row_ref, in_sems, out_sems,
    ) = refs
    length, lanes = q_ref.shape
    parts = [slice(g * QUAD, (g + 1) * QUAD) for g in range(lanes // QUAD)]
    spans = [slice(r * WIN, (r + 1) * WIN) for r in range(length // WIN)]
    places = [ds_ref, q_ref, k_ref, v_ref, g_ref, delta_ref]
    for n in range(halves):
        places.append(lse_ref.at[:, n * (lanes // halves) : (n + 1) * (lanes // halves)])
    loads = [pltpu.make_async_copy(a, b, in_sems.at[n]) for n, (a, b) in enumerate(zip(sources, places))]
    for load in loads:
        load.start()
    count = list_items(lo_ref, nw_ref, chunk_ref, row_ref, length)
    dk_acc[...] = jnp.zeros_like(dk_acc)
    dv_acc[...] = jnp.zeros_like(dv_acc)
    loads[0].wait()
    for cols in parts:
        bdk = block_diag(pk_ref[:, cols])
        for rows in spans:
            dq_acc[rows, cols] = dot(ds_ref[rows, cols], bdk)
    for load in loads[1:]:
        load.wait()
    ids = range(len(parts))

    @pl.loop(0, (count + 1) // 2)
    def _(n):
        def first(unit):
            (rows, keys, _), g = unit
            cols = parts[g]
            s = dot(q_ref[rows, cols], block_diag(k_ref[keys, cols]), NT)
            return s, dot(g_ref[rows, cols], block_diag(v_ref[keys, cols]), NT)

        def second(unit, pair):
            (rows, _, bias), g = unit
            cols = parts[g]
            p = jnp.exp(pair[0] + bias - lse_ref[rows, cols])
            return p.astype(bf16), (p * (pair[1] - delta_ref[rows, cols])).astype(bf16)

        def third(unit, pair):
            (rows, keys, _), g = unit
            cols = parts[g]
            dv_acc[keys, cols] += diag_of(dot(pair[0], g_ref[rows, cols], TN))
            dk_acc[keys, cols] += diag_of(dot(pair[1], q_ref[rows, cols], TN))
            dq_acc[rows, cols] += dot(pair[1], block_diag(k_ref[keys, cols]))

        items = [item_at(2 * n + i, chunk_ref, row_ref, segc_ref, segk_ref, length) for i in range(2)]
        staged([(one, g) for one in items for g in ids], first, second, third)

    stores = []
    ends = ((dq_acc, dq_ref, dq_hbm, HEAD_SCALE), (dk_acc, dk_ref, dk_hbm, 1.0), (dv_acc, dv_ref, dv_hbm, 1.0))
    for n, (acc, low, target, scale) in enumerate(ends):
        low[...] = (acc[...] * scale).astype(bf16)
        stores.append(pltpu.make_async_copy(low, target, out_sems.at[n]))
        stores[n].start()
    for store in stores:
        store.wait()


def attend_back(lo, nw, q, k, v, g, lse, delta, ds, pk, segc, segk):
    length, lanes = q.shape
    tall = (length, lanes)
    return pl.pallas_call(
        functools.partial(attend_back_kernel, halves=len(lse)),
        out_shape=(jax.ShapeDtypeStruct(tall, bf16),) * 3,
        in_specs=[sm(), sm(), vm(), vm(), vm()] + [hbm()] * (6 + len(lse)),
        out_specs=(hbm(),) * 3,
        scratch_shapes=[pltpu.VMEM(tall, t) for t in (bf16, bf16, bf16, bf16, f32, bf16, f32)]
        + [pltpu.VMEM(tall, f32)] * 3
        + [pltpu.VMEM(tall, bf16)] * 3
        + [pltpu.SMEM((ITEMS,), jnp.int32)] * 2
        + [pltpu.SemaphoreType.DMA((6 + len(lse),)), pltpu.SemaphoreType.DMA((3,))],
        compiler_params=pltpu.CompilerParams(vmem_limit_bytes=VMEM),
        cost_estimate=cost(length * lanes * 30000),
        name="attend_back",
    )(lo, nw, pk, segc, segk, ds, q, k, v, g, delta, *lse)


HID = 512


def mean_of(x):
    return jnp.mean(x, axis=-1, keepdims=True)


def centre(x):
    centred = x - mean_of(x)
    inv = lax.rsqrt(mean_of(centred * centred) + epsilon_norm)
    return centred * inv, inv


def pull_norm(pull, hat, inv):
    return inv * (pull - mean_of(pull) - hat * mean_of(pull * hat))


def gelu_pair(x):
    phi = 0.5 + 0.5 * lax.erf(x * 0.7071067811865476)
    bell = 0.3989422804014327 * jnp.exp(-0.5 * (x * x))
    return x * phi, phi + x * bell


def blocks_of(pieces):
    blocks, block, room = [], [], HID
    for piece in pieces:
        row = 0
        while row < piece.shape[1]:
            rows = min(room, piece.shape[1] - row)
            block.append((piece, row, rows))
            row, room = row + rows, room - rows
            if room == 0:
                blocks.append(block)
                block, room = [], HID
    return blocks


def most_of(pieces):
    return max(len(block) for block in blocks_of(pieces))


def block_copies(block, buffer, sems, slot):
    copies, place = [], 0
    for n, (piece, row, rows) in enumerate(block):
        source = piece.at[:, row : row + rows]
        copies.append(pltpu.make_async_copy(source, buffer.at[slot, :, place : place + rows], sems.at[slot, n]))
        place += rows
    return copies


def forward_block(low_ref, weights, sum_ref, slope_ref, cols):
    def second(rows, x):
        act, slope = gelu_pair(x)
        slope_ref[rows, cols] = slope.astype(bf16)
        return act.astype(bf16)

    def third(rows, act):
        sum_ref[rows, :] += dot(act, weights[1])

    spans = [slice(r, r + WIN) for r in range(0, low_ref.shape[0], WIN)]
    staged(spans, lambda rows: dot(low_ref[rows, :], weights[0], NT), second, third)


def ffn_kernel(*refs, halves, count, others):
    atts, (tok_ref, w_out_ref, gain_ref), refs = refs[:halves], refs[halves : halves + 3], refs[halves + 3 :]
    blocks, pieces, refs = blocks_of(refs[:count]), refs[count : count + others], refs[count + others :]
    hat_ref, inv_ref, low_ref, sum_ref, slope_ref, *refs = refs
    arrive, leave = [], []
    if others:
        target, *refs, held, join_sems = refs
        arrive, leave = join_copies(pieces, held, target, join_sems)
    buffer, sems = refs
    width = atts[0].shape[1]
    copies = [block_copies(block, buffer, sems, b % 2) for b, block in enumerate(blocks)]
    begin(copies[0])
    begin(arrive)

    def second(rows, x):
        hat, inv = centre(tok_ref[rows, :].astype(f32) + x)
        hat_ref[rows, :] = hat
        inv_ref[rows, :] = jnp.broadcast_to(inv, (WIN, 128))
        normed = gain_ref[...] * hat
        sum_ref[rows, :] = normed
        low_ref[rows, :] = normed.astype(bf16)

    def first(rows):
        return sum(dot(att_ref[rows, :], w_out_ref[n * width : (n + 1) * width, :]) for n, att_ref in enumerate(atts))

    spans = [slice(r, r + WIN) for r in range(0, tok_ref.shape[0], WIN)]
    staged(spans, first, second, lambda rows, x: None)
    finish(arrive)
    begin(leave)
    for b in range(len(blocks)):
        if b + 1 < len(blocks):
            begin(copies[b + 1])
        finish(copies[b])
        forward_block(low_ref, buffer.at[b % 2], sum_ref, slope_ref, slice(b * HID, (b + 1) * HID))
    finish(leave)


def ffn_forward(att, tokens, w_out, gain, pieces, others):
    length, lanes = tokens.shape
    hidden = sum(piece.shape[1] for piece in pieces)
    wide = jax.ShapeDtypeStruct((length, lanes), f32)
    outs = [
        wide,
        jax.ShapeDtypeStruct((length, 128), f32),
        jax.ShapeDtypeStruct((length, lanes), bf16),
        wide,
        jax.ShapeDtypeStruct((length, hidden), bf16),
    ]
    specs = [vm()] * 5
    scratch = [pltpu.VMEM((2, 2, HID, lanes), bf16), pltpu.SemaphoreType.DMA((2, most_of(pieces)))]
    if others:
        held = joined_shape(others)
        outs.append(held)
        specs.append(hbm())
        scratch += [pltpu.VMEM(held.shape, held.dtype), pltpu.SemaphoreType.DMA((len(others) + 1,))]
    return pl.pallas_call(
        functools.partial(ffn_kernel, halves=len(att), count=len(pieces), others=len(others)),
        out_shape=tuple(outs),
        in_specs=[vm()] * (len(att) + 3) + [hbm()] * (len(pieces) + len(others)),
        out_specs=tuple(specs),
        scratch_shapes=scratch,
        compiler_params=pltpu.CompilerParams(vmem_limit_bytes=VMEM),
        cost_estimate=cost(4 * length * lanes * (hidden + lanes)),
        name="ffn_forward",
    )(*att, tokens, w_out, gain, *pieces, *others)


def more_kernel(low_ref, start_ref, *refs, count):
    blocks = blocks_of(refs[:count])
    sum_ref, slope_ref, buffer, sems = refs[count:]
    copies = [block_copies(block, buffer, sems, b % 2) for b, block in enumerate(blocks)]
    begin(copies[0])
    sum_ref[...] = start_ref[...]
    for b in range(len(blocks)):
        if b + 1 < len(blocks):
            begin(copies[b + 1])
        finish(copies[b])
        forward_block(low_ref, buffer.at[b % 2], sum_ref, slope_ref, slice(b * HID, (b + 1) * HID))


def ffn_more(low, start, pieces):
    length, lanes = low.shape
    hidden = sum(piece.shape[1] for piece in pieces)
    return pl.pallas_call(
        functools.partial(more_kernel, count=len(pieces)),
        out_shape=(jax.ShapeDtypeStruct((length, lanes), f32), jax.ShapeDtypeStruct((length, hidden), bf16)),
        in_specs=[vm()] * 2 + [hbm()] * len(pieces),
        out_specs=(vm(),) * 2,
        scratch_shapes=[pltpu.VMEM((2, 2, HID, lanes), bf16), pltpu.SemaphoreType.DMA((2, most_of(pieces)))],
        compiler_params=pltpu.CompilerParams(vmem_limit_bytes=VMEM),
        cost_estimate=cost(4 * length * lanes * hidden),
        name="ffn_more",
    )(low, start, *pieces)


def middle_kernel(*refs, halves, early, late, groups):
    low_ref, inv_ref, gain_two_ref, gain_one_ref, pk_ref, pv_ref = refs[:6]
    sum_hbm, cot_hbm, hat_hbm, w_out_hbm, q_hbm = refs[6:11]
    seen, refs = refs[11 : 11 + 2 * halves], refs[11 + 2 * halves :]
    slopes, pieces, refs = refs[:groups], refs[groups : groups + early + late], refs[groups + early + late :]
    (layer_hbm, one_hbm, g_hbm, delta_hbm, ds_hbm, dpk_ref, dpv_ref) = refs[:7]
    (
        acc_ref, cot_ref, hat_ref, w_out_ref, q_ref, att_ref, lse_ref, layer_ref, one_ref, g_ref, delta_ref, ds_ref,
        grad_ref, late_ref, buffer, sbuf, sems, ssems, in_sems, out_sems,
    ) = refs[7:]
    length, lanes = low_ref.shape
    spans = [slice(r, r + WIN) for r in range(0, length, WIN)]
    parts = [slice(c, c + QUAD) for c in range(0, lanes, QUAD)]
    first_blocks, last_blocks = blocks_of(pieces[:early]), blocks_of(pieces[early:])
    order = last_blocks + first_blocks + last_blocks
    copies = [block_copies(block, buffer, sems, n % 2) for n, block in enumerate(order)]
    skip = len(last_blocks)
    slabs = [slope.at[:, c : c + HID] for slope in slopes for c in range(0, slope.shape[1], HID)]
    for n, source in enumerate(slabs, skip):
        copies[n].append(pltpu.make_async_copy(source, sbuf.at[n % 2], ssems.at[n % 2]))
    sources = (sum_hbm, cot_hbm, hat_hbm, w_out_hbm, q_hbm, *seen)
    places = [acc_ref, cot_ref, hat_ref, w_out_ref, q_ref]
    for n in range(halves):
        cols = slice(n * (lanes // halves), (n + 1) * (lanes // halves))
        places += [att_ref.at[:, cols], lse_ref.at[:, cols]]
    loads = [pltpu.make_async_copy(a, b, in_sems.at[n]) for n, (a, b) in enumerate(zip(sources, places))]
    results = (layer_ref, one_ref, g_ref, delta_ref, ds_ref)
    targets = (layer_hbm, one_hbm, g_hbm, delta_hbm, ds_hbm)
    stores = [pltpu.make_async_copy(a, b, out_sems.at[n]) for n, (a, b) in enumerate(zip(results, targets))]
    begin(copies[0])
    begin(loads[:1])

    def enter(n):
        if n + 1 < len(order):
            begin(copies[n + 1])
        if n == 0:
            finish(loads[:1])
            begin(loads[1:])
        finish(copies[n])
        return buffer.at[n % 2]

    for n in range(skip):
        forward_block(low_ref, enter(n), acc_ref, late_ref, slice(n * HID, (n + 1) * HID))

    finish(loads[1:3])
    for n in range(skip, len(order)):
        weights = enter(n)
        past = n - skip - len(first_blocks)

        def first(rows):
            if n == skip:
                hat, inv = centre(acc_ref[rows, :])
                layer_ref[rows, :] = (gain_two_ref[...] * hat).astype(bf16)
                grad = pull_norm(cot_ref[rows, :].astype(f32) * gain_two_ref[...], hat, inv)
                acc_ref[rows, :] = grad
                grad_ref[rows, :] = grad.astype(bf16)
            return dot(grad_ref[rows, :], weights[1], NT)

        def second(rows, x):
            slope = sbuf[n % 2, rows, :] if past < 0 else late_ref[rows, past * HID : (past + 1) * HID]
            return (x * slope.astype(f32)).astype(bf16)

        def third(rows, x):
            acc_ref[rows, :] += dot(x, weights[0])

        staged(spans, first, second, third)
        if n == skip:
            begin(stores[:1])
    finish(loads[3:])

    def first(rows):
        grad = pull_norm(acc_ref[rows, :] * gain_one_ref[...], hat_ref[rows, :], inv_ref[rows, 0:1])
        one_ref[rows, :] = grad
        return grad.astype(bf16)

    def second(rows, grad):
        g_ref[rows, :] = dot(grad, w_out_ref[...], NT).astype(bf16)

    staged(spans, first, second, lambda rows, x: None)
    begin(stores[1:3])

    ones = head_ones()
    sums = {}

    def first(unit):
        g, rows = unit
        cols = parts[g]
        up = g_ref[rows, cols]
        delta = head_sum(up.astype(f32) * att_ref[rows, cols].astype(f32), ones)
        return dot(q_ref[rows, cols], block_diag(pk_ref[:, cols]), NT), dot(up, block_diag(pv_ref[:, cols]), NT), delta

    def second(unit, three):
        g, rows = unit
        cols = parts[g]
        delta_ref[rows, cols] = three[2]
        p = jnp.exp(three[0] - lse_ref[rows, cols])
        ds = (p * (three[1] - three[2])).astype(bf16)
        ds_ref[rows, cols] = ds
        return p.astype(bf16), ds

    def third(unit, pair):
        g, rows = unit
        cols = parts[g]
        dpv, dpk = diag_of(dot(pair[0], g_ref[rows, cols], TN)), diag_of(dot(pair[1], q_ref[rows, cols], TN))
        if rows.start:
            dpv, dpk = sums[g][0] + dpv, sums[g][1] + dpk
        sums[g] = (dpv, dpk)
        if rows.stop == length:
            dpv_ref[:, cols], dpk_ref[:, cols] = dpv, dpk

    staged([(g, rows) for g in range(len(parts)) for rows in spans], first, second, third)
    begin(stores[3:])
    finish(stores)


def middle(low, inv, gain_two, gain_one, pk, pv, total, cot, hat, w_out, q, seen, slopes, early, late):
    length, lanes = low.shape
    slots = pk.shape[0]
    late_units = sum(piece.shape[1] for piece in late)
    flat = [each for pair in seen for each in pair]
    tall = (length, lanes)
    small = jax.ShapeDtypeStruct((slots, lanes), f32)
    holds = [f32, bf16, f32, None, bf16, bf16, f32, bf16, f32, bf16, f32, bf16, bf16]
    return pl.pallas_call(
        functools.partial(middle_kernel, halves=len(seen), early=len(early), late=len(late), groups=len(slopes)),
        out_shape=tuple(jax.ShapeDtypeStruct(tall, t) for t in (bf16, f32, bf16, f32, bf16)) + (small, small),
        in_specs=[vm()] * 6 + [hbm()] * (5 + 2 * len(seen) + len(slopes) + len(early) + len(late)),
        out_specs=(hbm(),) * 5 + (vm(), vm()),
        scratch_shapes=[pltpu.VMEM((lanes, lanes), bf16) if t is None else pltpu.VMEM(tall, t) for t in holds]
        + [
            pltpu.VMEM((length, late_units), bf16),
            pltpu.VMEM((2, 2, HID, lanes), bf16),
            pltpu.VMEM((2, length, HID), bf16),
            pltpu.SemaphoreType.DMA((2, most_of(early + late))),
            pltpu.SemaphoreType.DMA((2,)),
            pltpu.SemaphoreType.DMA((5 + len(flat),)),
            pltpu.SemaphoreType.DMA((5,)),
        ],
        compiler_params=pltpu.CompilerParams(vmem_limit_bytes=VMEM),
        cost_estimate=cost(40 * length * lanes * lanes),
        name="middle",
    )(low, inv, gain_two, gain_one, pk, pv, total, cot, hat, w_out, q, *flat, *slopes, *early, *late)


def project_kernel(dq_hbm, dk_hbm, dv_hbm, wq_hbm, wk_hbm, wv_hbm, one_hbm, out_hbm, grads, weights, out_ref, *sems):
    length, lanes = out_ref.shape
    spans = [slice(r, r + WIN) for r in range(0, length, WIN)]
    grad_sems, weight_sems, one_sem, out_sems = sems
    loads = []
    for n, (grad, weight) in enumerate(((dq_hbm, wq_hbm), (dk_hbm, wk_hbm), (dv_hbm, wv_hbm))):
        loads.append(
            (
                pltpu.make_async_copy(grad, grads.at[n], grad_sems.at[n]),
                pltpu.make_async_copy(weight, weights.at[n], weight_sems.at[n]),
            )
        )
        begin(loads[n])
        if n == 0:
            one = pltpu.make_async_copy(one_hbm, out_ref, one_sem.at[0])
            one.start()
    stores = [
        pltpu.make_async_copy(out_ref.at[rows, :], out_hbm.at[rows, :], out_sems.at[r]) for r, rows in enumerate(spans)
    ]
    finish(loads[0])
    first = [dot(grads[0, rows, :], weights[0], NT) for rows in spans[:1]]
    one.wait()
    out_ref[spans[0], :] += first[0]
    for rows in spans[1:]:
        out_ref[rows, :] += dot(grads[0, rows, :], weights[0], NT)
    finish(loads[1])
    finish(loads[2])
    for r, rows in enumerate(spans):
        more = dot(grads[1, rows, :], weights[1], NT) + dot(grads[2, rows, :], weights[2], NT)
        out_ref[rows, :] += more
        stores[r].start()
    finish(stores)


def project_back(grads, weights, grad_one):
    length, lanes = grad_one.shape
    return pl.pallas_call(
        project_kernel,
        out_shape=jax.ShapeDtypeStruct((length, lanes), f32),
        in_specs=[hbm()] * 7,
        out_specs=hbm(),
        scratch_shapes=[
            pltpu.VMEM((3, length, lanes), bf16),
            pltpu.VMEM((3, lanes, lanes), bf16),
            pltpu.VMEM((length, lanes), f32),
            pltpu.SemaphoreType.DMA((3,)),
            pltpu.SemaphoreType.DMA((3,)),
            pltpu.SemaphoreType.DMA((1,)),
            pltpu.SemaphoreType.DMA((length // WIN,)),
        ],
        compiler_params=pltpu.CompilerParams(vmem_limit_bytes=VMEM),
        cost_estimate=cost(6 * length * lanes * lanes),
        name="project_back",
    )(*grads, *weights, grad_one)


def swap(x, axis, bit):
    return lax.ppermute(x, axis, [(i, i ^ bit) for i in range(lax.axis_size(axis))])


def swap_two(x, one, two):
    if one[0] == two[0]:
        return swap(x, one[0], one[1] | two[1])
    wide = {"dp": lax.axis_size("mp"), "mp": 1}
    mask = one[1] * wide[one[0]] + two[1] * wide[two[0]]
    count = lax.axis_size("dp") * lax.axis_size("mp")
    return lax.ppermute(x, ("dp", "mp"), [(i, i ^ mask) for i in range(count)])


def gather_plain(w_in, w_back):
    both = jnp.stack([w_in.T, w_back])
    part = both.shape[1] // lax.axis_size("dp")
    mine = lax.dynamic_slice_in_dim(both, lax.axis_index("dp") * part, part, 1)
    return lax.all_gather(mine, ("dp", "mp"), axis=1, tiled=True)


def own_weights(w_in, w_back):
    both = jnp.stack([w_in.T, w_back])
    half = both.shape[1] // 2
    dp = lax.axis_index("dp")
    own = lax.dynamic_slice_in_dim(both, lax.rem(dp, 2) * half, half, 1)
    unit = half // 2
    mine = lax.dynamic_slice_in_dim(own, dp // 2 * unit, unit, 1)
    rest = lax.dynamic_slice_in_dim(own, (1 - dp // 2) * unit, unit, 1)
    return both, own, mine, rest


def with_other(pieces):
    return [each for piece in pieces for each in (piece, swap(piece, "dp", 1))]


def sum_everywhere(x, between):
    core = lax.rem(lax.axis_index("dp"), 2)
    half = x.shape[0] // 2
    keep = lax.dynamic_slice_in_dim(x, core * half, half, 0)
    give = lax.dynamic_slice_in_dim(x, (1 - core) * half, half, 0)
    part = keep + swap(give, "dp", 1)
    bits = [(axis, 1 << n) for axis in ("dp", "mp") for n in range(lax.axis_size(axis).bit_length() - 1)][1:]
    bits = sorted(bits, key=lambda pair: pair[1] if pair[0] == "mp" else 1)
    done = None
    for n in range(0, len(bits), 2):
        low = part.astype(bf16)
        pairs = bits[n : n + 2]
        came = [swap(low, *pair) for pair in pairs]
        if len(pairs) == 2:
            came.append(swap_two(low, *pairs))
        if between:
            done = between.pop(0)(done)
            came, done = lax.optimization_barrier((came, done))
        part = low.astype(f32) + came[0].astype(f32)
        if len(pairs) == 2:
            part = part + (came[1].astype(f32) + came[2].astype(f32))
    while between:
        done = between.pop(0)(done)
    other = swap(part, "dp", 1)
    return jnp.where(core == 0, jnp.concatenate([part, other]), jnp.concatenate([other, part])), done


def on_device(
    tokens, segment_ids, w_query, w_key, w_value, w_out, gain_one, gain_two, w_in, w_back,
    prefix_master, moment_one, moment_two, cotangent,
):
    stepwise = lax.axis_size("dp") == 4 and lax.axis_size("mp") == 8
    prefix_low = prefix_master.astype(bf16)
    prefix_keys, prefix_vals = prefix_low[0], prefix_low[1]
    first_gain, second_gain = gain_one[None, :], gain_two[None, :]
    lo, nw, segc, segk = windows(segment_ids[0])
    halves = 2
    width = tokens.shape[1] // halves
    if stepwise:
        both, own, mine, rest = own_weights(w_in, w_back)
        z_two, z_one, x_own = swap(mine, "mp", 4), swap(mine, "mp", 2), swap(own, "mp", 1)
    queries, keys_own, values_own, *first = attend_first(
        lo, nw, tokens, w_query, w_key, w_value, prefix_keys, prefix_vals, segc, segk, width
    )
    if stepwise:
        z_one, z_two, x_own, mine, rest, queries, keys_own, values_own = lax.optimization_barrier(
            (z_one, z_two, x_own, mine, rest, queries, keys_own, values_own)
        )
        z_three, z_last = swap(mine, "mp", 6), swap(rest, "mp", 2)
        x_two, y_two, x_one = swap(z_two, "mp", 1), swap(z_two, "dp", 2), swap(z_one, "mp", 1)
    moved = [x_own, z_one, z_two] if stepwise else []
    second = attend_rest(
        lo, nw, queries, keys_own, values_own, prefix_keys, prefix_vals, segc, segk, width, 1, moved
    )
    least, most = jnp.minimum(first[2], second[2]), jnp.maximum(first[3], second[3])
    redo = jnp.logical_not(jnp.all(jnp.logical_and(least > LEAST, most < MOST))).astype(jnp.int32)[None]
    held = attend_again(
        redo, lo, nw, prefix_keys, prefix_vals, segc, segk, queries, keys_own, values_own, first[:2], second[:2]
    )
    seen = [held[:2], held[2:]]
    attended = [held[0], held[2]]
    if stepwise:
        x_two, y_two, held, *attended = lax.optimization_barrier((x_two, y_two, second[4], *attended))
        yx_two = swap(x_two, "dp", 2)
        more = with_other([held])
        hat, inv, normed_low, total, slope, held = ffn_forward(
            attended, tokens, w_out, first_gain, [both], [x_two, y_two]
        )
        x_one, z_three, z_last, yx_two, held, more, normed_low, total = lax.optimization_barrier(
            (x_one, z_three, z_last, yx_two, held, more, normed_low, total)
        )
        x_three, y_three = swap(z_three, "mp", 1), swap(z_three, "dp", 2)
        again = with_other([held, x_one, yx_two])
        total, slope_more = ffn_more(normed_low, total, more)
        x_three, y_three, z_last, again, normed_low, total = lax.optimization_barrier(
            (x_three, y_three, z_last, again, normed_low, total)
        )
        yx_three, x_last = swap(x_three, "dp", 2), swap(z_last, "mp", 1)
        late = with_other([z_three, z_last, x_three])
        total, slope_again = ffn_more(normed_low, total, again)
        yx_three, x_last, y_three, late, total = lax.optimization_barrier((yx_three, x_last, y_three, late, total))
        early, slopes = [both] + more + again, [slope, slope_more, slope_again]
        late = late + with_other([y_three, x_last, yx_three])
    else:
        every = gather_plain(w_in, w_back)
        cut = every.shape[1] * 3 // 8
        early, late = [every[:, :cut]], [every[:, cut:]]
        hat, inv, normed_low, total, slope = ffn_forward(attended, tokens, w_out, first_gain, early, [])
        slopes = [slope]
    layer_output, grad_one, grad_att, delta, ds_prefix, dpk, dpv = middle(
        normed_low, inv, second_gain, first_gain, prefix_keys, prefix_vals,
        total, cotangent, hat, w_out, queries, seen, slopes, early, late,
    )
    logs = [lse for _, lse in seen]
    prefix_grad, input_grad = sum_everywhere(
        jnp.stack([dpk, dpv]),
        [
            lambda _: attend_back(
                lo, nw, queries, keys_own, values_own, grad_att, logs, delta, ds_prefix, prefix_keys, segc, segk
            ),
            lambda grads: project_back(grads, (w_query, w_key, w_value), grad_one),
        ],
    )
    new_first = beta_one * moment_one + (1.0 - beta_one) * prefix_grad
    new_second = beta_two * moment_two + (1.0 - beta_two) * prefix_grad * prefix_grad
    first_hat = new_first / (1.0 - beta_one**STEP)
    second_hat = new_second / (1.0 - beta_two**STEP)
    new_master = prefix_master * (1.0 - learn_rate * weight_decay) - learn_rate * first_hat / (
        jnp.sqrt(second_hat) + epsilon_adam
    )
    return (layer_output, input_grad, new_master, new_first, new_second, new_master.astype(bf16))


def solution(mesh):
    rows = P(("dp", "mp"), None)
    return jax.shard_map(
        on_device,
        mesh=mesh,
        in_specs=(rows, rows, P(), P(), P(), P(), P(), P(), P(None, "mp"), P("mp", None), P(), P(), P(), rows),
        out_specs=(rows, rows, P(), P(), P(), P()),
        check_vma=False,
    )
```

```python
import functools

import jax
import jax.numpy as jnp
from jax import lax
from jax.experimental import pallas as pl
from jax.experimental.pallas import tpu as pltpu
from jax.sharding import PartitionSpec as P

f32, bf16 = jnp.float32, jnp.bfloat16
STEP = 5
epsilon_norm = 1e-05
learn_rate = 1.0
weight_decay = 0.01
beta_one = 0.9
beta_two = 0.999
epsilon_adam = 1e-08
HEAD_SCALE = 0.125
NEG = -1e30
WIN = 256
KC = 64
QUAD = 256
LEAST, MOST = 1e-25, 1e30
ITEMS = 64
VMEM = 60 << 20
NN = (((1,), (0,)), ((), ()))
NT = (((1,), (1,)), ((), ()))
TN = (((0,), (0,)), ((), ()))


def dot(a, b, d=NN):
    return lax.dot_general(a, b, d, preferred_element_type=f32)


def vm():
    return pl.BlockSpec(memory_space=pltpu.VMEM)


def sm():
    return pl.BlockSpec(memory_space=pltpu.SMEM)


def hbm():
    return pl.BlockSpec(memory_space=pl.ANY)


def cost(flops, moved=8 << 20):
    return pl.CostEstimate(flops=4 * flops, bytes_accessed=moved, transcendentals=0)


def part_of(array, width, part):
    return pl.BlockSpec((array.shape[0], width), lambda i: (0, part))


def whole_of(array):
    return pl.BlockSpec(array.shape, lambda i: (0, 0))


def block_diag(piece):
    lane = lax.broadcasted_iota(jnp.int32, piece.shape, 1) // 64
    zero = jnp.zeros_like(piece)
    return jnp.concatenate([jnp.where(lane == h, piece, zero) for h in range(4)], axis=0)


def diag_of(full):
    lane = lax.broadcasted_iota(jnp.int32, (KC, 128), 1) < 64
    left = jnp.where(lane, full[0:64, 0:128], full[64:128, 0:128])
    right = jnp.where(lane, full[128:192, 128:256], full[192:256, 128:256])
    return jnp.concatenate([left, right], axis=1)


def head_ones():
    row = lax.broadcasted_iota(jnp.int32, (QUAD, QUAD), 0) // 64
    lane = lax.broadcasted_iota(jnp.int32, (QUAD, QUAD), 1) // 64
    return jnp.where(row == lane, 1.0, 0.0).astype(bf16)


def head_sum(x, ones):
    high = x.astype(bf16)
    return dot(high, ones) + dot((x - high.astype(f32)).astype(bf16), ones)


def head_max(x):
    lane = lax.broadcasted_iota(jnp.int32, x.shape, 1) < 64
    a = jnp.max(jnp.where(lane, x, NEG), axis=1, keepdims=True)
    b = jnp.max(jnp.where(lane, NEG, x), axis=1, keepdims=True)
    return jnp.where(lane, a, b)


def windows(seg):
    length = seg.shape[0]
    by = seg.reshape(length // KC, KC)
    first, last = by[:, 0], by[:, -1]
    lo = jnp.sum((seg[None, :] < first[:, None]).astype(jnp.int32), axis=1)
    hi = jnp.sum((seg[None, :] <= last[:, None]).astype(jnp.int32), axis=1)
    lo = lo // 16 * 16
    nw = (hi - lo + WIN - 1) // WIN
    segc = jnp.broadcast_to(seg[:, None], (length, 128))
    segk = jnp.concatenate([by, by], axis=1)
    return lo, nw, segc, segk


def list_items(lo_ref, nw_ref, chunk_ref, row_ref, length):
    def chunk(c, count):
        def one(w, count):
            chunk_ref[count] = c
            row_ref[count] = lo_ref[c] + w * WIN
            return count + 1

        return lax.fori_loop(0, nw_ref[c], one, count)

    count = lax.fori_loop(0, length // KC, chunk, 0)
    for n in range(2):
        chunk_ref[count + n] = 0
        row_ref[count + n] = length
    return count


def item_at(n, chunk_ref, row_ref, segc_ref, segk_ref, length):
    c, nominal = chunk_ref[n], row_ref[n]
    start = pl.multiple_of(jnp.minimum(nominal, length - WIN), 16)
    rows = pl.ds(start, WIN)
    keys = pl.ds(pl.multiple_of(c * KC, KC), KC)
    row_id = lax.broadcasted_iota(jnp.int32, (WIN, 128), 0) + start
    keep = jnp.logical_and(segc_ref[rows, :] == segk_ref[pl.ds(c, 1), :], row_id >= nominal)
    bias = jnp.where(keep, 0.0, NEG)
    return rows, keys, jnp.concatenate([bias, bias], axis=1)


def staged(units, first, second, third):
    raw, done = first(units[0]), None
    for n in range(len(units) + 1):
        upcoming = first(units[n + 1]) if n + 1 < len(units) else None
        fresh = second(units[n], raw) if n < len(units) else None
        if done is not None:
            third(units[n - 1], done)
        raw, done = upcoming, fresh


def join_copies(pieces, buffer, target, sems):
    copies, row = [], 0
    for n, piece in enumerate(pieces):
        rows = piece.shape[1]
        copies.append(pltpu.make_async_copy(piece, buffer.at[:, row : row + rows], sems.at[n]))
        row += rows
    return copies, [pltpu.make_async_copy(buffer, target, sems.at[len(pieces)])]


def begin(copies):
    for copy in copies:
        copy.start()


def finish(copies):
    for copy in copies:
        copy.wait()


def joined_shape(pieces):
    planes, _, lanes = pieces[0].shape
    return jax.ShapeDtypeStruct((planes, sum(piece.shape[1] for piece in pieces), lanes), pieces[0].dtype)


def attend_columns(count, q_ref, k_ref, v_ref, pk_ref, pv_ref, att_ref, lse_ref, l_ref, acc_ref, item):
    length, width = att_ref.shape
    parts = [slice(c, c + QUAD) for c in range(0, width, QUAD)]
    spans = [slice(r, r + WIN) for r in range(0, length, WIN)]
    ids = range(len(parts))
    ones = head_ones()
    bdk = [block_diag(pk_ref[:, cols]) for cols in parts]
    bdv = [block_diag(pv_ref[:, cols]) for cols in parts]

    def start_third(unit, p):
        rows, g = unit
        l_ref[rows, parts[g]] = p
        acc_ref[rows, parts[g]] = dot(p.astype(bf16), bdv[g])

    staged(
        [(rows, g) for g in ids for rows in spans],
        lambda u: dot(q_ref[u[0], parts[u[1]]], bdk[u[1]], NT),
        lambda u, s: jnp.exp(s),
        start_third,
    )

    @pl.loop(0, (count + 1) // 2)
    def _(n):
        def third(unit, p):
            (rows, keys, _), g = unit
            l_ref[rows, parts[g]] += p
            acc_ref[rows, parts[g]] += dot(p.astype(bf16), block_diag(v_ref[keys, parts[g]]))

        staged(
            [(one, g) for one in (item(2 * n), item(2 * n + 1)) for g in ids],
            lambda u: dot(q_ref[u[0][0], parts[u[1]]], block_diag(k_ref[u[0][1], parts[u[1]]]), NT),
            lambda u, s: jnp.exp(s + u[0][2]),
            third,
        )

    least, most = [], []
    for rows in spans:
        for cols in parts:
            total = head_sum(l_ref[rows, cols], ones)
            att_ref[rows, cols] = (acc_ref[rows, cols] / total).astype(bf16)
            lse_ref[rows, cols] = jnp.log(total)
            least.append(jnp.min(total, axis=0, keepdims=True))
            most.append(jnp.max(total, axis=0, keepdims=True))
    return functools.reduce(jnp.minimum, least), functools.reduce(jnp.maximum, most)


def attend_again_kernel(
    redo_ref, lo_ref, nw_ref, pk_ref, pv_ref, segc_ref, segk_ref, q_hbm, k_hbm, v_hbm, _a, _b, _c, _d,
    att_one, lse_one, att_two, lse_two,
    q_ref, k_ref, v_ref, part_pk, part_pv, att_ref, lse_ref, l_ref, acc_ref, chunk_ref, row_ref, sems,
):
    @pl.when(redo_ref[0] > 0)
    def _():
        length, width = att_ref.shape
        count = list_items(lo_ref, nw_ref, chunk_ref, row_ref, length)

        def item(n):
            return item_at(n, chunk_ref, row_ref, segc_ref, segk_ref, length)

        for part, (att_hbm, lse_hbm) in enumerate(((att_one, lse_one), (att_two, lse_two))):
            cols = slice(part * width, (part + 1) * width)
            loads = [
                pltpu.make_async_copy(a.at[:, cols], b, sems.at[n])
                for n, (a, b) in enumerate(((q_hbm, q_ref), (k_hbm, k_ref), (v_hbm, v_ref)))
            ]
            begin(loads)
            part_pk[...] = pk_ref[:, cols]
            part_pv[...] = pv_ref[:, cols]
            finish(loads)
            quads, tiles = width // QUAD, length // WIN

            def block(n):
                rows = pl.ds(pl.multiple_of(n // quads * WIN, WIN), WIN)
                return rows, pl.ds(pl.multiple_of(n % quads * QUAD, QUAD), QUAD)

            def entry(n):
                rows, keys, bias = item(n // quads)
                return rows, keys, bias, pl.ds(pl.multiple_of(n % quads * QUAD, QUAD), QUAD)

            @pl.loop(0, quads * tiles)
            def _(n):
                rows, quad = block(n)
                lse_ref[rows, quad] = dot(q_ref[rows, quad], block_diag(part_pk[:, quad]), NT)

            @pl.loop(0, quads * count)
            def _(n):
                rows, keys, bias, quad = entry(n)
                s = dot(q_ref[rows, quad], block_diag(k_ref[keys, quad]), NT) + bias
                lse_ref[rows, quad] = jnp.maximum(lse_ref[rows, quad], s)

            @pl.loop(0, 2 * quads * (length // KC))
            def _(n):
                rows = pl.ds(pl.multiple_of(n // (2 * quads) * KC, KC), KC)
                pair = pl.ds(pl.multiple_of(n % (2 * quads) * 128, 128), 128)
                lse_ref[rows, pair] = head_max(lse_ref[rows, pair])

            @pl.loop(0, quads * tiles)
            def _(n):
                rows, quad = block(n)
                p = jnp.exp(dot(q_ref[rows, quad], block_diag(part_pk[:, quad]), NT) - lse_ref[rows, quad])
                l_ref[rows, quad] = p
                acc_ref[rows, quad] = dot(p.astype(bf16), block_diag(part_pv[:, quad]))

            @pl.loop(0, quads * count)
            def _(n):
                rows, keys, bias, quad = entry(n)
                s = dot(q_ref[rows, quad], block_diag(k_ref[keys, quad]), NT)
                p = jnp.exp(s - lse_ref[rows, quad] + bias)
                l_ref[rows, quad] += p
                acc_ref[rows, quad] += dot(p.astype(bf16), block_diag(v_ref[keys, quad]))

            @pl.loop(0, quads * tiles)
            def _(n):
                rows, quad = block(n)
                total = head_sum(l_ref[rows, quad], head_ones())
                att_ref[rows, quad] = (acc_ref[rows, quad] / total).astype(bf16)
                lse_ref[rows, quad] += jnp.log(total)

            stores = [
                pltpu.make_async_copy(a, b, sems.at[n]) for n, (a, b) in enumerate(((att_ref, att_hbm), (lse_ref, lse_hbm)))
            ]
            begin(stores)
            finish(stores)


def attend_again(redo, lo, nw, pk, pv, segc, segk, q, k, v, first, second):
    length, width = first[0].shape
    slots = pk.shape[0]
    held = (*first, *second)
    return pl.pallas_call(
        attend_again_kernel,
        out_shape=tuple(jax.ShapeDtypeStruct(a.shape, a.dtype) for a in held),
        in_specs=[sm()] * 3 + [vm()] * 4 + [hbm()] * 7,
        out_specs=(hbm(),) * 4,
        input_output_aliases={10 + n: n for n in range(4)},
        scratch_shapes=[pltpu.VMEM((length, width), bf16)] * 3
        + [pltpu.VMEM((slots, width), bf16)] * 2
        + [pltpu.VMEM((length, width), t) for t in (bf16, f32, f32, f32)]
        + [pltpu.SMEM((ITEMS,), jnp.int32)] * 2
        + [pltpu.SemaphoreType.DMA((3,))],
        compiler_params=pltpu.CompilerParams(vmem_limit_bytes=VMEM),
        cost_estimate=cost(1 << 20, 1 << 20),
        name="attend_again",
    )(redo, lo, nw, pk, pv, segc, segk, q, k, v, *held)


def attend_first_kernel(
    lo_ref, nw_ref, x_ref, wq_hbm, wk_hbm, wv_hbm, pk_ref, pv_ref, segc_ref, segk_ref,
    q_hbm, k_hbm, v_hbm, att_ref, lse_ref, least_ref, most_ref,
    w_ref, q_ref, k_ref, v_ref, l_ref, acc_ref, chunk_ref, row_ref, in_sems, out_sems,
):
    length, lanes = x_ref.shape
    loads = [pltpu.make_async_copy(w, w_ref.at[n], in_sems.at[n]) for n, w in enumerate((wq_hbm, wk_hbm, wv_hbm))]
    stores = [
        pltpu.make_async_copy(a, b, out_sems.at[n])
        for n, (a, b) in enumerate(((q_ref, q_hbm), (k_ref, k_hbm), (v_ref, v_hbm)))
    ]
    for load in loads:
        load.start()
    count = list_items(lo_ref, nw_ref, chunk_ref, row_ref, length)
    for n, out_ref in enumerate((q_ref, k_ref, v_ref)):
        loads[n].wait()
        for c in range(0, lanes, QUAD):
            value = dot(x_ref[...], w_ref[n, :, c : c + QUAD])
            out_ref[:, c : c + QUAD] = (value * HEAD_SCALE if n == 0 else value).astype(bf16)
        stores[n].start()

    def item(n):
        return item_at(n, chunk_ref, row_ref, segc_ref, segk_ref, length)

    least_ref[...], most_ref[...] = attend_columns(
        count, q_ref, k_ref, v_ref, pk_ref, pv_ref, att_ref, lse_ref, l_ref, acc_ref, item
    )
    for store in stores:
        store.wait()


def attend_rest_kernel(*refs, count):
    lo_ref, nw_ref, q_ref, k_ref, v_ref, pk_ref, pv_ref, segc_ref, segk_ref = refs[:9]
    pieces, refs = refs[9 : 9 + count], refs[9 + count :]
    att_ref, lse_ref, least_ref, most_ref, *refs = refs
    arrive, leave = [], []
    if count:
        target, *refs, held, sems = refs
        arrive, leave = join_copies(pieces, held, target, sems)
    l_ref, acc_ref, chunk_ref, row_ref = refs
    begin(arrive)
    length = q_ref.shape[0]
    items = list_items(lo_ref, nw_ref, chunk_ref, row_ref, length)
    finish(arrive)
    begin(leave)

    def item(n):
        return item_at(n, chunk_ref, row_ref, segc_ref, segk_ref, length)

    least_ref[...], most_ref[...] = attend_columns(
        items, q_ref, k_ref, v_ref, pk_ref, pv_ref, att_ref, lse_ref, l_ref, acc_ref, item
    )
    finish(leave)


def attended_shapes(length, width):
    shape, lane = (length, width), jax.ShapeDtypeStruct((1, QUAD), f32)
    return [jax.ShapeDtypeStruct(shape, bf16), jax.ShapeDtypeStruct(shape, f32), lane, lane]


def attend_first(lo, nw, x, wq, wk, wv, pk, pv, segc, segk, width):
    length, lanes = x.shape
    low = jax.ShapeDtypeStruct((length, lanes), bf16)
    return pl.pallas_call(
        attend_first_kernel,
        out_shape=(low, low, low, *attended_shapes(length, width)),
        in_specs=[sm(), sm(), vm(), hbm(), hbm(), hbm(), vm(), vm(), vm(), vm()],
        out_specs=(hbm(), hbm(), hbm(), vm(), vm(), vm(), vm()),
        scratch_shapes=[pltpu.VMEM((3, lanes, lanes), bf16)]
        + [pltpu.VMEM((length, lanes), bf16)] * 3
        + [pltpu.VMEM((length, width), f32)] * 2
        + [pltpu.SMEM((ITEMS,), jnp.int32)] * 2
        + [pltpu.SemaphoreType.DMA((3,))] * 2,
        compiler_params=pltpu.CompilerParams(vmem_limit_bytes=VMEM),
        cost_estimate=cost(16 * length * lanes * lanes),
        name="attend_first",
    )(lo, nw, x, wq, wk, wv, pk, pv, segc, segk)


def attend_rest(lo, nw, q, k, v, pk, pv, segc, segk, width, part, pieces):
    length = q.shape[0]
    outs = attended_shapes(length, width)
    specs = [whole_of(each) for each in outs]
    scratch = [pltpu.VMEM((length, width), f32)] * 2 + [pltpu.SMEM((ITEMS,), jnp.int32)] * 2
    if pieces:
        held = joined_shape(pieces)
        outs.append(held)
        specs.append(hbm())
        scratch += [pltpu.VMEM(held.shape, held.dtype), pltpu.SemaphoreType.DMA((len(pieces) + 1,))]
    return pl.pallas_call(
        functools.partial(attend_rest_kernel, count=len(pieces)),
        grid=(1,),
        out_shape=tuple(outs),
        in_specs=[sm(), sm()]
        + [part_of(a, width, part) for a in (q, k, v, pk, pv)]
        + [whole_of(segc), whole_of(segk)]
        + [hbm()] * len(pieces),
        out_specs=tuple(specs),
        scratch_shapes=scratch,
        compiler_params=pltpu.CompilerParams(vmem_limit_bytes=VMEM),
        cost_estimate=cost(16000 * length * width),
        name="attend_rest",
    )(lo, nw, q, k, v, pk, pv, segc, segk, *pieces)


def attend_back_kernel(*refs, halves):
    lo_ref, nw_ref, pk_ref, segc_ref, segk_ref = refs[:5]
    sources, refs = refs[5 : 11 + halves], refs[11 + halves :]
    (
        dq_hbm, dk_hbm, dv_hbm,
        q_ref, k_ref, v_ref, g_ref, delta_ref, ds_ref, lse_ref,
        dq_acc, dk_acc, dv_acc, dq_ref, dk_ref, dv_ref, chunk_ref, row_ref, in_sems, out_sems,
    ) = refs
    length, lanes = q_ref.shape
    parts = [slice(g * QUAD, (g + 1) * QUAD) for g in range(lanes // QUAD)]
    spans = [slice(r * WIN, (r + 1) * WIN) for r in range(length // WIN)]
    places = [ds_ref, q_ref, k_ref, v_ref, g_ref, delta_ref]
    for n in range(halves):
        places.append(lse_ref.at[:, n * (lanes // halves) : (n + 1) * (lanes // halves)])
    loads = [pltpu.make_async_copy(a, b, in_sems.at[n]) for n, (a, b) in enumerate(zip(sources, places))]
    for load in loads:
        load.start()
    count = list_items(lo_ref, nw_ref, chunk_ref, row_ref, length)
    dk_acc[...] = jnp.zeros_like(dk_acc)
    dv_acc[...] = jnp.zeros_like(dv_acc)
    loads[0].wait()
    for cols in parts:
        bdk = block_diag(pk_ref[:, cols])
        for rows in spans:
            dq_acc[rows, cols] = dot(ds_ref[rows, cols], bdk)
    for load in loads[1:]:
        load.wait()
    ids = range(len(parts))

    @pl.loop(0, (count + 1) // 2)
    def _(n):
        def first(unit):
            (rows, keys, _), g = unit
            cols = parts[g]
            s = dot(q_ref[rows, cols], block_diag(k_ref[keys, cols]), NT)
            return s, dot(g_ref[rows, cols], block_diag(v_ref[keys, cols]), NT)

        def second(unit, pair):
            (rows, _, bias), g = unit
            cols = parts[g]
            p = jnp.exp(pair[0] + bias - lse_ref[rows, cols])
            return p.astype(bf16), (p * (pair[1] - delta_ref[rows, cols])).astype(bf16)

        def third(unit, pair):
            (rows, keys, _), g = unit
            cols = parts[g]
            dv_acc[keys, cols] += diag_of(dot(pair[0], g_ref[rows, cols], TN))
            dk_acc[keys, cols] += diag_of(dot(pair[1], q_ref[rows, cols], TN))
            dq_acc[rows, cols] += dot(pair[1], block_diag(k_ref[keys, cols]))

        items = [item_at(2 * n + i, chunk_ref, row_ref, segc_ref, segk_ref, length) for i in range(2)]
        staged([(one, g) for one in items for g in ids], first, second, third)

    stores = []
    ends = ((dq_acc, dq_ref, dq_hbm, HEAD_SCALE), (dk_acc, dk_ref, dk_hbm, 1.0), (dv_acc, dv_ref, dv_hbm, 1.0))
    for n, (acc, low, target, scale) in enumerate(ends):
        low[...] = (acc[...] * scale).astype(bf16)
        stores.append(pltpu.make_async_copy(low, target, out_sems.at[n]))
        stores[n].start()
    for store in stores:
        store.wait()


def attend_back(lo, nw, q, k, v, g, lse, delta, ds, pk, segc, segk):
    length, lanes = q.shape
    tall = (length, lanes)
    return pl.pallas_call(
        functools.partial(attend_back_kernel, halves=len(lse)),
        out_shape=(jax.ShapeDtypeStruct(tall, bf16),) * 3,
        in_specs=[sm(), sm(), vm(), vm(), vm()] + [hbm()] * (6 + len(lse)),
        out_specs=(hbm(),) * 3,
        scratch_shapes=[pltpu.VMEM(tall, t) for t in (bf16, bf16, bf16, bf16, f32, bf16, f32)]
        + [pltpu.VMEM(tall, f32)] * 3
        + [pltpu.VMEM(tall, bf16)] * 3
        + [pltpu.SMEM((ITEMS,), jnp.int32)] * 2
        + [pltpu.SemaphoreType.DMA((6 + len(lse),)), pltpu.SemaphoreType.DMA((3,))],
        compiler_params=pltpu.CompilerParams(vmem_limit_bytes=VMEM),
        cost_estimate=cost(length * lanes * 30000),
        name="attend_back",
    )(lo, nw, pk, segc, segk, ds, q, k, v, g, delta, *lse)


HID = 512


def mean_of(x):
    return jnp.mean(x, axis=-1, keepdims=True)


def centre(x):
    centred = x - mean_of(x)
    inv = lax.rsqrt(mean_of(centred * centred) + epsilon_norm)
    return centred * inv, inv


def pull_norm(pull, hat, inv):
    return inv * (pull - mean_of(pull) - hat * mean_of(pull * hat))


def gelu_pair(x):
    phi = 0.5 + 0.5 * lax.erf(x * 0.7071067811865476)
    bell = 0.3989422804014327 * jnp.exp(-0.5 * (x * x))
    return x * phi, phi + x * bell


def blocks_of(pieces):
    blocks, block, room = [], [], HID
    for piece in pieces:
        row = 0
        while row < piece.shape[1]:
            rows = min(room, piece.shape[1] - row)
            block.append((piece, row, rows))
            row, room = row + rows, room - rows
            if room == 0:
                blocks.append(block)
                block, room = [], HID
    return blocks


def most_of(pieces):
    return max(len(block) for block in blocks_of(pieces))


def block_copies(block, buffer, sems, slot):
    copies, place = [], 0
    for n, (piece, row, rows) in enumerate(block):
        source = piece.at[:, row : row + rows]
        copies.append(pltpu.make_async_copy(source, buffer.at[slot, :, place : place + rows], sems.at[slot, n]))
        place += rows
    return copies


def forward_block(low_ref, weights, sum_ref, slope_ref, cols):
    def second(rows, x):
        act, slope = gelu_pair(x)
        slope_ref[rows, cols] = slope.astype(bf16)
        return act.astype(bf16)

    def third(rows, act):
        sum_ref[rows, :] += dot(act, weights[1])

    spans = [slice(r, r + WIN) for r in range(0, low_ref.shape[0], WIN)]
    staged(spans, lambda rows: dot(low_ref[rows, :], weights[0], NT), second, third)


def ffn_kernel(*refs, halves, count, others):
    atts, (tok_ref, w_out_ref, gain_ref), refs = refs[:halves], refs[halves : halves + 3], refs[halves + 3 :]
    blocks, pieces, refs = blocks_of(refs[:count]), refs[count : count + others], refs[count + others :]
    hat_ref, inv_ref, low_ref, sum_ref, slope_ref, *refs = refs
    arrive, leave = [], []
    if others:
        target, *refs, held, join_sems = refs
        arrive, leave = join_copies(pieces, held, target, join_sems)
    buffer, sems = refs
    width = atts[0].shape[1]
    copies = [block_copies(block, buffer, sems, b % 2) for b, block in enumerate(blocks)]
    begin(copies[0])
    begin(arrive)

    def second(rows, x):
        hat, inv = centre(tok_ref[rows, :].astype(f32) + x)
        hat_ref[rows, :] = hat
        inv_ref[rows, :] = jnp.broadcast_to(inv, (WIN, 128))
        normed = gain_ref[...] * hat
        sum_ref[rows, :] = normed
        low_ref[rows, :] = normed.astype(bf16)

    def first(rows):
        return sum(dot(att_ref[rows, :], w_out_ref[n * width : (n + 1) * width, :]) for n, att_ref in enumerate(atts))

    spans = [slice(r, r + WIN) for r in range(0, tok_ref.shape[0], WIN)]
    staged(spans, first, second, lambda rows, x: None)
    finish(arrive)
    begin(leave)
    for b in range(len(blocks)):
        if b + 1 < len(blocks):
            begin(copies[b + 1])
        finish(copies[b])
        forward_block(low_ref, buffer.at[b % 2], sum_ref, slope_ref, slice(b * HID, (b + 1) * HID))
    finish(leave)


def ffn_forward(att, tokens, w_out, gain, pieces, others):
    length, lanes = tokens.shape
    hidden = sum(piece.shape[1] for piece in pieces)
    wide = jax.ShapeDtypeStruct((length, lanes), f32)
    outs = [
        wide,
        jax.ShapeDtypeStruct((length, 128), f32),
        jax.ShapeDtypeStruct((length, lanes), bf16),
        wide,
        jax.ShapeDtypeStruct((length, hidden), bf16),
    ]
    specs = [vm()] * 5
    scratch = [pltpu.VMEM((2, 2, HID, lanes), bf16), pltpu.SemaphoreType.DMA((2, most_of(pieces)))]
    if others:
        held = joined_shape(others)
        outs.append(held)
        specs.append(hbm())
        scratch += [pltpu.VMEM(held.shape, held.dtype), pltpu.SemaphoreType.DMA((len(others) + 1,))]
    return pl.pallas_call(
        functools.partial(ffn_kernel, halves=len(att), count=len(pieces), others=len(others)),
        out_shape=tuple(outs),
        in_specs=[vm()] * (len(att) + 3) + [hbm()] * (len(pieces) + len(others)),
        out_specs=tuple(specs),
        scratch_shapes=scratch,
        compiler_params=pltpu.CompilerParams(vmem_limit_bytes=VMEM),
        cost_estimate=cost(4 * length * lanes * (hidden + lanes)),
        name="ffn_forward",
    )(*att, tokens, w_out, gain, *pieces, *others)


def more_kernel(low_ref, start_ref, *refs, count):
    blocks = blocks_of(refs[:count])
    sum_ref, slope_ref, buffer, sems = refs[count:]
    copies = [block_copies(block, buffer, sems, b % 2) for b, block in enumerate(blocks)]
    begin(copies[0])
    sum_ref[...] = start_ref[...]
    for b in range(len(blocks)):
        if b + 1 < len(blocks):
            begin(copies[b + 1])
        finish(copies[b])
        forward_block(low_ref, buffer.at[b % 2], sum_ref, slope_ref, slice(b * HID, (b + 1) * HID))


def ffn_more(low, start, pieces):
    length, lanes = low.shape
    hidden = sum(piece.shape[1] for piece in pieces)
    return pl.pallas_call(
        functools.partial(more_kernel, count=len(pieces)),
        out_shape=(jax.ShapeDtypeStruct((length, lanes), f32), jax.ShapeDtypeStruct((length, hidden), bf16)),
        in_specs=[vm()] * 2 + [hbm()] * len(pieces),
        out_specs=(vm(),) * 2,
        scratch_shapes=[pltpu.VMEM((2, 2, HID, lanes), bf16), pltpu.SemaphoreType.DMA((2, most_of(pieces)))],
        compiler_params=pltpu.CompilerParams(vmem_limit_bytes=VMEM),
        cost_estimate=cost(4 * length * lanes * hidden),
        name="ffn_more",
    )(low, start, *pieces)


def middle_kernel(*refs, halves, early, late, groups):
    low_ref, inv_ref, gain_two_ref, gain_one_ref, pk_ref, pv_ref = refs[:6]
    sum_hbm, cot_hbm, hat_hbm, w_out_hbm, q_hbm = refs[6:11]
    seen, refs = refs[11 : 11 + 2 * halves], refs[11 + 2 * halves :]
    slopes, pieces, refs = refs[:groups], refs[groups : groups + early + late], refs[groups + early + late :]
    (layer_hbm, one_hbm, g_hbm, delta_hbm, ds_hbm, dpk_ref, dpv_ref) = refs[:7]
    (
        acc_ref, cot_ref, hat_ref, w_out_ref, q_ref, att_ref, lse_ref, layer_ref, one_ref, g_ref, delta_ref, ds_ref,
        grad_ref, late_ref, buffer, sbuf, sems, ssems, in_sems, out_sems,
    ) = refs[7:]
    length, lanes = low_ref.shape
    spans = [slice(r, r + WIN) for r in range(0, length, WIN)]
    parts = [slice(c, c + QUAD) for c in range(0, lanes, QUAD)]
    first_blocks, last_blocks = blocks_of(pieces[:early]), blocks_of(pieces[early:])
    order = last_blocks + first_blocks + last_blocks
    copies = [block_copies(block, buffer, sems, n % 2) for n, block in enumerate(order)]
    skip = len(last_blocks)
    slabs = [slope.at[:, c : c + HID] for slope in slopes for c in range(0, slope.shape[1], HID)]
    for n, source in enumerate(slabs, skip):
        copies[n].append(pltpu.make_async_copy(source, sbuf.at[n % 2], ssems.at[n % 2]))
    sources = (sum_hbm, cot_hbm, hat_hbm, w_out_hbm, q_hbm, *seen)
    places = [acc_ref, cot_ref, hat_ref, w_out_ref, q_ref]
    for n in range(halves):
        cols = slice(n * (lanes // halves), (n + 1) * (lanes // halves))
        places += [att_ref.at[:, cols], lse_ref.at[:, cols]]
    loads = [pltpu.make_async_copy(a, b, in_sems.at[n]) for n, (a, b) in enumerate(zip(sources, places))]
    results = (layer_ref, one_ref, g_ref, delta_ref, ds_ref)
    targets = (layer_hbm, one_hbm, g_hbm, delta_hbm, ds_hbm)
    stores = [pltpu.make_async_copy(a, b, out_sems.at[n]) for n, (a, b) in enumerate(zip(results, targets))]
    begin(copies[0])
    begin(loads[:1])

    def enter(n):
        if n + 1 < len(order):
            begin(copies[n + 1])
        if n == 0:
            finish(loads[:1])
            begin(loads[1:])
        finish(copies[n])
        return buffer.at[n % 2]

    for n in range(skip):
        forward_block(low_ref, enter(n), acc_ref, late_ref, slice(n * HID, (n + 1) * HID))

    finish(loads[1:3])
    for n in range(skip, len(order)):
        weights = enter(n)
        past = n - skip - len(first_blocks)

        def first(rows):
            if n == skip:
                hat, inv = centre(acc_ref[rows, :])
                layer_ref[rows, :] = (gain_two_ref[...] * hat).astype(bf16)
                grad = pull_norm(cot_ref[rows, :].astype(f32) * gain_two_ref[...], hat, inv)
                acc_ref[rows, :] = grad
                grad_ref[rows, :] = grad.astype(bf16)
            return dot(grad_ref[rows, :], weights[1], NT)

        def second(rows, x):
            slope = sbuf[n % 2, rows, :] if past < 0 else late_ref[rows, past * HID : (past + 1) * HID]
            return (x * slope.astype(f32)).astype(bf16)

        def third(rows, x):
            acc_ref[rows, :] += dot(x, weights[0])

        staged(spans, first, second, third)
        if n == skip:
            begin(stores[:1])
    finish(loads[3:])

    def first(rows):
        grad = pull_norm(acc_ref[rows, :] * gain_one_ref[...], hat_ref[rows, :], inv_ref[rows, 0:1])
        one_ref[rows, :] = grad
        return grad.astype(bf16)

    def second(rows, grad):
        g_ref[rows, :] = dot(grad, w_out_ref[...], NT).astype(bf16)

    staged(spans, first, second, lambda rows, x: None)
    begin(stores[1:3])

    ones = head_ones()
    sums = {}

    def first(unit):
        g, rows = unit
        cols = parts[g]
        up = g_ref[rows, cols]
        delta = head_sum(up.astype(f32) * att_ref[rows, cols].astype(f32), ones)
        return dot(q_ref[rows, cols], block_diag(pk_ref[:, cols]), NT), dot(up, block_diag(pv_ref[:, cols]), NT), delta

    def second(unit, three):
        g, rows = unit
        cols = parts[g]
        delta_ref[rows, cols] = three[2]
        p = jnp.exp(three[0] - lse_ref[rows, cols])
        ds = (p * (three[1] - three[2])).astype(bf16)
        ds_ref[rows, cols] = ds
        return p.astype(bf16), ds

    def third(unit, pair):
        g, rows = unit
        cols = parts[g]
        dpv, dpk = diag_of(dot(pair[0], g_ref[rows, cols], TN)), diag_of(dot(pair[1], q_ref[rows, cols], TN))
        if rows.start:
            dpv, dpk = sums[g][0] + dpv, sums[g][1] + dpk
        sums[g] = (dpv, dpk)
        if rows.stop == length:
            dpv_ref[:, cols], dpk_ref[:, cols] = dpv, dpk

    staged([(g, rows) for g in range(len(parts)) for rows in spans], first, second, third)
    begin(stores[3:])
    finish(stores)


def middle(low, inv, gain_two, gain_one, pk, pv, total, cot, hat, w_out, q, seen, slopes, early, late):
    length, lanes = low.shape
    slots = pk.shape[0]
    late_units = sum(piece.shape[1] for piece in late)
    flat = [each for pair in seen for each in pair]
    tall = (length, lanes)
    small = jax.ShapeDtypeStruct((slots, lanes), f32)
    holds = [f32, bf16, f32, None, bf16, bf16, f32, bf16, f32, bf16, f32, bf16, bf16]
    return pl.pallas_call(
        functools.partial(middle_kernel, halves=len(seen), early=len(early), late=len(late), groups=len(slopes)),
        out_shape=tuple(jax.ShapeDtypeStruct(tall, t) for t in (bf16, f32, bf16, f32, bf16)) + (small, small),
        in_specs=[vm()] * 6 + [hbm()] * (5 + 2 * len(seen) + len(slopes) + len(early) + len(late)),
        out_specs=(hbm(),) * 5 + (vm(), vm()),
        scratch_shapes=[pltpu.VMEM((lanes, lanes), bf16) if t is None else pltpu.VMEM(tall, t) for t in holds]
        + [
            pltpu.VMEM((length, late_units), bf16),
            pltpu.VMEM((2, 2, HID, lanes), bf16),
            pltpu.VMEM((2, length, HID), bf16),
            pltpu.SemaphoreType.DMA((2, most_of(early + late))),
            pltpu.SemaphoreType.DMA((2,)),
            pltpu.SemaphoreType.DMA((5 + len(flat),)),
            pltpu.SemaphoreType.DMA((5,)),
        ],
        compiler_params=pltpu.CompilerParams(vmem_limit_bytes=VMEM),
        cost_estimate=cost(40 * length * lanes * lanes),
        name="middle",
    )(low, inv, gain_two, gain_one, pk, pv, total, cot, hat, w_out, q, *flat, *slopes, *early, *late)


def project_kernel(dq_hbm, dk_hbm, dv_hbm, wq_hbm, wk_hbm, wv_hbm, one_hbm, out_hbm, grads, weights, out_ref, *sems):
    length, lanes = out_ref.shape
    spans = [slice(r, r + WIN) for r in range(0, length, WIN)]
    grad_sems, weight_sems, one_sem, out_sems = sems
    loads = []
    for n, (grad, weight) in enumerate(((dq_hbm, wq_hbm), (dk_hbm, wk_hbm), (dv_hbm, wv_hbm))):
        loads.append(
            (
                pltpu.make_async_copy(grad, grads.at[n], grad_sems.at[n]),
                pltpu.make_async_copy(weight, weights.at[n], weight_sems.at[n]),
            )
        )
        begin(loads[n])
        if n == 0:
            one = pltpu.make_async_copy(one_hbm, out_ref, one_sem.at[0])
            one.start()
    stores = [
        pltpu.make_async_copy(out_ref.at[rows, :], out_hbm.at[rows, :], out_sems.at[r]) for r, rows in enumerate(spans)
    ]
    finish(loads[0])
    first = [dot(grads[0, rows, :], weights[0], NT) for rows in spans[:1]]
    one.wait()
    out_ref[spans[0], :] += first[0]
    for rows in spans[1:]:
        out_ref[rows, :] += dot(grads[0, rows, :], weights[0], NT)
    finish(loads[1])
    finish(loads[2])
    for r, rows in enumerate(spans):
        more = dot(grads[1, rows, :], weights[1], NT) + dot(grads[2, rows, :], weights[2], NT)
        out_ref[rows, :] += more
        stores[r].start()
    finish(stores)


def project_back(grads, weights, grad_one):
    length, lanes = grad_one.shape
    return pl.pallas_call(
        project_kernel,
        out_shape=jax.ShapeDtypeStruct((length, lanes), f32),
        in_specs=[hbm()] * 7,
        out_specs=hbm(),
        scratch_shapes=[
            pltpu.VMEM((3, length, lanes), bf16),
            pltpu.VMEM((3, lanes, lanes), bf16),
            pltpu.VMEM((length, lanes), f32),
            pltpu.SemaphoreType.DMA((3,)),
            pltpu.SemaphoreType.DMA((3,)),
            pltpu.SemaphoreType.DMA((1,)),
            pltpu.SemaphoreType.DMA((length // WIN,)),
        ],
        compiler_params=pltpu.CompilerParams(vmem_limit_bytes=VMEM),
        cost_estimate=cost(6 * length * lanes * lanes),
        name="project_back",
    )(*grads, *weights, grad_one)


def swap(x, axis, bit):
    return lax.ppermute(x, axis, [(i, i ^ bit) for i in range(lax.axis_size(axis))])


def swap_two(x, one, two):
    if one[0] == two[0]:
        return swap(x, one[0], one[1] | two[1])
    wide = {"dp": lax.axis_size("mp"), "mp": 1}
    mask = one[1] * wide[one[0]] + two[1] * wide[two[0]]
    count = lax.axis_size("dp") * lax.axis_size("mp")
    return lax.ppermute(x, ("dp", "mp"), [(i, i ^ mask) for i in range(count)])


def gather_plain(w_in, w_back):
    both = jnp.stack([w_in.T, w_back])
    part = both.shape[1] // lax.axis_size("dp")
    mine = lax.dynamic_slice_in_dim(both, lax.axis_index("dp") * part, part, 1)
    return lax.all_gather(mine, ("dp", "mp"), axis=1, tiled=True)


def own_weights(w_in, w_back):
    both = jnp.stack([w_in.T, w_back])
    half = both.shape[1] // 2
    dp = lax.axis_index("dp")
    own = lax.dynamic_slice_in_dim(both, lax.rem(dp, 2) * half, half, 1)
    unit = half // 2
    mine = lax.dynamic_slice_in_dim(own, dp // 2 * unit, unit, 1)
    rest = lax.dynamic_slice_in_dim(own, (1 - dp // 2) * unit, unit, 1)
    return both, own, mine, rest


def with_other(pieces):
    return [each for piece in pieces for each in (piece, swap(piece, "dp", 1))]


def sum_everywhere(x, between):
    core = lax.rem(lax.axis_index("dp"), 2)
    half = x.shape[0] // 2
    keep = lax.dynamic_slice_in_dim(x, core * half, half, 0)
    give = lax.dynamic_slice_in_dim(x, (1 - core) * half, half, 0)
    part = keep + swap(give, "dp", 1)
    bits = [(axis, 1 << n) for axis in ("dp", "mp") for n in range(lax.axis_size(axis).bit_length() - 1)][1:]
    bits = sorted(bits, key=lambda pair: pair[1] if pair[0] == "mp" else 1)
    done = None
    for n in range(0, len(bits), 2):
        low = part.astype(bf16)
        pairs = bits[n : n + 2]
        came = [swap(low, *pair) for pair in pairs]
        if len(pairs) == 2:
            came.append(swap_two(low, *pairs))
        if between:
            done = between.pop(0)(done)
            came, done = lax.optimization_barrier((came, done))
        part = low.astype(f32) + came[0].astype(f32)
        if len(pairs) == 2:
            part = part + (came[1].astype(f32) + came[2].astype(f32))
    while between:
        done = between.pop(0)(done)
    other = swap(part, "dp", 1)
    return jnp.where(core == 0, jnp.concatenate([part, other]), jnp.concatenate([other, part])), done


def on_device(
    tokens, segment_ids, w_query, w_key, w_value, w_out, gain_one, gain_two, w_in, w_back,
    prefix_master, moment_one, moment_two, cotangent,
):
    stepwise = lax.axis_size("dp") == 4 and lax.axis_size("mp") == 8
    prefix_low = prefix_master.astype(bf16)
    prefix_keys, prefix_vals = prefix_low[0], prefix_low[1]
    first_gain, second_gain = gain_one[None, :], gain_two[None, :]
    lo, nw, segc, segk = windows(segment_ids[0])
    halves = 2
    width = tokens.shape[1] // halves
    if stepwise:
        both, own, mine, rest = own_weights(w_in, w_back)
        z_two, z_one, x_own = swap(mine, "mp", 4), swap(mine, "mp", 2), swap(own, "mp", 1)
    queries, keys_own, values_own, *first = attend_first(
        lo, nw, tokens, w_query, w_key, w_value, prefix_keys, prefix_vals, segc, segk, width
    )
    if stepwise:
        z_one, z_two, x_own, mine, rest, queries, keys_own, values_own = lax.optimization_barrier(
            (z_one, z_two, x_own, mine, rest, queries, keys_own, values_own)
        )
        z_three, z_last = swap(mine, "mp", 6), swap(rest, "mp", 2)
        x_two, y_two = swap(z_two, "mp", 1), swap(z_two, "dp", 2)
    moved = [x_own, z_one, z_two] if stepwise else []
    second = attend_rest(
        lo, nw, queries, keys_own, values_own, prefix_keys, prefix_vals, segc, segk, width, 1, moved
    )
    least, most = jnp.minimum(first[2], second[2]), jnp.maximum(first[3], second[3])
    redo = jnp.logical_not(jnp.all(jnp.logical_and(least > LEAST, most < MOST))).astype(jnp.int32)[None]
    held = attend_again(
        redo, lo, nw, prefix_keys, prefix_vals, segc, segk, queries, keys_own, values_own, first[:2], second[:2]
    )
    seen = [held[:2], held[2:]]
    attended = [held[0], held[2]]
    if stepwise:
        x_two, y_two, z_one, held, *attended = lax.optimization_barrier((x_two, y_two, z_one, second[4], *attended))
        yx_two, x_one = swap(x_two, "dp", 2), swap(z_one, "mp", 1)
        more = with_other([held])
        hat, inv, normed_low, total, slope, held = ffn_forward(
            attended, tokens, w_out, first_gain, [both], [x_two, y_two]
        )
        x_one, z_three, z_last, yx_two, held, more, normed_low, total = lax.optimization_barrier(
            (x_one, z_three, z_last, yx_two, held, more, normed_low, total)
        )
        x_three, y_three = swap(z_three, "mp", 1), swap(z_three, "dp", 2)
        again = with_other([held, x_one, yx_two])
        total, slope_more = ffn_more(normed_low, total, more)
        x_three, y_three, z_last, again, normed_low, total = lax.optimization_barrier(
            (x_three, y_three, z_last, again, normed_low, total)
        )
        yx_three, x_last = swap(x_three, "dp", 2), swap(z_last, "mp", 1)
        late = with_other([z_three, z_last, x_three])
        total, slope_again = ffn_more(normed_low, total, again)
        yx_three, x_last, y_three, late, total = lax.optimization_barrier((yx_three, x_last, y_three, late, total))
        early, slopes = [both] + more + again, [slope, slope_more, slope_again]
        late = late + with_other([y_three, x_last, yx_three])
    else:
        every = gather_plain(w_in, w_back)
        cut = every.shape[1] * 3 // 8
        early, late = [every[:, :cut]], [every[:, cut:]]
        hat, inv, normed_low, total, slope = ffn_forward(attended, tokens, w_out, first_gain, early, [])
        slopes = [slope]
    layer_output, grad_one, grad_att, delta, ds_prefix, dpk, dpv = middle(
        normed_low, inv, second_gain, first_gain, prefix_keys, prefix_vals,
        total, cotangent, hat, w_out, queries, seen, slopes, early, late,
    )
    logs = [lse for _, lse in seen]
    prefix_grad, input_grad = sum_everywhere(
        jnp.stack([dpk, dpv]),
        [
            lambda _: attend_back(
                lo, nw, queries, keys_own, values_own, grad_att, logs, delta, ds_prefix, prefix_keys, segc, segk
            ),
            lambda grads: project_back(grads, (w_query, w_key, w_value), grad_one),
        ],
    )
    new_first = beta_one * moment_one + (1.0 - beta_one) * prefix_grad
    new_second = beta_two * moment_two + (1.0 - beta_two) * prefix_grad * prefix_grad
    first_hat = new_first / (1.0 - beta_one**STEP)
    second_hat = new_second / (1.0 - beta_two**STEP)
    new_master = prefix_master * (1.0 - learn_rate * weight_decay) - learn_rate * first_hat / (
        jnp.sqrt(second_hat) + epsilon_adam
    )
    return (layer_output, input_grad, new_master, new_first, new_second, new_master.astype(bf16))


def solution(mesh):
    rows = P(("dp", "mp"), None)
    return jax.shard_map(
        on_device,
        mesh=mesh,
        in_specs=(rows, rows, P(), P(), P(), P(), P(), P(), P(None, "mp"), P("mp", None), P(), P(), P(), rows),
        out_specs=(rows, rows, P(), P(), P(), P()),
        check_vma=False,
    )
```

```python
import functools

import jax
import jax.numpy as jnp
from jax import lax
from jax.experimental import pallas as pl
from jax.experimental.pallas import tpu as pltpu
from jax.sharding import PartitionSpec as P

f32, bf16 = jnp.float32, jnp.bfloat16
STEP = 5
epsilon_norm = 1e-05
learn_rate = 1.0
weight_decay = 0.01
beta_one = 0.9
beta_two = 0.999
epsilon_adam = 1e-08
HEAD_SCALE = 0.125
NEG = -1e30
WIN = 256
KC = 64
QUAD = 256
LEAST, MOST = 1e-25, 1e30
ITEMS = 64
VMEM = 60 << 20
NN = (((1,), (0,)), ((), ()))
NT = (((1,), (1,)), ((), ()))
TN = (((0,), (0,)), ((), ()))


def dot(a, b, d=NN):
    return lax.dot_general(a, b, d, preferred_element_type=f32)


def vm():
    return pl.BlockSpec(memory_space=pltpu.VMEM)


def sm():
    return pl.BlockSpec(memory_space=pltpu.SMEM)


def hbm():
    return pl.BlockSpec(memory_space=pl.ANY)


def cost(flops, moved=8 << 20):
    return pl.CostEstimate(flops=4 * flops, bytes_accessed=moved, transcendentals=0)


def part_of(array, width, part):
    return pl.BlockSpec((array.shape[0], width), lambda i: (0, part))


def whole_of(array):
    return pl.BlockSpec(array.shape, lambda i: (0, 0))


def block_diag(piece):
    lane = lax.broadcasted_iota(jnp.int32, piece.shape, 1) // 64
    zero = jnp.zeros_like(piece)
    return jnp.concatenate([jnp.where(lane == h, piece, zero) for h in range(4)], axis=0)


def diag_of(full):
    lane = lax.broadcasted_iota(jnp.int32, (KC, 128), 1) < 64
    left = jnp.where(lane, full[0:64, 0:128], full[64:128, 0:128])
    right = jnp.where(lane, full[128:192, 128:256], full[192:256, 128:256])
    return jnp.concatenate([left, right], axis=1)


def head_ones():
    row = lax.broadcasted_iota(jnp.int32, (QUAD, QUAD), 0) // 64
    lane = lax.broadcasted_iota(jnp.int32, (QUAD, QUAD), 1) // 64
    return jnp.where(row == lane, 1.0, 0.0).astype(bf16)


def head_sum(x, ones):
    high = x.astype(bf16)
    return dot(high, ones) + dot((x - high.astype(f32)).astype(bf16), ones)


def head_max(x):
    lane = lax.broadcasted_iota(jnp.int32, x.shape, 1) < 64
    a = jnp.max(jnp.where(lane, x, NEG), axis=1, keepdims=True)
    b = jnp.max(jnp.where(lane, NEG, x), axis=1, keepdims=True)
    return jnp.where(lane, a, b)


def windows(seg):
    length = seg.shape[0]
    by = seg.reshape(length // KC, KC)
    first, last = by[:, 0], by[:, -1]
    lo = jnp.sum((seg[None, :] < first[:, None]).astype(jnp.int32), axis=1)
    hi = jnp.sum((seg[None, :] <= last[:, None]).astype(jnp.int32), axis=1)
    lo = lo // 16 * 16
    nw = (hi - lo + WIN - 1) // WIN
    segc = jnp.broadcast_to(seg[:, None], (length, 128))
    segk = jnp.concatenate([by, by], axis=1)
    return lo, nw, segc, segk


def list_items(lo_ref, nw_ref, chunk_ref, row_ref, length):
    def chunk(c, count):
        def one(w, count):
            chunk_ref[count] = c
            row_ref[count] = lo_ref[c] + w * WIN
            return count + 1

        return lax.fori_loop(0, nw_ref[c], one, count)

    count = lax.fori_loop(0, length // KC, chunk, 0)
    for n in range(2):
        chunk_ref[count + n] = 0
        row_ref[count + n] = length
    return count


def item_at(n, chunk_ref, row_ref, segc_ref, segk_ref, length):
    c, nominal = chunk_ref[n], row_ref[n]
    start = pl.multiple_of(jnp.minimum(nominal, length - WIN), 16)
    rows = pl.ds(start, WIN)
    keys = pl.ds(pl.multiple_of(c * KC, KC), KC)
    row_id = lax.broadcasted_iota(jnp.int32, (WIN, 128), 0) + start
    keep = jnp.logical_and(segc_ref[rows, :] == segk_ref[pl.ds(c, 1), :], row_id >= nominal)
    bias = jnp.where(keep, 0.0, NEG)
    return rows, keys, jnp.concatenate([bias, bias], axis=1)


def staged(units, first, second, third):
    raw, done = first(units[0]), None
    for n in range(len(units) + 1):
        upcoming = first(units[n + 1]) if n + 1 < len(units) else None
        fresh = second(units[n], raw) if n < len(units) else None
        if done is not None:
            third(units[n - 1], done)
        raw, done = upcoming, fresh


def join_copies(pieces, buffer, target, sems):
    copies, row = [], 0
    for n, piece in enumerate(pieces):
        rows = piece.shape[1]
        copies.append(pltpu.make_async_copy(piece, buffer.at[:, row : row + rows], sems.at[n]))
        row += rows
    return copies, [pltpu.make_async_copy(buffer, target, sems.at[len(pieces)])]


def begin(copies):
    for copy in copies:
        copy.start()


def finish(copies):
    for copy in copies:
        copy.wait()


def joined_shape(pieces):
    planes, _, lanes = pieces[0].shape
    return jax.ShapeDtypeStruct((planes, sum(piece.shape[1] for piece in pieces), lanes), pieces[0].dtype)


def attend_columns(count, q_ref, k_ref, v_ref, pk_ref, pv_ref, att_ref, lse_ref, l_ref, acc_ref, item):
    length, width = att_ref.shape
    parts = [slice(c, c + QUAD) for c in range(0, width, QUAD)]
    spans = [slice(r, r + WIN) for r in range(0, length, WIN)]
    ids = range(len(parts))
    ones = head_ones()
    bdk = [block_diag(pk_ref[:, cols]) for cols in parts]
    bdv = [block_diag(pv_ref[:, cols]) for cols in parts]

    def start_third(unit, p):
        rows, g = unit
        l_ref[rows, parts[g]] = p
        acc_ref[rows, parts[g]] = dot(p.astype(bf16), bdv[g])

    staged(
        [(rows, g) for g in ids for rows in spans],
        lambda u: dot(q_ref[u[0], parts[u[1]]], bdk[u[1]], NT),
        lambda u, s: jnp.exp(s),
        start_third,
    )

    @pl.loop(0, (count + 1) // 2)
    def _(n):
        def third(unit, p):
            (rows, keys, _), g = unit
            l_ref[rows, parts[g]] += p
            acc_ref[rows, parts[g]] += dot(p.astype(bf16), block_diag(v_ref[keys, parts[g]]))

        staged(
            [(one, g) for one in (item(2 * n), item(2 * n + 1)) for g in ids],
            lambda u: dot(q_ref[u[0][0], parts[u[1]]], block_diag(k_ref[u[0][1], parts[u[1]]]), NT),
            lambda u, s: jnp.exp(s + u[0][2]),
            third,
        )

    least, most = [], []
    for rows in spans:
        for cols in parts:
            total = head_sum(l_ref[rows, cols], ones)
            att_ref[rows, cols] = (acc_ref[rows, cols] / total).astype(bf16)
            lse_ref[rows, cols] = jnp.log(total)
            least.append(jnp.min(total, axis=0, keepdims=True))
            most.append(jnp.max(total, axis=0, keepdims=True))
    return functools.reduce(jnp.minimum, least), functools.reduce(jnp.maximum, most)


def attend_again_kernel(
    redo_ref, lo_ref, nw_ref, pk_ref, pv_ref, segc_ref, segk_ref, q_hbm, k_hbm, v_hbm, _a, _b, _c, _d,
    att_one, lse_one, att_two, lse_two,
    q_ref, k_ref, v_ref, part_pk, part_pv, att_ref, lse_ref, l_ref, acc_ref, chunk_ref, row_ref, sems,
):
    @pl.when(redo_ref[0] > 0)
    def _():
        length, width = att_ref.shape
        count = list_items(lo_ref, nw_ref, chunk_ref, row_ref, length)

        def item(n):
            return item_at(n, chunk_ref, row_ref, segc_ref, segk_ref, length)

        for part, (att_hbm, lse_hbm) in enumerate(((att_one, lse_one), (att_two, lse_two))):
            cols = slice(part * width, (part + 1) * width)
            loads = [
                pltpu.make_async_copy(a.at[:, cols], b, sems.at[n])
                for n, (a, b) in enumerate(((q_hbm, q_ref), (k_hbm, k_ref), (v_hbm, v_ref)))
            ]
            begin(loads)
            part_pk[...] = pk_ref[:, cols]
            part_pv[...] = pv_ref[:, cols]
            finish(loads)
            quads, tiles = width // QUAD, length // WIN

            def block(n):
                rows = pl.ds(pl.multiple_of(n // quads * WIN, WIN), WIN)
                return rows, pl.ds(pl.multiple_of(n % quads * QUAD, QUAD), QUAD)

            def entry(n):
                rows, keys, bias = item(n // quads)
                return rows, keys, bias, pl.ds(pl.multiple_of(n % quads * QUAD, QUAD), QUAD)

            @pl.loop(0, quads * tiles)
            def _(n):
                rows, quad = block(n)
                lse_ref[rows, quad] = dot(q_ref[rows, quad], block_diag(part_pk[:, quad]), NT)

            @pl.loop(0, quads * count)
            def _(n):
                rows, keys, bias, quad = entry(n)
                s = dot(q_ref[rows, quad], block_diag(k_ref[keys, quad]), NT) + bias
                lse_ref[rows, quad] = jnp.maximum(lse_ref[rows, quad], s)

            @pl.loop(0, 2 * quads * (length // KC))
            def _(n):
                rows = pl.ds(pl.multiple_of(n // (2 * quads) * KC, KC), KC)
                pair = pl.ds(pl.multiple_of(n % (2 * quads) * 128, 128), 128)
                lse_ref[rows, pair] = head_max(lse_ref[rows, pair])

            @pl.loop(0, quads * tiles)
            def _(n):
                rows, quad = block(n)
                p = jnp.exp(dot(q_ref[rows, quad], block_diag(part_pk[:, quad]), NT) - lse_ref[rows, quad])
                l_ref[rows, quad] = p
                acc_ref[rows, quad] = dot(p.astype(bf16), block_diag(part_pv[:, quad]))

            @pl.loop(0, quads * count)
            def _(n):
                rows, keys, bias, quad = entry(n)
                s = dot(q_ref[rows, quad], block_diag(k_ref[keys, quad]), NT)
                p = jnp.exp(s - lse_ref[rows, quad] + bias)
                l_ref[rows, quad] += p
                acc_ref[rows, quad] += dot(p.astype(bf16), block_diag(v_ref[keys, quad]))

            @pl.loop(0, quads * tiles)
            def _(n):
                rows, quad = block(n)
                total = head_sum(l_ref[rows, quad], head_ones())
                att_ref[rows, quad] = (acc_ref[rows, quad] / total).astype(bf16)
                lse_ref[rows, quad] += jnp.log(total)

            stores = [
                pltpu.make_async_copy(a, b, sems.at[n]) for n, (a, b) in enumerate(((att_ref, att_hbm), (lse_ref, lse_hbm)))
            ]
            begin(stores)
            finish(stores)


def attend_again(redo, lo, nw, pk, pv, segc, segk, q, k, v, first, second):
    length, width = first[0].shape
    slots = pk.shape[0]
    held = (*first, *second)
    return pl.pallas_call(
        attend_again_kernel,
        out_shape=tuple(jax.ShapeDtypeStruct(a.shape, a.dtype) for a in held),
        in_specs=[sm()] * 3 + [vm()] * 4 + [hbm()] * 7,
        out_specs=(hbm(),) * 4,
        input_output_aliases={10 + n: n for n in range(4)},
        scratch_shapes=[pltpu.VMEM((length, width), bf16)] * 3
        + [pltpu.VMEM((slots, width), bf16)] * 2
        + [pltpu.VMEM((length, width), t) for t in (bf16, f32, f32, f32)]
        + [pltpu.SMEM((ITEMS,), jnp.int32)] * 2
        + [pltpu.SemaphoreType.DMA((3,))],
        compiler_params=pltpu.CompilerParams(vmem_limit_bytes=VMEM),
        cost_estimate=cost(1 << 20, 1 << 20),
        name="attend_again",
    )(redo, lo, nw, pk, pv, segc, segk, q, k, v, *held)


def attend_first_kernel(
    lo_ref, nw_ref, x_ref, wq_hbm, wk_hbm, wv_hbm, pk_ref, pv_ref, segc_ref, segk_ref,
    q_hbm, k_hbm, v_hbm, att_ref, lse_ref, least_ref, most_ref,
    w_ref, q_ref, k_ref, v_ref, l_ref, acc_ref, chunk_ref, row_ref, in_sems, out_sems,
):
    length, lanes = x_ref.shape
    loads = [pltpu.make_async_copy(w, w_ref.at[n], in_sems.at[n]) for n, w in enumerate((wq_hbm, wk_hbm, wv_hbm))]
    stores = [
        pltpu.make_async_copy(a, b, out_sems.at[n])
        for n, (a, b) in enumerate(((q_ref, q_hbm), (k_ref, k_hbm), (v_ref, v_hbm)))
    ]
    for load in loads:
        load.start()
    count = list_items(lo_ref, nw_ref, chunk_ref, row_ref, length)
    for n, out_ref in enumerate((q_ref, k_ref, v_ref)):
        loads[n].wait()
        for c in range(0, lanes, QUAD):
            value = dot(x_ref[...], w_ref[n, :, c : c + QUAD])
            out_ref[:, c : c + QUAD] = (value * HEAD_SCALE if n == 0 else value).astype(bf16)
        stores[n].start()

    def item(n):
        return item_at(n, chunk_ref, row_ref, segc_ref, segk_ref, length)

    least_ref[...], most_ref[...] = attend_columns(
        count, q_ref, k_ref, v_ref, pk_ref, pv_ref, att_ref, lse_ref, l_ref, acc_ref, item
    )
    for store in stores:
        store.wait()


def attend_rest_kernel(*refs, count):
    lo_ref, nw_ref, q_ref, k_ref, v_ref, pk_ref, pv_ref, segc_ref, segk_ref = refs[:9]
    pieces, refs = refs[9 : 9 + count], refs[9 + count :]
    att_ref, lse_ref, least_ref, most_ref, *refs = refs
    arrive, leave = [], []
    if count:
        target, *refs, held, sems = refs
        arrive, leave = join_copies(pieces, held, target, sems)
    l_ref, acc_ref, chunk_ref, row_ref = refs
    begin(arrive)
    length = q_ref.shape[0]
    items = list_items(lo_ref, nw_ref, chunk_ref, row_ref, length)
    finish(arrive)
    begin(leave)

    def item(n):
        return item_at(n, chunk_ref, row_ref, segc_ref, segk_ref, length)

    least_ref[...], most_ref[...] = attend_columns(
        items, q_ref, k_ref, v_ref, pk_ref, pv_ref, att_ref, lse_ref, l_ref, acc_ref, item
    )
    finish(leave)


def attended_shapes(length, width):
    shape, lane = (length, width), jax.ShapeDtypeStruct((1, QUAD), f32)
    return [jax.ShapeDtypeStruct(shape, bf16), jax.ShapeDtypeStruct(shape, f32), lane, lane]


def attend_first(lo, nw, x, wq, wk, wv, pk, pv, segc, segk, width):
    length, lanes = x.shape
    low = jax.ShapeDtypeStruct((length, lanes), bf16)
    return pl.pallas_call(
        attend_first_kernel,
        out_shape=(low, low, low, *attended_shapes(length, width)),
        in_specs=[sm(), sm(), vm(), hbm(), hbm(), hbm(), vm(), vm(), vm(), vm()],
        out_specs=(hbm(), hbm(), hbm(), vm(), vm(), vm(), vm()),
        scratch_shapes=[pltpu.VMEM((3, lanes, lanes), bf16)]
        + [pltpu.VMEM((length, lanes), bf16)] * 3
        + [pltpu.VMEM((length, width), f32)] * 2
        + [pltpu.SMEM((ITEMS,), jnp.int32)] * 2
        + [pltpu.SemaphoreType.DMA((3,))] * 2,
        compiler_params=pltpu.CompilerParams(vmem_limit_bytes=VMEM),
        cost_estimate=cost(16 * length * lanes * lanes),
        name="attend_first",
    )(lo, nw, x, wq, wk, wv, pk, pv, segc, segk)


def attend_rest(lo, nw, q, k, v, pk, pv, segc, segk, width, part, pieces):
    length = q.shape[0]
    outs = attended_shapes(length, width)
    specs = [whole_of(each) for each in outs]
    scratch = [pltpu.VMEM((length, width), f32)] * 2 + [pltpu.SMEM((ITEMS,), jnp.int32)] * 2
    if pieces:
        held = joined_shape(pieces)
        outs.append(held)
        specs.append(hbm())
        scratch += [pltpu.VMEM(held.shape, held.dtype), pltpu.SemaphoreType.DMA((len(pieces) + 1,))]
    return pl.pallas_call(
        functools.partial(attend_rest_kernel, count=len(pieces)),
        grid=(1,),
        out_shape=tuple(outs),
        in_specs=[sm(), sm()]
        + [part_of(a, width, part) for a in (q, k, v, pk, pv)]
        + [whole_of(segc), whole_of(segk)]
        + [hbm()] * len(pieces),
        out_specs=tuple(specs),
        scratch_shapes=scratch,
        compiler_params=pltpu.CompilerParams(vmem_limit_bytes=VMEM),
        cost_estimate=cost(16000 * length * width),
        name="attend_rest",
    )(lo, nw, q, k, v, pk, pv, segc, segk, *pieces)


def attend_back_kernel(*refs, halves):
    lo_ref, nw_ref, pk_ref, segc_ref, segk_ref = refs[:5]
    sources, refs = refs[5 : 11 + halves], refs[11 + halves :]
    (
        dq_hbm, dk_hbm, dv_hbm,
        q_ref, k_ref, v_ref, g_ref, delta_ref, ds_ref, lse_ref,
        dq_acc, dk_acc, dv_acc, dq_ref, dk_ref, dv_ref, chunk_ref, row_ref, in_sems, out_sems,
    ) = refs
    length, lanes = q_ref.shape
    parts = [slice(g * QUAD, (g + 1) * QUAD) for g in range(lanes // QUAD)]
    spans = [slice(r * WIN, (r + 1) * WIN) for r in range(length // WIN)]
    places = [ds_ref, q_ref, k_ref, v_ref, g_ref, delta_ref]
    for n in range(halves):
        places.append(lse_ref.at[:, n * (lanes // halves) : (n + 1) * (lanes // halves)])
    loads = [pltpu.make_async_copy(a, b, in_sems.at[n]) for n, (a, b) in enumerate(zip(sources, places))]
    for load in loads:
        load.start()
    count = list_items(lo_ref, nw_ref, chunk_ref, row_ref, length)
    dk_acc[...] = jnp.zeros_like(dk_acc)
    dv_acc[...] = jnp.zeros_like(dv_acc)
    loads[0].wait()
    for cols in parts:
        bdk = block_diag(pk_ref[:, cols])
        for rows in spans:
            dq_acc[rows, cols] = dot(ds_ref[rows, cols], bdk)
    for load in loads[1:]:
        load.wait()
    ids = range(len(parts))

    @pl.loop(0, (count + 1) // 2)
    def _(n):
        def first(unit):
            (rows, keys, _), g = unit
            cols = parts[g]
            s = dot(q_ref[rows, cols], block_diag(k_ref[keys, cols]), NT)
            return s, dot(g_ref[rows, cols], block_diag(v_ref[keys, cols]), NT)

        def second(unit, pair):
            (rows, _, bias), g = unit
            cols = parts[g]
            p = jnp.exp(pair[0] + bias - lse_ref[rows, cols])
            return p.astype(bf16), (p * (pair[1] - delta_ref[rows, cols])).astype(bf16)

        def third(unit, pair):
            (rows, keys, _), g = unit
            cols = parts[g]
            dv_acc[keys, cols] += diag_of(dot(pair[0], g_ref[rows, cols], TN))
            dk_acc[keys, cols] += diag_of(dot(pair[1], q_ref[rows, cols], TN))
            dq_acc[rows, cols] += dot(pair[1], block_diag(k_ref[keys, cols]))

        items = [item_at(2 * n + i, chunk_ref, row_ref, segc_ref, segk_ref, length) for i in range(2)]
        staged([(one, g) for one in items for g in ids], first, second, third)

    stores = []
    ends = ((dq_acc, dq_ref, dq_hbm, HEAD_SCALE), (dk_acc, dk_ref, dk_hbm, 1.0), (dv_acc, dv_ref, dv_hbm, 1.0))
    for n, (acc, low, target, scale) in enumerate(ends):
        low[...] = (acc[...] * scale).astype(bf16)
        stores.append(pltpu.make_async_copy(low, target, out_sems.at[n]))
        stores[n].start()
    for store in stores:
        store.wait()


def attend_back(lo, nw, q, k, v, g, lse, delta, ds, pk, segc, segk):
    length, lanes = q.shape
    tall = (length, lanes)
    return pl.pallas_call(
        functools.partial(attend_back_kernel, halves=len(lse)),
        out_shape=(jax.ShapeDtypeStruct(tall, bf16),) * 3,
        in_specs=[sm(), sm(), vm(), vm(), vm()] + [hbm()] * (6 + len(lse)),
        out_specs=(hbm(),) * 3,
        scratch_shapes=[pltpu.VMEM(tall, t) for t in (bf16, bf16, bf16, bf16, f32, bf16, f32)]
        + [pltpu.VMEM(tall, f32)] * 3
        + [pltpu.VMEM(tall, bf16)] * 3
        + [pltpu.SMEM((ITEMS,), jnp.int32)] * 2
        + [pltpu.SemaphoreType.DMA((6 + len(lse),)), pltpu.SemaphoreType.DMA((3,))],
        compiler_params=pltpu.CompilerParams(vmem_limit_bytes=VMEM),
        cost_estimate=cost(length * lanes * 30000),
        name="attend_back",
    )(lo, nw, pk, segc, segk, ds, q, k, v, g, delta, *lse)


HID = 512


def mean_of(x):
    return jnp.mean(x, axis=-1, keepdims=True)


def centre(x):
    centred = x - mean_of(x)
    inv = lax.rsqrt(mean_of(centred * centred) + epsilon_norm)
    return centred * inv, inv


def pull_norm(pull, hat, inv):
    return inv * (pull - mean_of(pull) - hat * mean_of(pull * hat))


def gelu_pair(x):
    phi = 0.5 + 0.5 * lax.erf(x * 0.7071067811865476)
    bell = 0.3989422804014327 * jnp.exp(-0.5 * (x * x))
    return x * phi, phi + x * bell


def blocks_of(pieces):
    blocks, block, room = [], [], HID
    for piece in pieces:
        row = 0
        while row < piece.shape[1]:
            rows = min(room, piece.shape[1] - row)
            block.append((piece, row, rows))
            row, room = row + rows, room - rows
            if room == 0:
                blocks.append(block)
                block, room = [], HID
    return blocks


def most_of(pieces):
    return max(len(block) for block in blocks_of(pieces))


def block_copies(block, buffer, sems, slot):
    copies, place = [], 0
    for n, (piece, row, rows) in enumerate(block):
        source = piece.at[:, row : row + rows]
        copies.append(pltpu.make_async_copy(source, buffer.at[slot, :, place : place + rows], sems.at[slot, n]))
        place += rows
    return copies


def forward_block(low_ref, weights, sum_ref, slope_ref, cols):
    def second(rows, x):
        act, slope = gelu_pair(x)
        slope_ref[rows, cols] = slope.astype(bf16)
        return act.astype(bf16)

    def third(rows, act):
        sum_ref[rows, :] += dot(act, weights[1])

    spans = [slice(r, r + WIN) for r in range(0, low_ref.shape[0], WIN)]
    staged(spans, lambda rows: dot(low_ref[rows, :], weights[0], NT), second, third)


def ffn_kernel(*refs, halves, count, others):
    atts, (tok_ref, w_out_ref, gain_ref), refs = refs[:halves], refs[halves : halves + 3], refs[halves + 3 :]
    blocks, pieces, refs = blocks_of(refs[:count]), refs[count : count + others], refs[count + others :]
    hat_ref, inv_ref, low_ref, sum_ref, slope_ref, *refs = refs
    arrive, leave = [], []
    if others:
        target, *refs, held, join_sems = refs
        arrive, leave = join_copies(pieces, held, target, join_sems)
    buffer, sems = refs
    width = atts[0].shape[1]
    copies = [block_copies(block, buffer, sems, b % 2) for b, block in enumerate(blocks)]
    begin(copies[0])
    begin(arrive)

    def second(rows, x):
        hat, inv = centre(tok_ref[rows, :].astype(f32) + x)
        hat_ref[rows, :] = hat
        inv_ref[rows, :] = jnp.broadcast_to(inv, (WIN, 128))
        normed = gain_ref[...] * hat
        sum_ref[rows, :] = normed
        low_ref[rows, :] = normed.astype(bf16)

    def first(rows):
        return sum(dot(att_ref[rows, :], w_out_ref[n * width : (n + 1) * width, :]) for n, att_ref in enumerate(atts))

    spans = [slice(r, r + WIN) for r in range(0, tok_ref.shape[0], WIN)]
    staged(spans, first, second, lambda rows, x: None)
    finish(arrive)
    begin(leave)
    for b in range(len(blocks)):
        if b + 1 < len(blocks):
            begin(copies[b + 1])
        finish(copies[b])
        forward_block(low_ref, buffer.at[b % 2], sum_ref, slope_ref, slice(b * HID, (b + 1) * HID))
    finish(leave)


def ffn_forward(att, tokens, w_out, gain, pieces, others):
    length, lanes = tokens.shape
    hidden = sum(piece.shape[1] for piece in pieces)
    wide = jax.ShapeDtypeStruct((length, lanes), f32)
    outs = [
        wide,
        jax.ShapeDtypeStruct((length, 128), f32),
        jax.ShapeDtypeStruct((length, lanes), bf16),
        wide,
        jax.ShapeDtypeStruct((length, hidden), bf16),
    ]
    specs = [vm()] * 5
    scratch = [pltpu.VMEM((2, 2, HID, lanes), bf16), pltpu.SemaphoreType.DMA((2, most_of(pieces)))]
    if others:
        held = joined_shape(others)
        outs.append(held)
        specs.append(hbm())
        scratch += [pltpu.VMEM(held.shape, held.dtype), pltpu.SemaphoreType.DMA((len(others) + 1,))]
    return pl.pallas_call(
        functools.partial(ffn_kernel, halves=len(att), count=len(pieces), others=len(others)),
        out_shape=tuple(outs),
        in_specs=[vm()] * (len(att) + 3) + [hbm()] * (len(pieces) + len(others)),
        out_specs=tuple(specs),
        scratch_shapes=scratch,
        compiler_params=pltpu.CompilerParams(vmem_limit_bytes=VMEM),
        cost_estimate=cost(4 * length * lanes * (hidden + lanes)),
        name="ffn_forward",
    )(*att, tokens, w_out, gain, *pieces, *others)


def more_kernel(low_ref, start_ref, *refs, count):
    blocks = blocks_of(refs[:count])
    sum_ref, slope_ref, buffer, sems = refs[count:]
    copies = [block_copies(block, buffer, sems, b % 2) for b, block in enumerate(blocks)]
    begin(copies[0])
    sum_ref[...] = start_ref[...]
    for b in range(len(blocks)):
        if b + 1 < len(blocks):
            begin(copies[b + 1])
        finish(copies[b])
        forward_block(low_ref, buffer.at[b % 2], sum_ref, slope_ref, slice(b * HID, (b + 1) * HID))


def ffn_more(low, start, pieces):
    length, lanes = low.shape
    hidden = sum(piece.shape[1] for piece in pieces)
    return pl.pallas_call(
        functools.partial(more_kernel, count=len(pieces)),
        out_shape=(jax.ShapeDtypeStruct((length, lanes), f32), jax.ShapeDtypeStruct((length, hidden), bf16)),
        in_specs=[vm()] * 2 + [hbm()] * len(pieces),
        out_specs=(vm(),) * 2,
        scratch_shapes=[pltpu.VMEM((2, 2, HID, lanes), bf16), pltpu.SemaphoreType.DMA((2, most_of(pieces)))],
        compiler_params=pltpu.CompilerParams(vmem_limit_bytes=VMEM),
        cost_estimate=cost(4 * length * lanes * hidden),
        name="ffn_more",
    )(low, start, *pieces)


def middle_kernel(*refs, halves, early, late, groups):
    low_ref, inv_ref, gain_two_ref, gain_one_ref, pk_ref, pv_ref = refs[:6]
    sum_hbm, cot_hbm, hat_hbm, w_out_hbm, q_hbm = refs[6:11]
    seen, refs = refs[11 : 11 + 2 * halves], refs[11 + 2 * halves :]
    slopes, pieces, refs = refs[:groups], refs[groups : groups + early + late], refs[groups + early + late :]
    (layer_hbm, one_hbm, g_hbm, delta_hbm, ds_hbm, dpk_ref, dpv_ref) = refs[:7]
    (
        acc_ref, cot_ref, hat_ref, w_out_ref, q_ref, att_ref, lse_ref, layer_ref, one_ref, g_ref, delta_ref, ds_ref,
        grad_ref, late_ref, buffer, sbuf, sems, ssems, in_sems, out_sems,
    ) = refs[7:]
    length, lanes = low_ref.shape
    spans = [slice(r, r + WIN) for r in range(0, length, WIN)]
    parts = [slice(c, c + QUAD) for c in range(0, lanes, QUAD)]
    first_blocks, last_blocks = blocks_of(pieces[:early]), blocks_of(pieces[early:])
    order = last_blocks + first_blocks + last_blocks
    copies = [block_copies(block, buffer, sems, n % 2) for n, block in enumerate(order)]
    skip = len(last_blocks)
    slabs = [slope.at[:, c : c + HID] for slope in slopes for c in range(0, slope.shape[1], HID)]
    for n, source in enumerate(slabs, skip):
        copies[n].append(pltpu.make_async_copy(source, sbuf.at[n % 2], ssems.at[n % 2]))
    sources = (sum_hbm, cot_hbm, hat_hbm, w_out_hbm, q_hbm, *seen)
    places = [acc_ref, cot_ref, hat_ref, w_out_ref, q_ref]
    for n in range(halves):
        cols = slice(n * (lanes // halves), (n + 1) * (lanes // halves))
        places += [att_ref.at[:, cols], lse_ref.at[:, cols]]
    loads = [pltpu.make_async_copy(a, b, in_sems.at[n]) for n, (a, b) in enumerate(zip(sources, places))]
    results = [layer_ref, one_ref, g_ref]
    targets = [layer_hbm, one_hbm, g_hbm]
    for cols in parts:
        results += [delta_ref.at[:, cols], ds_ref.at[:, cols]]
        targets += [delta_hbm.at[:, cols], ds_hbm.at[:, cols]]
    stores = [pltpu.make_async_copy(a, b, out_sems.at[n]) for n, (a, b) in enumerate(zip(results, targets))]
    begin(copies[0])
    begin(loads[:1])

    def enter(n):
        if n + 1 < len(order):
            begin(copies[n + 1])
        if n == 0:
            finish(loads[:1])
            begin(loads[1:])
        finish(copies[n])
        return buffer.at[n % 2]

    for n in range(skip):
        forward_block(low_ref, enter(n), acc_ref, late_ref, slice(n * HID, (n + 1) * HID))

    finish(loads[1:3])
    for n in range(skip, len(order)):
        weights = enter(n)
        past = n - skip - len(first_blocks)

        def first(rows):
            if n == skip:
                hat, inv = centre(acc_ref[rows, :])
                layer_ref[rows, :] = (gain_two_ref[...] * hat).astype(bf16)
                grad = pull_norm(cot_ref[rows, :].astype(f32) * gain_two_ref[...], hat, inv)
                acc_ref[rows, :] = grad
                grad_ref[rows, :] = grad.astype(bf16)
            return dot(grad_ref[rows, :], weights[1], NT)

        def second(rows, x):
            slope = sbuf[n % 2, rows, :] if past < 0 else late_ref[rows, past * HID : (past + 1) * HID]
            return (x * slope.astype(f32)).astype(bf16)

        def third(rows, x):
            acc_ref[rows, :] += dot(x, weights[0])

        staged(spans, first, second, third)
        if n == skip:
            begin(stores[:1])
    finish(loads[3:])

    def first(rows):
        grad = pull_norm(acc_ref[rows, :] * gain_one_ref[...], hat_ref[rows, :], inv_ref[rows, 0:1])
        one_ref[rows, :] = grad
        return grad.astype(bf16)

    def second(rows, grad):
        g_ref[rows, :] = dot(grad, w_out_ref[...], NT).astype(bf16)

    staged(spans, first, second, lambda rows, x: None)
    begin(stores[1:3])

    ones = head_ones()
    sums = {}

    def first(unit):
        g, rows = unit
        cols = parts[g]
        up = g_ref[rows, cols]
        delta = head_sum(up.astype(f32) * att_ref[rows, cols].astype(f32), ones)
        return dot(q_ref[rows, cols], block_diag(pk_ref[:, cols]), NT), dot(up, block_diag(pv_ref[:, cols]), NT), delta

    def second(unit, three):
        g, rows = unit
        cols = parts[g]
        delta_ref[rows, cols] = three[2]
        p = jnp.exp(three[0] - lse_ref[rows, cols])
        ds = (p * (three[1] - three[2])).astype(bf16)
        ds_ref[rows, cols] = ds
        return p.astype(bf16), ds

    def third(unit, pair):
        g, rows = unit
        cols = parts[g]
        dpv, dpk = diag_of(dot(pair[0], g_ref[rows, cols], TN)), diag_of(dot(pair[1], q_ref[rows, cols], TN))
        if rows.start:
            dpv, dpk = sums[g][0] + dpv, sums[g][1] + dpk
        sums[g] = (dpv, dpk)
        if rows.stop == length:
            dpv_ref[:, cols], dpk_ref[:, cols] = dpv, dpk
            begin(stores[3 + 2 * g : 5 + 2 * g])

    staged([(g, rows) for g in range(len(parts)) for rows in spans], first, second, third)
    finish(stores)


def middle(low, inv, gain_two, gain_one, pk, pv, total, cot, hat, w_out, q, seen, slopes, early, late):
    length, lanes = low.shape
    slots = pk.shape[0]
    late_units = sum(piece.shape[1] for piece in late)
    flat = [each for pair in seen for each in pair]
    tall = (length, lanes)
    small = jax.ShapeDtypeStruct((slots, lanes), f32)
    holds = [f32, bf16, f32, None, bf16, bf16, f32, bf16, f32, bf16, f32, bf16, bf16]
    return pl.pallas_call(
        functools.partial(middle_kernel, halves=len(seen), early=len(early), late=len(late), groups=len(slopes)),
        out_shape=tuple(jax.ShapeDtypeStruct(tall, t) for t in (bf16, f32, bf16, f32, bf16)) + (small, small),
        in_specs=[vm()] * 6 + [hbm()] * (5 + 2 * len(seen) + len(slopes) + len(early) + len(late)),
        out_specs=(hbm(),) * 5 + (vm(), vm()),
        scratch_shapes=[pltpu.VMEM((lanes, lanes), bf16) if t is None else pltpu.VMEM(tall, t) for t in holds]
        + [
            pltpu.VMEM((length, late_units), bf16),
            pltpu.VMEM((2, 2, HID, lanes), bf16),
            pltpu.VMEM((2, length, HID), bf16),
            pltpu.SemaphoreType.DMA((2, most_of(early + late))),
            pltpu.SemaphoreType.DMA((2,)),
            pltpu.SemaphoreType.DMA((5 + len(flat),)),
            pltpu.SemaphoreType.DMA((3 + 2 * (lanes // QUAD),)),
        ],
        compiler_params=pltpu.CompilerParams(vmem_limit_bytes=VMEM),
        cost_estimate=cost(40 * length * lanes * lanes),
        name="middle",
    )(low, inv, gain_two, gain_one, pk, pv, total, cot, hat, w_out, q, *flat, *slopes, *early, *late)


def project_kernel(dq_hbm, dk_hbm, dv_hbm, wq_hbm, wk_hbm, wv_hbm, one_hbm, out_hbm, grads, weights, out_ref, *sems):
    length, lanes = out_ref.shape
    spans = [slice(r, r + WIN) for r in range(0, length, WIN)]
    grad_sems, weight_sems, one_sem, out_sems = sems
    loads = []
    for n, (grad, weight) in enumerate(((dq_hbm, wq_hbm), (dk_hbm, wk_hbm), (dv_hbm, wv_hbm))):
        loads.append(
            (
                pltpu.make_async_copy(grad, grads.at[n], grad_sems.at[n]),
                pltpu.make_async_copy(weight, weights.at[n], weight_sems.at[n]),
            )
        )
        begin(loads[n])
        if n == 0:
            one = pltpu.make_async_copy(one_hbm, out_ref, one_sem.at[0])
            one.start()
    stores = [
        pltpu.make_async_copy(out_ref.at[rows, :], out_hbm.at[rows, :], out_sems.at[r]) for r, rows in enumerate(spans)
    ]
    finish(loads[0])
    first = [dot(grads[0, rows, :], weights[0], NT) for rows in spans[:1]]
    one.wait()
    out_ref[spans[0], :] += first[0]
    for rows in spans[1:]:
        out_ref[rows, :] += dot(grads[0, rows, :], weights[0], NT)
    finish(loads[1])
    finish(loads[2])
    for r, rows in enumerate(spans):
        more = dot(grads[1, rows, :], weights[1], NT) + dot(grads[2, rows, :], weights[2], NT)
        out_ref[rows, :] += more
        stores[r].start()
    finish(stores)


def project_back(grads, weights, grad_one):
    length, lanes = grad_one.shape
    return pl.pallas_call(
        project_kernel,
        out_shape=jax.ShapeDtypeStruct((length, lanes), f32),
        in_specs=[hbm()] * 7,
        out_specs=hbm(),
        scratch_shapes=[
            pltpu.VMEM((3, length, lanes), bf16),
            pltpu.VMEM((3, lanes, lanes), bf16),
            pltpu.VMEM((length, lanes), f32),
            pltpu.SemaphoreType.DMA((3,)),
            pltpu.SemaphoreType.DMA((3,)),
            pltpu.SemaphoreType.DMA((1,)),
            pltpu.SemaphoreType.DMA((length // WIN,)),
        ],
        compiler_params=pltpu.CompilerParams(vmem_limit_bytes=VMEM),
        cost_estimate=cost(6 * length * lanes * lanes),
        name="project_back",
    )(*grads, *weights, grad_one)


def swap(x, axis, bit):
    return lax.ppermute(x, axis, [(i, i ^ bit) for i in range(lax.axis_size(axis))])


def swap_two(x, one, two):
    if one[0] == two[0]:
        return swap(x, one[0], one[1] | two[1])
    wide = {"dp": lax.axis_size("mp"), "mp": 1}
    mask = one[1] * wide[one[0]] + two[1] * wide[two[0]]
    count = lax.axis_size("dp") * lax.axis_size("mp")
    return lax.ppermute(x, ("dp", "mp"), [(i, i ^ mask) for i in range(count)])


def gather_plain(w_in, w_back):
    both = jnp.stack([w_in.T, w_back])
    part = both.shape[1] // lax.axis_size("dp")
    mine = lax.dynamic_slice_in_dim(both, lax.axis_index("dp") * part, part, 1)
    return lax.all_gather(mine, ("dp", "mp"), axis=1, tiled=True)


def own_weights(w_in, w_back):
    both = jnp.stack([w_in.T, w_back])
    half = both.shape[1] // 2
    dp = lax.axis_index("dp")
    own = lax.dynamic_slice_in_dim(both, lax.rem(dp, 2) * half, half, 1)
    unit = half // 2
    mine = lax.dynamic_slice_in_dim(own, dp // 2 * unit, unit, 1)
    rest = lax.dynamic_slice_in_dim(own, (1 - dp // 2) * unit, unit, 1)
    return both, own, mine, rest


def with_other(pieces):
    return [each for piece in pieces for each in (piece, swap(piece, "dp", 1))]


def sum_everywhere(x, between):
    core = lax.rem(lax.axis_index("dp"), 2)
    half = x.shape[0] // 2
    keep = lax.dynamic_slice_in_dim(x, core * half, half, 0)
    give = lax.dynamic_slice_in_dim(x, (1 - core) * half, half, 0)
    part = keep + swap(give, "dp", 1)
    bits = [(axis, 1 << n) for axis in ("dp", "mp") for n in range(lax.axis_size(axis).bit_length() - 1)][1:]
    bits = sorted(bits, key=lambda pair: pair[1] if pair[0] == "mp" else 1)
    done = None
    for n in range(0, len(bits), 2):
        low = part.astype(bf16)
        pairs = bits[n : n + 2]
        came = [swap(low, *pair) for pair in pairs]
        if len(pairs) == 2:
            came.append(swap_two(low, *pairs))
        if between:
            done = between.pop(0)(done)
            came, done = lax.optimization_barrier((came, done))
        part = low.astype(f32) + came[0].astype(f32)
        if len(pairs) == 2:
            part = part + (came[1].astype(f32) + came[2].astype(f32))
    while between:
        done = between.pop(0)(done)
    other = swap(part, "dp", 1)
    return jnp.where(core == 0, jnp.concatenate([part, other]), jnp.concatenate([other, part])), done


def on_device(
    tokens, segment_ids, w_query, w_key, w_value, w_out, gain_one, gain_two, w_in, w_back,
    prefix_master, moment_one, moment_two, cotangent,
):
    stepwise = lax.axis_size("dp") == 4 and lax.axis_size("mp") == 8
    prefix_low = prefix_master.astype(bf16)
    prefix_keys, prefix_vals = prefix_low[0], prefix_low[1]
    first_gain, second_gain = gain_one[None, :], gain_two[None, :]
    lo, nw, segc, segk = windows(segment_ids[0])
    halves = 2
    width = tokens.shape[1] // halves
    if stepwise:
        both, own, mine, rest = own_weights(w_in, w_back)
        z_two, z_one, x_own = swap(mine, "mp", 4), swap(mine, "mp", 2), swap(own, "mp", 1)
    queries, keys_own, values_own, *first = attend_first(
        lo, nw, tokens, w_query, w_key, w_value, prefix_keys, prefix_vals, segc, segk, width
    )
    if stepwise:
        z_one, z_two, x_own, mine, rest, queries, keys_own, values_own = lax.optimization_barrier(
            (z_one, z_two, x_own, mine, rest, queries, keys_own, values_own)
        )
        z_three, z_last = swap(mine, "mp", 6), swap(rest, "mp", 2)
        x_two, y_two = swap(z_two, "mp", 1), swap(z_two, "dp", 2)
    moved = [x_own, z_one, z_two] if stepwise else []
    second = attend_rest(
        lo, nw, queries, keys_own, values_own, prefix_keys, prefix_vals, segc, segk, width, 1, moved
    )
    least, most = jnp.minimum(first[2], second[2]), jnp.maximum(first[3], second[3])
    redo = jnp.logical_not(jnp.all(jnp.logical_and(least > LEAST, most < MOST))).astype(jnp.int32)[None]
    held = attend_again(
        redo, lo, nw, prefix_keys, prefix_vals, segc, segk, queries, keys_own, values_own, first[:2], second[:2]
    )
    seen = [held[:2], held[2:]]
    attended = [held[0], held[2]]
    if stepwise:
        x_two, y_two, z_one, held, *attended = lax.optimization_barrier((x_two, y_two, z_one, second[4], *attended))
        yx_two, x_one = swap(x_two, "dp", 2), swap(z_one, "mp", 1)
        more = with_other([held])
        hat, inv, normed_low, total, slope, held = ffn_forward(
            attended, tokens, w_out, first_gain, [both], [x_two, y_two]
        )
        x_one, z_three, z_last, yx_two, held, more, normed_low, total = lax.optimization_barrier(
            (x_one, z_three, z_last, yx_two, held, more, normed_low, total)
        )
        x_three, y_three = swap(z_three, "mp", 1), swap(z_three, "dp", 2)
        again = with_other([held, x_one, yx_two])
        total, slope_more = ffn_more(normed_low, total, more)
        x_three, y_three, z_last, again, normed_low, total = lax.optimization_barrier(
            (x_three, y_three, z_last, again, normed_low, total)
        )
        yx_three, x_last = swap(x_three, "dp", 2), swap(z_last, "mp", 1)
        late = with_other([z_three, z_last, x_three])
        total, slope_again = ffn_more(normed_low, total, again)
        yx_three, x_last, y_three, late, total = lax.optimization_barrier((yx_three, x_last, y_three, late, total))
        early, slopes = [both] + more + again, [slope, slope_more, slope_again]
        late = late + with_other([y_three, x_last, yx_three])
    else:
        every = gather_plain(w_in, w_back)
        cut = every.shape[1] * 3 // 8
        early, late = [every[:, :cut]], [every[:, cut:]]
        hat, inv, normed_low, total, slope = ffn_forward(attended, tokens, w_out, first_gain, early, [])
        slopes = [slope]
    layer_output, grad_one, grad_att, delta, ds_prefix, dpk, dpv = middle(
        normed_low, inv, second_gain, first_gain, prefix_keys, prefix_vals,
        total, cotangent, hat, w_out, queries, seen, slopes, early, late,
    )
    logs = [lse for _, lse in seen]
    prefix_grad, input_grad = sum_everywhere(
        jnp.stack([dpk, dpv]),
        [
            lambda _: attend_back(
                lo, nw, queries, keys_own, values_own, grad_att, logs, delta, ds_prefix, prefix_keys, segc, segk
            ),
            lambda grads: project_back(grads, (w_query, w_key, w_value), grad_one),
        ],
    )
    new_first = beta_one * moment_one + (1.0 - beta_one) * prefix_grad
    new_second = beta_two * moment_two + (1.0 - beta_two) * prefix_grad * prefix_grad
    first_hat = new_first / (1.0 - beta_one**STEP)
    second_hat = new_second / (1.0 - beta_two**STEP)
    new_master = prefix_master * (1.0 - learn_rate * weight_decay) - learn_rate * first_hat / (
        jnp.sqrt(second_hat) + epsilon_adam
    )
    return (layer_output, input_grad, new_master, new_first, new_second, new_master.astype(bf16))


def solution(mesh):
    rows = P(("dp", "mp"), None)
    return jax.shard_map(
        on_device,
        mesh=mesh,
        in_specs=(rows, rows, P(), P(), P(), P(), P(), P(), P(None, "mp"), P("mp", None), P(), P(), P(), rows),
        out_specs=(rows, rows, P(), P(), P(), P()),
        check_vma=False,
    )
```
